32 devices in a mesh: row: 8 (over z, y), col: 4 (over x, core).
Axes of the slice: x: 2, y: 2, z: 4, core: 2. Of those that a mesh axis runs over, the one named last changes fastest.
Arguments:
- fock_matrix: bfloat16 [1536, 1536], P('row', 'col'), as said below
- density: bfloat16 [1536, 1536], P('row', 'col'), as said below
- margin: bfloat16 [1536, 1536], P('row', 'col'), as said below
- fill_patterns: int32 [3, 48, 48], P(None, 'row', 'col'), may hold values from 0 to 1, as said below
- first_filters: int32 [3, 48, 48], P(None, 'row', 'col'), may hold values from 0 to 1, as said below
- owner_order: int32 [48], replicated, may hold values from 0 to 47, as said below
- second_filters: int32 [7, 48, 48], P(None, 'row', 'col'), may hold values from 0 to 1, as said below
Outputs:
- evolved: bfloat16 [1536, 1536], P('row', 'col')
The draws below stay inside these ranges and needn't reach their ends.
Inputs may be any that keep to these rules, and one draw needn't show every extreme that they name: `fock_matrix`: Symmetric. `density`: Symmetric. `margin`: Symmetric, with unit diagonal. `fill_patterns`: each entry says whether a block is kept; each pattern is symmetric and keeps every diagonal block. `first_filters`: each entry says whether a block of the product is kept; each filter is symmetric and keeps every diagonal block. `second_filters`: each entry says whether a block of the product is kept, indexed in owner order; each filter is symmetric and keeps every diagonal block. `owner_order`: A permutation of the 48 block indices.
All inputs are finite; a program needn't handle non-finite values.
Results may differ from the reference program's by a relative error of at most 0.012.
Values may be sent and summed in bfloat16 or wider, within the bound.
No kernel may reach another device: no remote copies, remote signals or barrier semaphores. Data moves between devices by JAX's collectives and lax.ppermute only.
A program may use at most 64 MiB of HBM per device.

```python
import jax
import jax.numpy as jnp

BLK = 32
PANEL = 6
TERMS = 6
SQUARINGS = 2
NB = 48
N = 1536


def pattern(key, variant, layers):
    weights = jax.random.randint(jax.random.fold_in(key, 11), (NB,), 1, 9)
    threshold = weights[:, None] * weights[None, :]
    rolled = jax.random.randint(jax.random.fold_in(key, variant), (layers, NB, NB), 0, 96)
    retained = (rolled < threshold[None]).astype(jnp.int32)
    retained = jnp.maximum(retained, jnp.swapaxes(retained, 1, 2))
    diagonal = (jnp.arange(NB)[:, None] == jnp.arange(NB)[None, :]).astype(jnp.int32)
    return jnp.maximum(retained, diagonal[None])


def symmetric(key, scale):
    raw = jax.random.normal(key, (N, N), jnp.float32)
    return (raw + raw.T) * (0.70710678 * scale)


def draw_fock_matrix(key, part):
    return symmetric(jax.random.fold_in(key, 31), 11.0 / N).astype(jnp.bfloat16)


def draw_density(key, part):
    return symmetric(jax.random.fold_in(key, 32), 1.0).astype(jnp.bfloat16)


def draw_margin(key, part):
    off = symmetric(jax.random.fold_in(key, 33), 0.35 / N ** 0.5)
    unit = (jnp.arange(N)[:, None] == jnp.arange(N)[None, :]).astype(jnp.float32)
    return (off * (1.0 - unit) + unit).astype(jnp.bfloat16)


def draw_fill_patterns(key, part):
    return pattern(key, 21, 3)


def draw_first_filters(key, part):
    return pattern(key, 22, 3)


def draw_second_filters(key, part):
    return pattern(key, 23, TERMS - 1 + SQUARINGS)


def place_value(order, position, target):
    located = jnp.argmax(order == target).astype(jnp.int32)
    former = order[position]
    order = order.at[located].set(former)
    return order.at[position].set(target)


def draw_owner_order(key, part):
    order = jax.random.permutation(jax.random.fold_in(key, 41), NB).astype(jnp.int32)
    anchor = jax.random.randint(jax.random.fold_in(key, 42), (), 0, NB).astype(jnp.int32)
    order = place_value(order, anchor, (anchor - PANEL) % NB)
    opposite = (anchor + NB // 2) % NB
    order = place_value(order, opposite, anchor)
    following = (anchor + PANEL) % NB
    order = place_value(order, following, (anchor + 2 * PANEL) % NB)
    return order


def setup_inputs(seed: int = 0) -> dict:
    keys = jax.random.split(jax.random.key(seed), 8)
    return {
        "fock_matrix": draw_fock_matrix(jax.random.fold_in(keys[7], 71), 0),
        "density": draw_density(jax.random.fold_in(keys[7], 71), 0),
        "margin": draw_margin(jax.random.fold_in(keys[7], 71), 0),
        "fill_patterns": draw_fill_patterns(jax.random.fold_in(keys[7], 71), 0),
        "first_filters": draw_first_filters(jax.random.fold_in(keys[7], 71), 0),
        "owner_order": draw_owner_order(jax.random.fold_in(keys[7], 71), 0),
        "second_filters": draw_second_filters(jax.random.fold_in(keys[7], 71), 0),
    }


def expand(mask, values):
    row_blocks = mask.shape[0]
    column_blocks = mask.shape[1]
    block_size = values.shape[0] // row_blocks
    shaped = values.reshape(row_blocks, block_size, column_blocks, block_size) * mask[:, None, :, None].astype(values.dtype)
    return shaped.reshape(values.shape)


def product(former, latter):
    return jnp.dot(former, latter, preferred_element_type=jnp.float32)


def reference(fock_matrix, density, margin, fill_patterns, first_filters, owner_order, second_filters):
    masked_fock = expand(fill_patterns[0], fock_matrix)
    masked_density = expand(fill_patterns[1], density)
    masked_margin = expand(fill_patterns[2], margin)
    fock_density = expand(first_filters[0], product(masked_fock, masked_density)).astype(jnp.bfloat16)
    margin_density = expand(first_filters[1], product(masked_margin, masked_density)).astype(jnp.bfloat16)
    generator = product(fock_density, masked_margin) - product(margin_density, masked_fock)
    generator = expand(first_filters[2], generator).astype(jnp.bfloat16)
    blocks = generator.reshape(NB, BLK, NB, BLK)
    reordered = jnp.take(jnp.take(blocks, owner_order, axis=0), owner_order, axis=2).reshape(N, N)
    scaled = (reordered.astype(jnp.float32) * 0.25).astype(jnp.bfloat16)
    identity = jnp.eye(N, dtype=jnp.float32)
    series = (identity + scaled.astype(jnp.float32) / 6.0).astype(jnp.bfloat16)
    for number in range(TERMS - 1):
        degree = TERMS - 1 - number
        series = (identity + expand(second_filters[number], product(scaled, series)) / degree).astype(jnp.bfloat16)
    for number in range(SQUARINGS):
        series = expand(second_filters[TERMS - 1 + number], product(series, series)).astype(jnp.bfloat16)
    return series
```

```python
import functools

import jax
import jax.numpy as jnp
from jax import lax
from jax.experimental import pallas as pl
from jax.experimental.pallas import tpu as pltpu
from jax.sharding import PartitionSpec as P

BLK = 32
TERMS = 6
SQUARINGS = 2
FIRST = 3
AXES = ("row", "col")
F32 = jnp.float32
BF16 = jnp.bfloat16
TAIL = 16
VMEM_LIMIT = 60 * 1024 * 1024


def coordinates(r, c):
    return r // 2, r % 2, c // 2, c % 2


def permutation(rows, cols, source):
    pairs = []
    for r in range(rows):
        for c in range(cols):
            sr, sc = source(*coordinates(r, c))
            pairs.append((sr * cols + sc, r * cols + c))
    return pairs


class Moves:
    def __init__(self, rows, cols):
        self.rows, self.cols = rows, cols

    def move(self, value, source):
        return lax.ppermute(value, AXES, permutation(self.rows, self.cols, source))

    def relabel(self, value, k=0):
        return self.move(value, lambda z, y, x, e: (2 * (z ^ k) + e, 2 * x + y))

    def along_z(self, value, k):
        return self.move(value, lambda z, y, x, e: (2 * (z ^ k) + y, 2 * x + e))

    def in_plane(self, value, s):
        return self.move(value, lambda z, y, x, e: (2 * z + (y ^ (s & 1)), 2 * (x ^ (s >> 1)) + e))

    def core(self, value):
        return self.move(value, lambda z, y, x, e: (2 * z + y, 2 * x + 1 - e))


def place():
    r, c = lax.axis_index("row"), lax.axis_index("col")
    z, y, x, e = r // 2, r % 2, c // 2, c % 2
    return z, 2 * x + y, e


def iota(shape, axis):
    return lax.broadcasted_iota(jnp.int32, shape, axis)


def dot(a, b):
    return jnp.dot(a, b, preferred_element_type=F32)


def repeat_rows(rows, blocks):
    return (iota((rows, blocks), 0) // BLK == iota((rows, blocks), 1)).astype(BF16)


def repeat_columns(blocks, columns, first=0):
    return (iota((blocks, columns), 0) == iota((blocks, columns), 1) // BLK + first).astype(BF16)


def block_mask(tail, number, rows, columns):
    blocks = columns // BLK
    wide = dot(repeat_rows(rows, tail.shape[0]), tail).astype(BF16)
    return dot(wide, repeat_columns(tail.shape[1], columns, number * blocks))


def call(kernel, outs, ins, scratch, name):
    return pl.pallas_call(
        kernel,
        out_shape=outs,
        in_specs=ins,
        out_specs=jax.tree.map(lambda _: pl.BlockSpec(memory_space=pltpu.VMEM), outs),
        scratch_shapes=scratch,
        name=name,
        compiler_params=pltpu.CompilerParams(vmem_limit_bytes=VMEM_LIMIT),
    )


ANY = pl.BlockSpec(memory_space=pl.ANY)
INVMEM = pl.BlockSpec(memory_space=pltpu.VMEM)
INSMEM = pl.BlockSpec(memory_space=pltpu.SMEM)


def mask_kernel(fock, density, margin, fills, firsts, seconds, masked_density, pair):
    rows, columns = fock.shape
    row_blocks, column_blocks = rows // BLK, columns // BLK
    tall = repeat_rows(rows, row_blocks)
    wide = repeat_columns(column_blocks, columns)

    def masked(ref, number):
        mask = dot(dot(tall, fills[number].astype(BF16)).astype(BF16), wide)
        return (ref[...].astype(F32) * mask).astype(BF16)

    masked_density[...] = masked(density, 1)
    pair[0:rows, :] = masked(fock, 0)
    pair[rows : 2 * rows, :] = masked(margin, 2)
    top = (iota((TAIL, row_blocks), 0) == iota((TAIL, row_blocks), 1)).astype(BF16)
    tail = jnp.zeros((TAIL, columns), F32)
    for number in range(firsts.shape[0] + seconds.shape[0]):
        ref = firsts[number] if number < FIRST else seconds[number - FIRST]
        column = iota((column_blocks, columns), 1) - number * column_blocks
        spread = (iota((column_blocks, columns), 0) == column).astype(BF16)
        tail += dot(dot(top, ref.astype(BF16)).astype(BF16), spread)
    pair[2 * rows :, :] = tail.astype(BF16)


def copy_all(copies):
    for one in copies:
        one.start()
    for one in copies:
        one.wait()


def first_kernel(count, *refs):
    pairs, near, far = refs[:count], refs[count : 2 * count], refs[2 * count : 3 * count]
    out, left, right, tail, sems = refs[3 * count :]
    z, q, e = place()
    rows = near[0].shape[0]
    copies = [pltpu.make_async_copy(pairs[0].at[2 * rows :], tail, sems.at[0])]
    for s in range(count):
        copies.append(
            pltpu.make_async_copy(pairs[s].at[: 2 * rows], left.at[q ^ s], sems.at[len(copies)])
        )
        for ref, core in ((near[s], e), (far[s], 1 - e)):
            copies.append(
                pltpu.make_async_copy(
                    ref, right.at[z ^ s, pl.ds(core * rows, rows)], sems.at[len(copies)]
                )
            )
    copy_all(copies)
    total = dot(left[0], right[0])
    for k in range(1, count):
        total += dot(left[k], right[k])
    columns = total.shape[1]
    for number in range(2):
        part = pl.ds(number * rows, rows)
        mask = block_mask(tail[...], number, rows, columns)
        out[part, :] = (total[number * rows : (number + 1) * rows] * mask).astype(BF16)


def generator_kernel(count, *refs):
    lefts, near, far = refs[:count], refs[count : 2 * count], refs[2 * count : 3 * count]
    out, left, right, tail, sems = refs[3 * count :]
    z, q, e = place()
    rows = lefts[0].shape[0] // 2
    copies = [pltpu.make_async_copy(near[0].at[2 * rows :], tail, sems.at[0])]
    for s in range(count):
        copies.append(pltpu.make_async_copy(lefts[s], left.at[q ^ s], sems.at[len(copies)]))
        for ref, core in ((near[s], e), (far[s], 1 - e)):
            for half in range(2):
                copies.append(
                    pltpu.make_async_copy(
                        ref.at[pl.ds(half * rows, rows)],
                        right.at[1 - half, z ^ s, pl.ds(core * rows, rows)],
                        sems.at[len(copies)],
                    )
                )
    copy_all(copies)
    plus = dot(left[0, :rows], right[0, 0])
    minus = dot(left[0, rows:], right[1, 0])
    for k in range(1, count):
        plus += dot(left[k, :rows], right[0, k])
        minus += dot(left[k, rows:], right[1, k])
    mask = block_mask(tail[...], 2, rows, out.shape[1])
    generator = ((plus - minus) * mask).astype(BF16)
    out[...] = (generator.astype(F32) * 0.25).astype(BF16)


def series_kernel(layout, count, *refs):
    pieces = refs[: len(layout)]
    tails = refs[len(layout) : len(layout) + 2 * count]
    order = refs[len(layout) + 2 * count]
    panel, mine, whole, unit, current, wides, masks, sems = refs[len(layout) + 2 * count + 1 :]
    z, q, e = place()
    size, columns = panel.shape
    rows = mine.shape[0]
    copies = []
    for ref, (slots, plane, lane) in zip(pieces, layout):
        core = e if lane == 0 else 1 - e
        for index, k in enumerate(slots):
            copies.append(
                pltpu.make_async_copy(
                    ref.at[index],
                    whole.at[
                        pl.ds((2 * (z ^ k) + core) * rows, rows),
                        pl.ds(pl.multiple_of((q ^ plane) * columns, 128), columns),
                    ],
                    sems.at[len(copies)],
                )
            )
    for index, ref in enumerate(tails):
        core = e if index < count else 1 - e
        copies.append(
            pltpu.make_async_copy(
                ref.at[2 * rows :], wides.at[2 * (z ^ (index % count)) + core], sems.at[len(copies)]
            )
        )
    for one in copies:
        one.start()

    column_blocks = columns // BLK
    row_blocks = rows // BLK
    unit[...] = jnp.zeros_like(unit)
    inner = iota((BLK, columns), 1)
    for b in range(column_blocks):
        first = pl.multiple_of(order[q * column_blocks + b] * BLK, BLK)
        unit[pl.ds(first, BLK), :] = (inner == iota((BLK, columns), 0) + b * BLK).astype(BF16)

    for one in copies:
        one.wait()

    for p in range(wides.shape[0]):
        for a in range(row_blocks):
            first = pl.multiple_of(order[p * row_blocks + a] * BLK, BLK)
            row = wides[p][a : a + 1, :128]
            masks[pl.ds(first, BLK), :] = jnp.broadcast_to(row, (BLK, 128))

    tiles = size // rows

    def step(number, source, target):
        degree = TERMS - number
        if number > 0:
            spread = repeat_columns(128, columns, (FIRST + number - 1) * column_blocks)

        def body(t, carry):
            part = pl.ds(pl.multiple_of(t * rows, rows), rows)
            value = dot(whole[part, :], source[...])
            if number > 0:
                value = value * dot(masks[part, :], spread)
            target[part, :] = (unit[part, :].astype(F32) + value / degree).astype(BF16)
            return carry

        lax.fori_loop(0, tiles, body, 0)

    step(0, unit, current.at[0])
    for number in range(1, TERMS):
        step(number, current.at[(number - 1) % 2], current.at[number % 2])
    last = current.at[(TERMS - 1) % 2]
    for a in range(size // BLK):
        first = pl.multiple_of(order[a] * BLK, BLK)
        panel[a * BLK : (a + 1) * BLK, :] = last[pl.ds(first, BLK), :]
    start = (2 * z + e) * rows
    mine[...] = panel[pl.ds(pl.multiple_of(start, rows), rows), :]


def square_kernel(count, *refs):
    lefts = refs[:count]
    panel, pair, out, left, right, tail, sems = refs[count:]
    z, q, e = place()
    rows, columns = out.shape
    copies = [
        pltpu.make_async_copy(pair.at[2 * rows :], tail, sems.at[0]),
        pltpu.make_async_copy(panel, right, sems.at[1]),
    ]
    for s in range(count):
        copies.append(pltpu.make_async_copy(lefts[s], left.at[q ^ s], sems.at[len(copies)]))
    copy_all(copies)
    total = dot(left[0], right[0:columns])
    for k in range(1, count):
        total += dot(left[k], right[k * columns : (k + 1) * columns])
    mask = block_mask(tail[...], FIRST + TERMS - 1, rows, columns)
    out[...] = (total * mask).astype(BF16)


def evolve_kernel(count, *refs):
    lefts, near, far = refs[:count], refs[count : 2 * count], refs[2 * count : 3 * count]
    pair, out, left, right, tail, sems = refs[3 * count :]
    z, q, e = place()
    rows, columns = out.shape
    copies = [pltpu.make_async_copy(pair.at[2 * rows :], tail, sems.at[0])]
    for s in range(count):
        copies.append(pltpu.make_async_copy(lefts[s], left.at[q ^ s], sems.at[len(copies)]))
        for ref, core in ((near[s], e), (far[s], 1 - e)):
            copies.append(
                pltpu.make_async_copy(
                    ref, right.at[z ^ s, pl.ds(core * rows, rows)], sems.at[len(copies)]
                )
            )
    copy_all(copies)
    total = dot(left[0], right[0])
    for k in range(1, count):
        total += dot(left[k], right[k])
    mask = block_mask(tail[...], FIRST + TERMS, rows, columns)
    out[...] = (total * mask).astype(BF16)


def on_device(
    mesh_rows,
    mesh_cols,
    fock_matrix,
    density,
    margin,
    fill_patterns,
    first_filters,
    owner_order,
    second_filters,
):
    moves = Moves(mesh_rows, mesh_cols)
    count = mesh_cols
    slots = range(1, count)
    rows, columns = fock_matrix.shape
    size = rows * mesh_rows
    block = jax.ShapeDtypeStruct((rows, columns), BF16)

    masked_density, pair = call(
        mask_kernel,
        [block, jax.ShapeDtypeStruct((2 * rows + TAIL, columns), BF16)],
        [INVMEM] * 6,
        [],
        "mask",
    )(fock_matrix, density, margin, fill_patterns, first_filters, second_filters)

    density_near = [moves.relabel(masked_density, k) for k in range(count)]
    density_far = [moves.core(value) for value in density_near]
    pair = moves.relabel(pair)
    pair_rows = [pair] + [moves.in_plane(pair, s) for s in slots]
    pair_near = [pair] + [moves.along_z(pair, k) for k in slots]
    pair_far = [moves.core(value) for value in pair_near]

    products = call(
        functools.partial(first_kernel, count),
        jax.ShapeDtypeStruct((2 * rows, columns), BF16),
        [ANY] * (3 * count),
        [
            pltpu.VMEM((count, 2 * rows, columns), BF16),
            pltpu.VMEM((count, columns, columns), BF16),
            pltpu.VMEM((TAIL, columns), BF16),
            pltpu.SemaphoreType.DMA((1 + 3 * count,)),
        ],
        "first",
    )(*pair_rows, *density_near, *density_far)
    products = [products] + [moves.in_plane(products, s) for s in slots]

    generator = call(
        functools.partial(generator_kernel, count),
        block,
        [ANY] * (3 * count),
        [
            pltpu.VMEM((count, 2 * rows, columns), BF16),
            pltpu.VMEM((2, count, columns, columns), BF16),
            pltpu.VMEM((TAIL, columns), BF16),
            pltpu.SemaphoreType.DMA((1 + 5 * count,)),
        ],
        "generator",
    )(*products, *pair_near, *pair_far)

    lines = [generator] + [moves.along_z(generator, k) for k in slots]
    half = count // 2
    layout, pieces = [], []
    for first in (0, half):
        chosen = tuple(range(first, first + half))
        group = jnp.stack([lines[k] for k in chosen])
        planes = {0: [(chosen, group)]}
        for s in slots:
            if count == 4 and s == 3:
                continue
            planes[s] = [(chosen, moves.in_plane(group, s))]
        if count == 4:
            planes[3] = [
                (chosen[:1], moves.in_plane(planes[2][0][1][:1], 1)),
                (chosen[1:], moves.in_plane(planes[1][0][1][1:], 2)),
            ]
        for s, parts in planes.items():
            for held, value in parts:
                layout += [(held, s, 0), (held, s, 1)]
                pieces += [value, moves.core(value)]

    panel, mine = call(
        functools.partial(series_kernel, layout, count),
        [jax.ShapeDtypeStruct((size, columns), BF16), block],
        [ANY] * (len(layout) + 2 * count) + [INSMEM],
        [
            pltpu.VMEM((size, size), BF16),
            pltpu.VMEM((size, columns), BF16),
            pltpu.VMEM((2, size, columns), BF16),
            pltpu.VMEM((mesh_rows, TAIL, columns), BF16),
            pltpu.VMEM((size, 128), BF16),
            pltpu.SemaphoreType.DMA((mesh_rows * mesh_cols + 2 * count,)),
        ],
        "series",
    )(*pieces, *pair_near, *pair_far, owner_order)

    lefts = [mine] + [moves.in_plane(mine, s) for s in slots]
    square = call(
        functools.partial(square_kernel, count),
        block,
        [ANY] * (count + 2),
        [
            pltpu.VMEM((count, rows, columns), BF16),
            pltpu.VMEM((size, columns), BF16),
            pltpu.VMEM((TAIL, columns), BF16),
            pltpu.SemaphoreType.DMA((2 + count,)),
        ],
        "square",
    )(*lefts, panel, pair)

    near = [square] + [moves.along_z(square, k) for k in slots]
    lefts = [square] + [moves.in_plane(square, s) for s in slots]
    far = [moves.core(value) for value in near]
    evolved = call(
        functools.partial(evolve_kernel, count),
        block,
        [ANY] * (3 * count + 1),
        [
            pltpu.VMEM((count, rows, columns), BF16),
            pltpu.VMEM((count, columns, columns), BF16),
            pltpu.VMEM((TAIL, columns), BF16),
            pltpu.SemaphoreType.DMA((1 + 3 * count,)),
        ],
        "evolve",
    )(*lefts, *near, *far, pair)
    return moves.relabel(evolved)


def solution(mesh):
    return jax.shard_map(
        functools.partial(on_device, mesh.shape["row"], mesh.shape["col"]),
        mesh=mesh,
        in_specs=(
            P("row", "col"),
            P("row", "col"),
            P("row", "col"),
            P(None, "row", "col"),
            P(None, "row", "col"),
            P(),
            P(None, "row", "col"),
        ),
        out_specs=P("row", "col"),
        check_vma=False,
    )
```

```python
import functools

import jax
import jax.numpy as jnp
from jax import lax
from jax.experimental import pallas as pl
from jax.experimental.pallas import tpu as pltpu
from jax.sharding import PartitionSpec as P

BLK = 32
TERMS = 6
SQUARINGS = 2
FIRST = 3
AXES = ("row", "col")
F32 = jnp.float32
BF16 = jnp.bfloat16
TAIL = 16
VMEM_LIMIT = 60 * 1024 * 1024


def coordinates(r, c):
    return r // 2, r % 2, c // 2, c % 2


def permutation(rows, cols, source):
    pairs = []
    for r in range(rows):
        for c in range(cols):
            sr, sc = source(*coordinates(r, c))
            pairs.append((sr * cols + sc, r * cols + c))
    return pairs


class Moves:
    def __init__(self, rows, cols):
        self.rows, self.cols = rows, cols

    def move(self, value, source):
        return lax.ppermute(value, AXES, permutation(self.rows, self.cols, source))

    def relabel(self, value, k=0):
        return self.move(value, lambda z, y, x, e: (2 * (z ^ k) + e, 2 * x + y))

    def along_z(self, value, k):
        return self.move(value, lambda z, y, x, e: (2 * (z ^ k) + y, 2 * x + e))

    def in_plane(self, value, s):
        return self.move(value, lambda z, y, x, e: (2 * z + (y ^ (s & 1)), 2 * (x ^ (s >> 1)) + e))

    def core(self, value):
        return self.move(value, lambda z, y, x, e: (2 * z + y, 2 * x + 1 - e))


def place():
    r, c = lax.axis_index("row"), lax.axis_index("col")
    z, y, x, e = r // 2, r % 2, c // 2, c % 2
    return z, 2 * x + y, e


def iota(shape, axis):
    return lax.broadcasted_iota(jnp.int32, shape, axis)


def dot(a, b):
    return jnp.dot(a, b, preferred_element_type=F32)


def repeat_rows(rows, blocks):
    return (iota((rows, blocks), 0) // BLK == iota((rows, blocks), 1)).astype(BF16)


def repeat_columns(blocks, columns, first=0):
    return (iota((blocks, columns), 0) == iota((blocks, columns), 1) // BLK + first).astype(BF16)


def block_mask(tail, number, rows, columns):
    blocks = columns // BLK
    wide = dot(repeat_rows(rows, tail.shape[0]), tail).astype(BF16)
    return dot(wide, repeat_columns(tail.shape[1], columns, number * blocks))


def call(kernel, outs, ins, scratch, name, flops=1000):
    return pl.pallas_call(
        kernel,
        out_shape=outs,
        in_specs=ins,
        out_specs=jax.tree.map(lambda _: pl.BlockSpec(memory_space=pltpu.VMEM), outs),
        scratch_shapes=scratch,
        name=name,
        compiler_params=pltpu.CompilerParams(vmem_limit_bytes=VMEM_LIMIT),
        cost_estimate=pl.CostEstimate(flops=flops, bytes_accessed=1000, transcendentals=0),
    )


ANY = pl.BlockSpec(memory_space=pl.ANY)
INVMEM = pl.BlockSpec(memory_space=pltpu.VMEM)
INSMEM = pl.BlockSpec(memory_space=pltpu.SMEM)


def mask_kernel(fock, density, margin, fills, firsts, seconds, masked_density, pair):
    rows, columns = fock.shape
    row_blocks, column_blocks = rows // BLK, columns // BLK
    tall = repeat_rows(rows, row_blocks)
    wide = repeat_columns(column_blocks, columns)

    def masked(ref, number):
        mask = dot(dot(tall, fills[number].astype(BF16)).astype(BF16), wide)
        return (ref[...].astype(F32) * mask).astype(BF16)

    masked_density[...] = masked(density, 1)
    pair[0:rows, :] = masked(fock, 0)
    pair[rows : 2 * rows, :] = masked(margin, 2)
    top = (iota((TAIL, row_blocks), 0) == iota((TAIL, row_blocks), 1)).astype(BF16)
    tail = jnp.zeros((TAIL, columns), F32)
    for number in range(firsts.shape[0] + seconds.shape[0]):
        ref = firsts[number] if number < FIRST else seconds[number - FIRST]
        column = iota((column_blocks, columns), 1) - number * column_blocks
        spread = (iota((column_blocks, columns), 0) == column).astype(BF16)
        tail += dot(dot(top, ref.astype(BF16)).astype(BF16), spread)
    pair[2 * rows :, :] = tail.astype(BF16)


def chunk(index, length):
    return pl.ds(pl.multiple_of(index * length, length), length)


def start_all(copies):
    for one in copies:
        one.start()


def wait_all(copies):
    for one in copies:
        one.wait()


def repeat(times, body, unrolled):
    if unrolled:
        for t in range(times):
            body(t)
    else:

        def step(t, carry):
            body(t)
            return carry

        lax.fori_loop(0, times, step, 0)


def tail_of(copy, tail):
    copy.wait()
    return tail[...]


def first_kernel(count, *refs):
    pairs, near, far = refs[:count], refs[count : 2 * count], refs[2 * count : 3 * count]
    out, left, right, tail, sems = refs[3 * count :]
    z, q, e = place()
    rows, columns = near[0].shape
    copies = [pltpu.make_async_copy(pairs[0].at[2 * rows :], tail, sems.at[0])]
    for s in range(count):
        copies.append(
            pltpu.make_async_copy(
                pairs[s].at[: 2 * rows], left.at[:, chunk(q ^ s, columns)], sems.at[len(copies)]
            )
        )
        for ref, core in ((near[s], e), (far[s], 1 - e)):
            copies.append(
                pltpu.make_async_copy(
                    ref, right.at[chunk(2 * (z ^ s) + core, rows)], sems.at[len(copies)]
                )
            )
    start_all(copies)
    filters = tail_of(copies[0], tail)
    masks = [block_mask(filters, n, rows, columns) for n in range(2)]
    wait_all(copies[1:])
    total = dot(left[...], right[...])
    for n in range(2):
        part = slice(n * rows, (n + 1) * rows)
        out[part, :] = (total[part] * masks[n]).astype(BF16)


def generator_kernel(count, *refs):
    lefts, near, far = refs[:count], refs[count : 2 * count], refs[2 * count : 3 * count]
    out, left, right, tail, sems = refs[3 * count :]
    z, q, e = place()
    rows, columns = out.shape
    copies = [pltpu.make_async_copy(near[0].at[2 * rows :], tail, sems.at[0])]
    for s in range(count):
        for half in range(2):
            part = pl.ds(half * rows, rows)
            copies.append(
                pltpu.make_async_copy(
                    lefts[s].at[part], left.at[half, :, chunk(q ^ s, columns)], sems.at[len(copies)]
                )
            )
            for ref, core in ((near[s], e), (far[s], 1 - e)):
                copies.append(
                    pltpu.make_async_copy(
                        ref.at[part],
                        right.at[1 - half, chunk(2 * (z ^ s) + core, rows)],
                        sems.at[len(copies)],
                    )
                )
    start_all(copies)
    mask = block_mask(tail_of(copies[0], tail), 2, rows, columns)
    wait_all(copies[1:])
    plus = dot(left[0], right[0])
    minus = dot(left[1], right[1])
    generator = ((plus - minus) * mask).astype(BF16)
    out[...] = (generator.astype(F32) * 0.25).astype(BF16)


def series_kernel(layout, count, *refs):
    pieces = refs[: len(layout)]
    tails = refs[len(layout) : len(layout) + 2 * count]
    order = refs[len(layout) + 2 * count]
    panel, mine, whole, turned, wides, spread, sems = refs[len(layout) + 2 * count + 1 :]
    z, q, e = place()
    rows, columns = mine.shape
    size = panel.shape[1]
    row_blocks, column_blocks, blocks = rows // BLK, columns // BLK, size // BLK
    copies, early = [], []
    for ref, (slots, plane, lane) in zip(pieces, layout):
        core = e if lane == 0 else 1 - e
        for index, k in enumerate(slots):
            copies.append(
                pltpu.make_async_copy(
                    ref.at[index],
                    whole.at[chunk(2 * (z ^ k) + core, rows), chunk(q ^ plane, columns)],
                    sems.at[len(copies)],
                )
            )
    for index, ref in enumerate(tails):
        core = e if index < count else 1 - e
        early.append(
            pltpu.make_async_copy(
                ref.at[2 * rows :],
                wides.at[2 * (z ^ (index % count)) + core],
                sems.at[len(copies) + len(early)],
            )
        )
    start_all(early)
    start_all(copies)
    wait_all(early)
    filters = jnp.zeros((128, size), F32)
    for p in range(2 * count):
        column = iota((TAIL, size), 1) // BLK
        row = iota((TAIL, size), 0)
        near = ((row < row_blocks) & (column == row + p * row_blocks)).astype(BF16)
        filters += lax.dot_general(
            wides[p][:, :128], near, (((0,), (0,)), ((), ())), preferred_element_type=F32
        )
    spread[...] = filters

    wait_all(copies)
    small = size <= 1536

    def turn(t):
        tile = jnp.concatenate(
            [whole[chunk(order[t * column_blocks + a], BLK), :] for a in range(column_blocks)],
            axis=0,
        )
        turned[:, chunk(t, columns)] = tile.T

    def place_rows(b):
        whole[chunk(b, BLK), :] = turned[chunk(order[b], BLK), :]

    repeat(count, turn, small)
    repeat(blocks, place_rows, small)

    first = (2 * q + e) * rows
    unit = (iota((rows, size), 1) == iota((rows, size), 0) + first).astype(F32)
    own = unit + whole[chunk(2 * q + e, rows), :].astype(F32) / TERMS
    panel[...] = own.astype(BF16)
    width = size if small else 512
    for number in range(1, TERMS):
        current = panel[...]
        base = (FIRST + number - 1) * column_blocks + e * row_blocks

        def advance(t):
            part = chunk(t, width)
            product = dot(current, whole[:, part])
            mask = jnp.concatenate(
                [
                    jnp.broadcast_to(spread[pl.ds(base + b, 1), part], (BLK, width))
                    for b in range(row_blocks)
                ],
                axis=0,
            )
            here = iota((rows, width), 1) + t * width == iota((rows, width), 0) + first
            panel[:, part] = (here.astype(F32) + product * mask / (TERMS - number)).astype(BF16)

        repeat(size // width, advance, small)
    mine[...] = panel[:, chunk(z, columns)]


def turned_mask(tails, number, e, rows, columns):
    row_blocks, column_blocks = rows // BLK, columns // BLK
    pick = iota((rows, 128), 0) // BLK + number * column_blocks + e * row_blocks
    pick = (pick == iota((rows, 128), 1)).astype(BF16)
    mask = jnp.zeros((rows, columns), F32)
    for core in range(2):
        row = iota((TAIL, columns), 0)
        near = (row < row_blocks) & (iota((TAIL, columns), 1) // BLK == row + core * row_blocks)
        chosen = lax.dot_general(
            pick, tails[core][:, :128], (((1,), (1,)), ((), ())), preferred_element_type=F32
        )
        mask += dot(chosen.astype(BF16), near.astype(BF16))
    return mask


def square_kernel(count, *refs):
    near, far = refs[:count], refs[count : 2 * count]
    panel, pair, other, out, right, tails, sems = refs[2 * count :]
    z, q, e = place()
    rows, columns = out.shape
    copies = [
        pltpu.make_async_copy(pair.at[2 * rows :], tails.at[e], sems.at[0]),
        pltpu.make_async_copy(other.at[2 * rows :], tails.at[1 - e], sems.at[1]),
    ]
    for s in range(count):
        for ref, core in ((near[s], e), (far[s], 1 - e)):
            copies.append(
                pltpu.make_async_copy(
                    ref, right.at[chunk(2 * (q ^ s) + core, rows)], sems.at[len(copies)]
                )
            )
    start_all(copies)
    wait_all(copies[:2])
    mask = turned_mask(tails, FIRST + TERMS - 1, e, rows, columns)
    wait_all(copies[2:])
    out[...] = (dot(panel[...], right[...]) * mask).astype(BF16)


def evolve_kernel(count, *refs):
    groups = [refs[n * count : (n + 1) * count] for n in range(4)]
    line_near, line_far, plane_near, plane_far = groups
    pair, other, out, left, right, tails, sems = refs[4 * count :]
    z, q, e = place()
    rows, columns = out.shape
    copies = [
        pltpu.make_async_copy(pair.at[2 * rows :], tails.at[e], sems.at[0]),
        pltpu.make_async_copy(other.at[2 * rows :], tails.at[1 - e], sems.at[1]),
    ]
    for s in range(count):
        for ref, core in ((line_near[s], e), (line_far[s], 1 - e)):
            copies.append(
                pltpu.make_async_copy(
                    ref, left.at[chunk(core, rows), chunk(z ^ s, columns)], sems.at[len(copies)]
                )
            )
        for ref, core in ((plane_near[s], e), (plane_far[s], 1 - e)):
            copies.append(
                pltpu.make_async_copy(
                    ref, right.at[chunk(2 * (q ^ s) + core, rows)], sems.at[len(copies)]
                )
            )
    start_all(copies)
    wait_all(copies[:2])
    mask = block_mask(tails[pl.ds(e, 1)][0], FIRST + TERMS, rows, columns)
    wait_all(copies[2:])
    total = dot(left[...], right[...]).T
    chosen = jnp.where(e == 0, total[:rows], total[rows:])
    out[...] = (chosen * mask).astype(BF16)


def on_device(
    mesh_rows,
    mesh_cols,
    fock_matrix,
    density,
    margin,
    fill_patterns,
    first_filters,
    owner_order,
    second_filters,
):
    moves = Moves(mesh_rows, mesh_cols)
    count = mesh_cols
    slots = range(1, count)
    rows, columns = fock_matrix.shape
    size = rows * mesh_rows
    block = jax.ShapeDtypeStruct((rows, columns), BF16)

    masked_density, pair = call(
        mask_kernel,
        [block, jax.ShapeDtypeStruct((2 * rows + TAIL, columns), BF16)],
        [INVMEM] * 6,
        [],
        "mask",
    )(fock_matrix, density, margin, fill_patterns, first_filters, second_filters)

    density_near = [moves.relabel(masked_density, k) for k in range(count)]
    density_far = [moves.core(value) for value in density_near]
    held = pair
    pair = moves.relabel(held)
    pair_near = [pair] + [moves.relabel(held, k) for k in slots]
    pair_rows = [pair] + [moves.in_plane(pair, s) for s in slots]
    pair_far = [moves.core(value) for value in pair_near]

    products = call(
        functools.partial(first_kernel, count),
        jax.ShapeDtypeStruct((2 * rows, columns), BF16),
        [ANY] * (3 * count),
        [
            pltpu.VMEM((2 * rows, size), BF16),
            pltpu.VMEM((size, columns), BF16),
            pltpu.VMEM((TAIL, columns), BF16),
            pltpu.SemaphoreType.DMA((1 + 3 * count,)),
        ],
        "first",
    )(*pair_rows, *density_near, *density_far)
    products = [products] + [moves.in_plane(products, s) for s in slots]

    generator = call(
        functools.partial(generator_kernel, count),
        block,
        [ANY] * (3 * count),
        [
            pltpu.VMEM((2, rows, size), BF16),
            pltpu.VMEM((2, size, columns), BF16),
            pltpu.VMEM((TAIL, columns), BF16),
            pltpu.SemaphoreType.DMA((1 + 6 * count,)),
        ],
        "generator",
    )(*products, *pair_near, *pair_far)

    lines = [generator] + [moves.along_z(generator, k) for k in slots]
    half = count // 2
    layout, pieces = [], []
    for first in (0, half):
        chosen = tuple(range(first, first + half))
        group = jnp.stack([lines[k] for k in chosen])
        planes = {0: [(chosen, group)]}
        for s in slots:
            if count == 4 and s == 3:
                continue
            planes[s] = [(chosen, moves.in_plane(group, s))]
        if count == 4:
            planes[3] = [
                (chosen[:1], moves.in_plane(planes[2][0][1][:1], 1)),
                (chosen[1:], moves.in_plane(planes[1][0][1][1:], 2)),
            ]
        for s, parts in planes.items():
            for held, value in parts:
                layout += [(held, s, 0), (held, s, 1)]
                pieces += [value, moves.core(value)]

    panel, mine = call(
        functools.partial(series_kernel, layout, count),
        [jax.ShapeDtypeStruct((rows, size), BF16), block],
        [ANY] * (len(layout) + 2 * count) + [INSMEM],
        [
            pltpu.VMEM((size, size), BF16),
            pltpu.VMEM((size, size), BF16),
            pltpu.VMEM((mesh_rows, TAIL, columns), BF16),
            pltpu.VMEM((128, size), F32),
            pltpu.SemaphoreType.DMA((mesh_rows * mesh_cols + 2 * count,)),
        ],
        "series",
    )(*pieces, *pair_near, *pair_far, owner_order)

    near = [mine] + [moves.in_plane(mine, s) for s in slots]
    far = [moves.core(value) for value in near]
    square = call(
        functools.partial(square_kernel, count),
        block,
        [ANY] * (2 * count) + [INVMEM, ANY, ANY],
        [
            pltpu.VMEM((size, columns), BF16),
            pltpu.VMEM((2, TAIL, columns), BF16),
            pltpu.SemaphoreType.DMA((2 + 2 * count,)),
        ],
        "square",
    )(*near, *far, panel, pair, pair_far[0])

    line_near = [square] + [moves.along_z(square, k) for k in slots]
    line_far = [moves.core(value) for value in line_near]
    plane_near = [square] + [moves.in_plane(square, s) for s in slots]
    plane_far = [line_far[0]] + [moves.core(value) for value in plane_near[1:]]
    evolved = call(
        functools.partial(evolve_kernel, count),
        block,
        [ANY] * (4 * count + 2),
        [
            pltpu.VMEM((columns, size), BF16),
            pltpu.VMEM((size, columns), BF16),
            pltpu.VMEM((2, TAIL, columns), BF16),
            pltpu.SemaphoreType.DMA((2 + 4 * count,)),
        ],
        "evolve",
    )(*line_near, *line_far, *plane_near, *plane_far, pair, pair_far[0])
    return moves.relabel(evolved)


def solution(mesh):
    return jax.shard_map(
        functools.partial(on_device, mesh.shape["row"], mesh.shape["col"]),
        mesh=mesh,
        in_specs=(
            P("row", "col"),
            P("row", "col"),
            P("row", "col"),
            P(None, "row", "col"),
            P(None, "row", "col"),
            P(),
            P(None, "row", "col"),
        ),
        out_specs=P("row", "col"),
        check_vma=False,
    )
```

```python
import functools

import jax
import jax.numpy as jnp
from jax import lax
from jax.experimental import pallas as pl
from jax.experimental.pallas import tpu as pltpu
from jax.sharding import PartitionSpec as P

BLK = 32
TERMS = 6
SQUARINGS = 2
FIRST = 3
AXES = ("row", "col")
F32 = jnp.float32
BF16 = jnp.bfloat16
TAIL = 16
VMEM_LIMIT = 60 * 1024 * 1024


def coordinates(r, c):
    return r // 2, r % 2, c // 2, c % 2


def permutation(rows, cols, source):
    pairs = []
    for r in range(rows):
        for c in range(cols):
            sr, sc = source(*coordinates(r, c))
            pairs.append((sr * cols + sc, r * cols + c))
    return pairs


class Moves:
    def __init__(self, rows, cols):
        self.rows, self.cols = rows, cols

    def move(self, value, source):
        return lax.ppermute(value, AXES, permutation(self.rows, self.cols, source))

    def relabel(self, value, k=0):
        return self.move(value, lambda z, y, x, e: (2 * (z ^ k) + e, 2 * x + y))

    def along_z(self, value, k):
        return self.move(value, lambda z, y, x, e: (2 * (z ^ k) + y, 2 * x + e))

    def in_plane(self, value, s):
        return self.move(value, lambda z, y, x, e: (2 * z + (y ^ (s & 1)), 2 * (x ^ (s >> 1)) + e))

    def core(self, value):
        return self.move(value, lambda z, y, x, e: (2 * z + y, 2 * x + 1 - e))


def place():
    r, c = lax.axis_index("row"), lax.axis_index("col")
    z, y, x, e = r // 2, r % 2, c // 2, c % 2
    return z, 2 * x + y, e


def iota(shape, axis):
    return lax.broadcasted_iota(jnp.int32, shape, axis)


def dot(a, b):
    return jnp.dot(a, b, preferred_element_type=F32)


def repeat_rows(rows, blocks):
    return (iota((rows, blocks), 0) // BLK == iota((rows, blocks), 1)).astype(BF16)


def repeat_columns(blocks, columns, first=0):
    return (iota((blocks, columns), 0) == iota((blocks, columns), 1) // BLK + first).astype(BF16)


def block_mask(tail, number, rows, columns):
    blocks = columns // BLK
    wide = dot(repeat_rows(rows, tail.shape[0]), tail).astype(BF16)
    return dot(wide, repeat_columns(tail.shape[1], columns, number * blocks))


def call(kernel, outs, ins, scratch, name, flops=1000):
    return pl.pallas_call(
        kernel,
        out_shape=outs,
        in_specs=ins,
        out_specs=jax.tree.map(lambda _: pl.BlockSpec(memory_space=pltpu.VMEM), outs),
        scratch_shapes=scratch,
        name=name,
        compiler_params=pltpu.CompilerParams(vmem_limit_bytes=VMEM_LIMIT),
        cost_estimate=pl.CostEstimate(flops=flops, bytes_accessed=1000, transcendentals=0),
    )


ANY = pl.BlockSpec(memory_space=pl.ANY)
INVMEM = pl.BlockSpec(memory_space=pltpu.VMEM)
INSMEM = pl.BlockSpec(memory_space=pltpu.SMEM)


def mask_kernel(fock, density, margin, fills, firsts, seconds, masked_density, pair):
    rows, columns = fock.shape
    row_blocks, column_blocks = rows // BLK, columns // BLK
    tall = repeat_rows(rows, row_blocks)
    wide = repeat_columns(column_blocks, columns)

    def masked(ref, number):
        mask = dot(dot(tall, fills[number].astype(BF16)).astype(BF16), wide)
        return (ref[...].astype(F32) * mask).astype(BF16)

    masked_density[...] = masked(density, 1)
    pair[TAIL : TAIL + rows, :] = masked(fock, 0)
    pair[TAIL + rows :, :] = masked(margin, 2)
    top = (iota((TAIL, row_blocks), 0) == iota((TAIL, row_blocks), 1)).astype(BF16)
    tail = jnp.zeros((TAIL, columns), F32)
    for number in range(firsts.shape[0] + seconds.shape[0]):
        ref = firsts[number] if number < FIRST else seconds[number - FIRST]
        column = iota((column_blocks, columns), 1) - number * column_blocks
        spread = (iota((column_blocks, columns), 0) == column).astype(BF16)
        tail += dot(dot(top, ref.astype(BF16)).astype(BF16), spread)
    pair[:TAIL, :] = tail.astype(BF16)


def chunk(index, length):
    return pl.ds(pl.multiple_of(index * length, length), length)


def start_all(copies):
    for one in copies:
        one.start()


def wait_all(copies):
    for one in copies:
        one.wait()


def repeat(times, body, unrolled):
    if unrolled:
        for t in range(times):
            body(t)
    else:

        def step(t, carry):
            body(t)
            return carry

        lax.fori_loop(0, times, step, 0)


def tail_of(copy, tail):
    copy.wait()
    return tail[...]


def first_kernel(count, starts, *refs):
    pair, parts = refs[0], refs[1 : 1 + 2 * count]
    near, far = refs[1 + 2 * count : 1 + 3 * count], refs[1 + 3 * count : 1 + 4 * count]
    out, left, right, tail, sems = refs[1 + 4 * count :]
    z, q, e = place()
    rows, columns = near[0].shape
    copies = [pltpu.make_async_copy(pair.at[:TAIL], tail, sems.at[0])]

    def bring(source, target):
        copies.append(pltpu.make_async_copy(source, target, sems.at[len(copies)]))

    for s in range(count):
        for half in range(2):
            bring(
                parts[2 * s + half].at[pl.ds(starts[s][half], rows)],
                left.at[pl.ds(half * rows, rows), chunk(q ^ s, columns)],
            )
        bring(near[s], right.at[chunk(2 * (z ^ s) + e, rows)])
        bring(far[s], right.at[chunk(2 * (z ^ s) + 1 - e, rows)])
    start_all(copies)
    filters = tail_of(copies[0], tail)
    masks = [block_mask(filters, n, rows, columns) for n in range(2)]
    wait_all(copies[1:])
    total = dot(left[...], right[...])
    for n in range(2):
        part = slice(n * rows, (n + 1) * rows)
        out[part, :] = (total[part] * masks[n]).astype(BF16)


def generator_kernel(count, starts, *refs):
    parts, own, other = refs[: 2 * count], refs[2 * count], refs[2 * count + 1]
    rest = refs[2 * count + 2 :]
    fock_near, fock_far, margin_near, margin_far = [
        rest[n * (count - 1) : (n + 1) * (count - 1)] for n in range(4)
    ]
    out, left, right, tail, sems = rest[4 * (count - 1) :]
    z, q, e = place()
    rows, columns = out.shape
    copies = [pltpu.make_async_copy(own.at[:TAIL], tail, sems.at[0])]

    def bring(source, target):
        copies.append(pltpu.make_async_copy(source, target, sems.at[len(copies)]))

    for half in range(2):
        for s in range(count):
            bring(
                parts[2 * s + half].at[pl.ds(starts[s][half], rows)],
                left.at[half, :, chunk(q ^ s, columns)],
            )
        part = pl.ds(TAIL + half * rows, rows)
        bring(own.at[part], right.at[1 - half, chunk(2 * z + e, rows)])
        bring(other.at[part], right.at[1 - half, chunk(2 * z + 1 - e, rows)])
    for k in range(1, count):
        for refs_of, core in ((fock_near, e), (fock_far, 1 - e)):
            bring(refs_of[k - 1].at[TAIL:], right.at[1, chunk(2 * (z ^ k) + core, rows)])
        for refs_of, core in ((margin_near, e), (margin_far, 1 - e)):
            bring(refs_of[k - 1], right.at[0, chunk(2 * (z ^ k) + core, rows)])
    start_all(copies)
    mask = block_mask(tail_of(copies[0], tail), 2, rows, columns)
    wait_all(copies[1:])
    plus = dot(left[0], right[0])
    minus = dot(left[1], right[1])
    generator = ((plus - minus) * mask).astype(BF16)
    out[...] = (generator.astype(F32) * 0.25).astype(BF16)


def series_kernel(layout, count, *refs):
    pieces = refs[: len(layout)]
    tails = refs[len(layout) : len(layout) + 2 * count]
    order = refs[len(layout) + 2 * count]
    panel, mine, whole, turned, wides, spread, sems = refs[len(layout) + 2 * count + 1 :]
    z, q, e = place()
    rows, columns = mine.shape
    size = panel.shape[1]
    row_blocks, column_blocks, blocks = rows // BLK, columns // BLK, size // BLK
    copies, early = [], []
    for ref, (slots, plane, lane) in zip(pieces, layout):
        core = e if lane == 0 else 1 - e
        for index, k in enumerate(slots):
            copies.append(
                pltpu.make_async_copy(
                    ref.at[index],
                    whole.at[chunk(2 * (z ^ k) + core, rows), chunk(q ^ plane, columns)],
                    sems.at[len(copies)],
                )
            )
    for index, ref in enumerate(tails):
        core = e if index < count else 1 - e
        early.append(
            pltpu.make_async_copy(
                ref.at[:TAIL],
                wides.at[2 * (z ^ (index % count)) + core],
                sems.at[len(copies) + len(early)],
            )
        )
    start_all(early)
    start_all(copies)
    wait_all(early)
    filters = jnp.zeros((128, size), F32)
    for p in range(2 * count):
        column = iota((TAIL, size), 1) // BLK
        row = iota((TAIL, size), 0)
        near = ((row < row_blocks) & (column == row + p * row_blocks)).astype(BF16)
        filters += lax.dot_general(
            wides[p][:, :128], near, (((0,), (0,)), ((), ())), preferred_element_type=F32
        )
    spread[...] = filters

    wait_all(copies)
    small = size <= 1536

    def turn(t):
        tile = jnp.concatenate(
            [whole[chunk(order[t * column_blocks + a], BLK), :] for a in range(column_blocks)],
            axis=0,
        )
        turned[:, chunk(t, columns)] = tile.T

    def place_rows(b):
        whole[chunk(b, BLK), :] = turned[chunk(order[b], BLK), :]

    repeat(count, turn, small)
    repeat(blocks, place_rows, small)

    first = (2 * q + e) * rows
    unit = (iota((rows, size), 1) == iota((rows, size), 0) + first).astype(F32)
    own = unit + whole[chunk(2 * q + e, rows), :].astype(F32) / TERMS
    panel[...] = own.astype(BF16)
    width = size if small else 512
    for number in range(1, TERMS):
        current = panel[...]
        base = (FIRST + number - 1) * column_blocks + e * row_blocks

        def advance(t):
            part = chunk(t, width)
            product = dot(current, whole[:, part])
            mask = jnp.concatenate(
                [
                    jnp.broadcast_to(spread[pl.ds(base + b, 1), part], (BLK, width))
                    for b in range(row_blocks)
                ],
                axis=0,
            )
            here = iota((rows, width), 1) + t * width == iota((rows, width), 0) + first
            panel[:, part] = (here.astype(F32) + product * mask / (TERMS - number)).astype(BF16)

        repeat(size // width, advance, small)
    mine[...] = panel[:, chunk(z, columns)]


def turned_mask(tails, number, e, rows, columns):
    row_blocks, column_blocks = rows // BLK, columns // BLK
    pick = iota((rows, 128), 0) // BLK + number * column_blocks + e * row_blocks
    pick = (pick == iota((rows, 128), 1)).astype(BF16)
    mask = jnp.zeros((rows, columns), F32)
    for core in range(2):
        row = iota((TAIL, columns), 0)
        near = (row < row_blocks) & (iota((TAIL, columns), 1) // BLK == row + core * row_blocks)
        chosen = lax.dot_general(
            pick, tails[core][:, :128], (((1,), (1,)), ((), ())), preferred_element_type=F32
        )
        mask += dot(chosen.astype(BF16), near.astype(BF16))
    return mask


def square_kernel(count, *refs):
    near, far = refs[:count], refs[count : 2 * count]
    panel, pair, other, out, right, tails, sems = refs[2 * count :]
    z, q, e = place()
    rows, columns = out.shape
    copies = [
        pltpu.make_async_copy(pair.at[:TAIL], tails.at[e], sems.at[0]),
        pltpu.make_async_copy(other.at[:TAIL], tails.at[1 - e], sems.at[1]),
    ]
    for s in range(count):
        for ref, core in ((near[s], e), (far[s], 1 - e)):
            copies.append(
                pltpu.make_async_copy(
                    ref, right.at[chunk(2 * (q ^ s) + core, rows)], sems.at[len(copies)]
                )
            )
    start_all(copies)
    wait_all(copies[:2])
    mask = turned_mask(tails, FIRST + TERMS - 1, e, rows, columns)
    wait_all(copies[2:])
    out[...] = (dot(panel[...], right[...]) * mask).astype(BF16)


def evolve_kernel(count, *refs):
    groups = [refs[n * count : (n + 1) * count] for n in range(4)]
    line_near, line_far, plane_near, plane_far = groups
    pair, other, out, left, right, tails, sems = refs[4 * count :]
    z, q, e = place()
    rows, columns = out.shape
    copies = [
        pltpu.make_async_copy(pair.at[:TAIL], tails.at[e], sems.at[0]),
        pltpu.make_async_copy(other.at[:TAIL], tails.at[1 - e], sems.at[1]),
    ]
    for s in range(count):
        for ref, core in ((line_near[s], e), (line_far[s], 1 - e)):
            copies.append(
                pltpu.make_async_copy(
                    ref, left.at[chunk(core, rows), chunk(z ^ s, columns)], sems.at[len(copies)]
                )
            )
        for ref, core in ((plane_near[s], e), (plane_far[s], 1 - e)):
            copies.append(
                pltpu.make_async_copy(
                    ref, right.at[chunk(2 * (q ^ s) + core, rows)], sems.at[len(copies)]
                )
            )
    start_all(copies)
    wait_all(copies[:2])
    mask = block_mask(tails[pl.ds(e, 1)][0], FIRST + TERMS, rows, columns)
    wait_all(copies[2:])
    total = dot(left[...], right[...]).T
    chosen = jnp.where(e == 0, total[:rows], total[rows:])
    out[...] = (chosen * mask).astype(BF16)


def on_device(
    mesh_rows,
    mesh_cols,
    fock_matrix,
    density,
    margin,
    fill_patterns,
    first_filters,
    owner_order,
    second_filters,
):
    moves = Moves(mesh_rows, mesh_cols)
    count = mesh_cols
    slots = range(1, count)
    rows, columns = fock_matrix.shape
    size = rows * mesh_rows
    block = jax.ShapeDtypeStruct((rows, columns), BF16)

    masked_density, pair = call(
        mask_kernel,
        [block, jax.ShapeDtypeStruct((TAIL + 2 * rows, columns), BF16)],
        [INVMEM] * 6,
        [],
        "mask",
    )(fock_matrix, density, margin, fill_patterns, first_filters, second_filters)

    def plane_parts(value, first):
        parts = [value, value]
        starts = [(first, first + rows)]
        planes = {}
        for s in slots:
            if count == 4 and s == 3:
                top, bottom = planes[2][:rows], planes[1][rows:]
                parts += [moves.in_plane(top, 1), moves.in_plane(bottom, 2)]
                starts.append((0, 0))
            else:
                planes[s] = moves.in_plane(value[first : first + 2 * rows], s)
                parts += [planes[s], planes[s]]
                starts.append((0, rows))
        return parts, starts

    density_near = [moves.relabel(masked_density, k) for k in range(count)]
    pair = moves.relabel(pair)
    soon, *density_near = lax.optimization_barrier((pair, *density_near))
    parts, starts = plane_parts(soon, TAIL)
    fock_near = [moves.along_z(pair[: TAIL + rows], k) for k in slots]
    lone, *density_near = lax.optimization_barrier((pair[TAIL + rows :], *density_near))
    margin_near = [moves.along_z(lone, k) for k in slots]
    density_far = [moves.core(value) for value in density_near]
    pair_far = moves.core(pair)
    parts, fock_near, pair_far = lax.optimization_barrier((parts, fock_near, pair_far))

    products = call(
        functools.partial(first_kernel, count, starts),
        jax.ShapeDtypeStruct((2 * rows, columns), BF16),
        [ANY] * (1 + 4 * count),
        [
            pltpu.VMEM((2 * rows, size), BF16),
            pltpu.VMEM((size, columns), BF16),
            pltpu.VMEM((TAIL, columns), BF16),
            pltpu.SemaphoreType.DMA((1 + 4 * count,)),
        ],
        "first",
    )(pair, *parts, *density_near, *density_far)
    parts, starts = plane_parts(products, 0)
    parts, margin_near = lax.optimization_barrier((parts, margin_near))
    fock_far = [moves.core(value) for value in fock_near]
    margin_far = [moves.core(value) for value in margin_near]

    generator = call(
        functools.partial(generator_kernel, count, starts),
        block,
        [ANY] * (2 * count + 2 + 4 * (count - 1)),
        [
            pltpu.VMEM((2, rows, size), BF16),
            pltpu.VMEM((2, size, columns), BF16),
            pltpu.VMEM((TAIL, columns), BF16),
            pltpu.SemaphoreType.DMA((1 + 6 * count,)),
        ],
        "generator",
    )(*parts, pair, pair_far, *fock_near, *fock_far, *margin_near, *margin_far)
    tails = [pair, *fock_near, pair_far, *fock_far]

    first = jnp.stack([generator, moves.along_z(generator, 1)])
    held, groups = (0, 1), [((0, 1), first)]
    for k in range(2, count, 2):
        groups.append(((k, k ^ 1), moves.along_z(first, k)))
    layout, pieces = [], []

    def keep(held, s, value):
        layout.extend([(held, s, 0), (held, s, 1)])
        pieces.extend([value, moves.core(value)])

    corners = []
    for held, group in groups:
        group, *corners = lax.optimization_barrier((group, *corners))
        for s, value in enumerate(corners):
            keep(before[s : s + 1], 3, value)
        before = held
        keep(held, 0, group)
        planes = {s: moves.in_plane(group, s) for s in slots if not (count == 4 and s == 3)}
        for s, value in planes.items():
            keep(held, s, value)
        if count == 4:
            corners = [moves.in_plane(planes[2][:1], 1), moves.in_plane(planes[1][1:], 2)]
    for s, value in enumerate(corners):
        keep(before[s : s + 1], 3, value)

    panel, mine = call(
        functools.partial(series_kernel, layout, count),
        [jax.ShapeDtypeStruct((rows, size), BF16), block],
        [ANY] * (len(layout) + 2 * count) + [INSMEM],
        [
            pltpu.VMEM((size, size), BF16),
            pltpu.VMEM((size, size), BF16),
            pltpu.VMEM((mesh_rows, TAIL, columns), BF16),
            pltpu.VMEM((128, size), F32),
            pltpu.SemaphoreType.DMA((mesh_rows * mesh_cols + 2 * count,)),
        ],
        "series",
    )(*pieces, *tails, owner_order)

    near = [mine] + [moves.in_plane(mine, s) for s in slots]
    far = [moves.core(value) for value in near]
    square = call(
        functools.partial(square_kernel, count),
        block,
        [ANY] * (2 * count) + [INVMEM, ANY, ANY],
        [
            pltpu.VMEM((size, columns), BF16),
            pltpu.VMEM((2, TAIL, columns), BF16),
            pltpu.SemaphoreType.DMA((2 + 2 * count,)),
        ],
        "square",
    )(*near, *far, panel, pair, pair_far)

    line_near = [square] + [moves.along_z(square, k) for k in slots]
    line_far = [moves.core(value) for value in line_near]
    plane_near = [square] + [moves.in_plane(square, s) for s in slots]
    plane_far = [line_far[0]] + [moves.core(value) for value in plane_near[1:]]
    evolved = call(
        functools.partial(evolve_kernel, count),
        block,
        [ANY] * (4 * count + 2),
        [
            pltpu.VMEM((columns, size), BF16),
            pltpu.VMEM((size, columns), BF16),
            pltpu.VMEM((2, TAIL, columns), BF16),
            pltpu.SemaphoreType.DMA((2 + 4 * count,)),
        ],
        "evolve",
    )(*line_near, *line_far, *plane_near, *plane_far, pair, pair_far)
    return moves.relabel(evolved)


def solution(mesh):
    return jax.shard_map(
        functools.partial(on_device, mesh.shape["row"], mesh.shape["col"]),
        mesh=mesh,
        in_specs=(
            P("row", "col"),
            P("row", "col"),
            P("row", "col"),
            P(None, "row", "col"),
            P(None, "row", "col"),
            P(),
            P(None, "row", "col"),
        ),
        out_specs=P("row", "col"),
        check_vma=False,
    )
```

```python
import functools

import jax
import jax.numpy as jnp
from jax import lax
from jax.experimental import pallas as pl
from jax.experimental.pallas import tpu as pltpu
from jax.sharding import PartitionSpec as P

BLK = 32
TERMS = 6
SQUARINGS = 2
FIRST = 3
AXES = ("row", "col")
F32 = jnp.float32
BF16 = jnp.bfloat16
TAIL = 16
VMEM_LIMIT = 60 * 1024 * 1024


def coordinates(r, c):
    return r // 2, r % 2, c // 2, c % 2


def permutation(rows, cols, source):
    pairs = []
    for r in range(rows):
        for c in range(cols):
            sr, sc = source(*coordinates(r, c))
            pairs.append((sr * cols + sc, r * cols + c))
    return pairs


class Moves:
    def __init__(self, rows, cols):
        self.rows, self.cols = rows, cols

    def move(self, value, source):
        return lax.ppermute(value, AXES, permutation(self.rows, self.cols, source))

    def relabel(self, value, k=0):
        return self.move(value, lambda z, y, x, e: (2 * (z ^ k) + e, 2 * x + y))

    def along_z(self, value, k):
        return self.move(value, lambda z, y, x, e: (2 * (z ^ k) + y, 2 * x + e))

    def line(self, value, relabel=False):
        bits = [1 << b for b in range((self.rows // 2).bit_length() - 1)]
        held = {0: value}
        for bit in reversed(bits):
            for k, part in list(held.items()):
                if k == 0 and relabel:
                    held[bit] = self.relabel(value, bit)
                else:
                    held[k | bit] = self.along_z(part, bit)
        return [held[k] for k in range(1, self.rows // 2)]

    def in_plane(self, value, s):
        return self.move(value, lambda z, y, x, e: (2 * z + (y ^ (s & 1)), 2 * (x ^ (s >> 1)) + e))

    def core(self, value):
        return self.move(value, lambda z, y, x, e: (2 * z + y, 2 * x + 1 - e))


def place():
    r, c = lax.axis_index("row"), lax.axis_index("col")
    z, y, x, e = r // 2, r % 2, c // 2, c % 2
    return z, 2 * x + y, e


def iota(shape, axis):
    return lax.broadcasted_iota(jnp.int32, shape, axis)


def dot(a, b):
    return jnp.dot(a, b, preferred_element_type=F32)


def repeat_rows(rows, blocks):
    return (iota((rows, blocks), 0) // BLK == iota((rows, blocks), 1)).astype(BF16)


def repeat_columns(blocks, columns, first=0):
    return (iota((blocks, columns), 0) == iota((blocks, columns), 1) // BLK + first).astype(BF16)


def block_mask(tail, number, rows, columns):
    blocks = columns // BLK
    wide = dot(repeat_rows(rows, tail.shape[0]), tail).astype(BF16)
    return dot(wide, repeat_columns(tail.shape[1], columns, number * blocks))


def call(kernel, outs, ins, scratch, name, flops=1000):
    return pl.pallas_call(
        kernel,
        out_shape=outs,
        in_specs=ins,
        out_specs=jax.tree.map(lambda _: pl.BlockSpec(memory_space=pltpu.VMEM), outs),
        scratch_shapes=scratch,
        name=name,
        compiler_params=pltpu.CompilerParams(vmem_limit_bytes=VMEM_LIMIT),
        cost_estimate=pl.CostEstimate(flops=flops, bytes_accessed=1000, transcendentals=0),
    )


ANY = pl.BlockSpec(memory_space=pl.ANY)
INVMEM = pl.BlockSpec(memory_space=pltpu.VMEM)
INSMEM = pl.BlockSpec(memory_space=pltpu.SMEM)


def mask_kernel(fock, density, margin, fills, firsts, seconds, masked_density, pair):
    rows, columns = fock.shape
    row_blocks, column_blocks = rows // BLK, columns // BLK
    tall = repeat_rows(rows, row_blocks)
    wide = repeat_columns(column_blocks, columns)

    def masked(ref, number):
        mask = dot(dot(tall, fills[number].astype(BF16)).astype(BF16), wide)
        return (ref[...].astype(F32) * mask).astype(BF16)

    masked_density[...] = masked(density, 1)
    pair[TAIL : TAIL + rows, :] = masked(fock, 0)
    pair[TAIL + rows :, :] = masked(margin, 2)
    top = (iota((TAIL, row_blocks), 0) == iota((TAIL, row_blocks), 1)).astype(BF16)
    tail = jnp.zeros((TAIL, columns), F32)
    for number in range(firsts.shape[0] + seconds.shape[0]):
        ref = firsts[number] if number < FIRST else seconds[number - FIRST]
        column = iota((column_blocks, columns), 1) - number * column_blocks
        spread = (iota((column_blocks, columns), 0) == column).astype(BF16)
        tail += dot(dot(top, ref.astype(BF16)).astype(BF16), spread)
    pair[:TAIL, :] = tail.astype(BF16)


def chunk(index, length):
    return pl.ds(pl.multiple_of(index * length, length), length)


def start_all(copies):
    for one in copies:
        one.start()


def wait_all(copies):
    for one in copies:
        one.wait()


def repeat(times, body, unrolled):
    if unrolled:
        for t in range(times):
            body(t)
    else:

        def step(t, carry):
            body(t)
            return carry

        lax.fori_loop(0, times, step, 0)


def tail_of(copy, tail):
    copy.wait()
    return tail[...]


def first_kernel(count, starts, *refs):
    pair, parts = refs[0], refs[1 : 1 + 2 * count]
    near, far = refs[1 + 2 * count : 1 + 3 * count], refs[1 + 3 * count : 1 + 4 * count]
    out, left, right, tail, sems = refs[1 + 4 * count :]
    z, q, e = place()
    rows, columns = near[0].shape
    copies = [pltpu.make_async_copy(pair.at[:TAIL], tail, sems.at[0])]

    def bring(source, target):
        copies.append(pltpu.make_async_copy(source, target, sems.at[len(copies)]))

    for s in range(count):
        for half in range(2):
            bring(
                parts[2 * s + half].at[pl.ds(starts[s][half], rows)],
                left.at[pl.ds(half * rows, rows), chunk(q ^ s, columns)],
            )
        bring(near[s], right.at[chunk(2 * (z ^ s) + e, rows)])
        bring(far[s], right.at[chunk(2 * (z ^ s) + 1 - e, rows)])
    start_all(copies)
    filters = tail_of(copies[0], tail)
    masks = [block_mask(filters, n, rows, columns) for n in range(2)]
    wait_all(copies[1:])
    total = dot(left[...], right[...])
    for n in range(2):
        part = slice(n * rows, (n + 1) * rows)
        out[part, :] = (total[part] * masks[n]).astype(BF16)


def generator_kernel(count, starts, *refs):
    parts, own, other = refs[: 2 * count], refs[2 * count], refs[2 * count + 1]
    rest = refs[2 * count + 2 :]
    fock_near, fock_far, margin_near, margin_far = [
        rest[n * (count - 1) : (n + 1) * (count - 1)] for n in range(4)
    ]
    out, left, right, tail, sems = rest[4 * (count - 1) :]
    z, q, e = place()
    rows, columns = out.shape
    copies = [pltpu.make_async_copy(own.at[:TAIL], tail, sems.at[0])]

    def bring(source, target):
        copies.append(pltpu.make_async_copy(source, target, sems.at[len(copies)]))

    for half in range(2):
        for s in range(count):
            bring(
                parts[2 * s + half].at[pl.ds(starts[s][half], rows)],
                left.at[half, :, chunk(q ^ s, columns)],
            )
        part = pl.ds(TAIL + half * rows, rows)
        bring(own.at[part], right.at[1 - half, chunk(2 * z + e, rows)])
        bring(other.at[part], right.at[1 - half, chunk(2 * z + 1 - e, rows)])
    for k in range(1, count):
        for refs_of, core in ((fock_near, e), (fock_far, 1 - e)):
            bring(refs_of[k - 1].at[TAIL:], right.at[1, chunk(2 * (z ^ k) + core, rows)])
        for refs_of, core in ((margin_near, e), (margin_far, 1 - e)):
            bring(refs_of[k - 1], right.at[0, chunk(2 * (z ^ k) + core, rows)])
    start_all(copies)
    mask = block_mask(tail_of(copies[0], tail), 2, rows, columns)
    wait_all(copies[1:])
    plus = dot(left[0], right[0])
    minus = dot(left[1], right[1])
    generator = ((plus - minus) * mask).astype(BF16)
    out[...] = (generator.astype(F32) * 0.25).astype(BF16)


def series_kernel(layout, count, *refs):
    pieces = refs[: len(layout)]
    tails = refs[len(layout) : len(layout) + 2 * count]
    order = refs[len(layout) + 2 * count]
    panel, mine, whole, turned, wides, spread, sems = refs[len(layout) + 2 * count + 1 :]
    z, q, e = place()
    rows, columns = mine.shape
    size = panel.shape[1]
    row_blocks, column_blocks, blocks = rows // BLK, columns // BLK, size // BLK
    copies, early = [], []
    for ref, (slots, plane, lane) in zip(pieces, layout):
        core = e if lane == 0 else 1 - e
        for index, k in enumerate(slots):
            copies.append(
                pltpu.make_async_copy(
                    ref.at[index],
                    whole.at[chunk(2 * (z ^ k) + core, rows), chunk(q ^ plane, columns)],
                    sems.at[len(copies)],
                )
            )
    for index, ref in enumerate(tails):
        core = e if index < count else 1 - e
        early.append(
            pltpu.make_async_copy(
                ref.at[:TAIL],
                wides.at[2 * (z ^ (index % count)) + core],
                sems.at[len(copies) + len(early)],
            )
        )
    start_all(early)
    start_all(copies)
    wait_all(early)
    filters = jnp.zeros((128, size), F32)
    for p in range(2 * count):
        column = iota((TAIL, size), 1) // BLK
        row = iota((TAIL, size), 0)
        near = ((row < row_blocks) & (column == row + p * row_blocks)).astype(BF16)
        filters += lax.dot_general(
            wides[p][:, :128], near, (((0,), (0,)), ((), ())), preferred_element_type=F32
        )
    spread[...] = filters

    wait_all(copies)
    small = size <= 1536

    def turn(t):
        tile = jnp.concatenate(
            [whole[chunk(order[t * column_blocks + a], BLK), :] for a in range(column_blocks)],
            axis=0,
        )
        turned[:, chunk(t, columns)] = tile.T

    def place_rows(b):
        whole[chunk(b, BLK), :] = turned[chunk(order[b], BLK), :]

    repeat(count, turn, small)
    repeat(blocks, place_rows, small)

    first = (2 * q + e) * rows
    unit = (iota((rows, size), 1) == iota((rows, size), 0) + first).astype(F32)
    own = unit + whole[chunk(2 * q + e, rows), :].astype(F32) / TERMS
    panel[...] = own.astype(BF16)
    width = size if small else 512
    for number in range(1, TERMS):
        current = panel[...]
        base = (FIRST + number - 1) * column_blocks + e * row_blocks

        def advance(t):
            part = chunk(t, width)
            product = dot(current, whole[:, part])
            mask = jnp.concatenate(
                [
                    jnp.broadcast_to(spread[pl.ds(base + b, 1), part], (BLK, width))
                    for b in range(row_blocks)
                ],
                axis=0,
            )
            here = iota((rows, width), 1) + t * width == iota((rows, width), 0) + first
            panel[:, part] = (here.astype(F32) + product * mask / (TERMS - number)).astype(BF16)

        repeat(size // width, advance, small)
    mine[...] = panel[:, chunk(z, columns)]


def turned_mask(tails, number, e, rows, columns):
    row_blocks, column_blocks = rows // BLK, columns // BLK
    pick = iota((rows, 128), 0) // BLK + number * column_blocks + e * row_blocks
    pick = (pick == iota((rows, 128), 1)).astype(BF16)
    mask = jnp.zeros((rows, columns), F32)
    for core in range(2):
        row = iota((TAIL, columns), 0)
        near = (row < row_blocks) & (iota((TAIL, columns), 1) // BLK == row + core * row_blocks)
        chosen = lax.dot_general(
            pick, tails[core][:, :128], (((1,), (1,)), ((), ())), preferred_element_type=F32
        )
        mask += dot(chosen.astype(BF16), near.astype(BF16))
    return mask


def square_kernel(count, *refs):
    near, far = refs[:count], refs[count : 2 * count]
    panel, pair, other, out, right, tails, sems = refs[2 * count :]
    z, q, e = place()
    rows, columns = out.shape
    copies = [
        pltpu.make_async_copy(pair.at[:TAIL], tails.at[e], sems.at[0]),
        pltpu.make_async_copy(other.at[:TAIL], tails.at[1 - e], sems.at[1]),
    ]
    for s in range(count):
        for ref, core in ((near[s], e), (far[s], 1 - e)):
            copies.append(
                pltpu.make_async_copy(
                    ref, right.at[chunk(2 * (q ^ s) + core, rows)], sems.at[len(copies)]
                )
            )
    start_all(copies)
    wait_all(copies[:2])
    mask = turned_mask(tails, FIRST + TERMS - 1, e, rows, columns)
    wait_all(copies[2:])
    out[...] = (dot(panel[...], right[...]) * mask).astype(BF16)


def evolve_kernel(count, *refs):
    groups = [refs[n * count : (n + 1) * count] for n in range(4)]
    line_near, line_far, plane_near, plane_far = groups
    pair, other, out, left, right, tails, sems = refs[4 * count :]
    z, q, e = place()
    rows, columns = out.shape
    copies = [
        pltpu.make_async_copy(pair.at[:TAIL], tails.at[e], sems.at[0]),
        pltpu.make_async_copy(other.at[:TAIL], tails.at[1 - e], sems.at[1]),
    ]
    for s in range(count):
        for ref, core in ((line_near[s], e), (line_far[s], 1 - e)):
            copies.append(
                pltpu.make_async_copy(
                    ref, left.at[chunk(core, rows), chunk(z ^ s, columns)], sems.at[len(copies)]
                )
            )
        for ref, core in ((plane_near[s], e), (plane_far[s], 1 - e)):
            copies.append(
                pltpu.make_async_copy(
                    ref, right.at[chunk(2 * (q ^ s) + core, rows)], sems.at[len(copies)]
                )
            )
    start_all(copies)
    wait_all(copies[:2])
    mask = block_mask(tails[pl.ds(e, 1)][0], FIRST + TERMS, rows, columns)
    wait_all(copies[2:])
    total = dot(left[...], right[...]).T
    chosen = jnp.where(e == 0, total[:rows], total[rows:])
    out[...] = (chosen * mask).astype(BF16)


def on_device(
    mesh_rows,
    mesh_cols,
    fock_matrix,
    density,
    margin,
    fill_patterns,
    first_filters,
    owner_order,
    second_filters,
):
    moves = Moves(mesh_rows, mesh_cols)
    count = mesh_cols
    slots = range(1, count)
    half = count // 2
    rows, columns = fock_matrix.shape
    size = rows * mesh_rows
    block = jax.ShapeDtypeStruct((rows, columns), BF16)

    masked_density, pair = call(
        mask_kernel,
        [block, jax.ShapeDtypeStruct((TAIL + 2 * rows, columns), BF16)],
        [INVMEM] * 6,
        [],
        "mask",
    )(fock_matrix, density, margin, fill_patterns, first_filters, second_filters)

    def plane_parts(value, first):
        parts = [value, value]
        starts = [(first, first + rows)]
        planes = {}
        for s in slots:
            if count == 4 and s == 3:
                top, bottom = planes[2][:rows], planes[1][rows:]
                parts += [moves.in_plane(top, 1), moves.in_plane(bottom, 2)]
                starts.append((0, 0))
            else:
                planes[s] = moves.in_plane(value[first : first + 2 * rows], s)
                parts += [planes[s], planes[s]]
                starts.append((0, rows))
        return parts, starts

    density_near = [moves.relabel(masked_density)] + moves.line(masked_density, True)
    pair = moves.relabel(pair)
    soon, density_near[half] = lax.optimization_barrier((pair, density_near[half]))
    parts, starts = plane_parts(soon, TAIL)
    fock_near = moves.line(pair[: TAIL + rows])
    lone, *density_near = lax.optimization_barrier((pair[TAIL + rows :], *density_near))
    margin_near = moves.line(lone)
    density_far = [moves.core(value) for value in density_near]
    pair_far = moves.core(pair)
    parts, fock_near, pair_far, margin_near[half - 1] = lax.optimization_barrier(
        (parts, fock_near, pair_far, margin_near[half - 1])
    )

    products = call(
        functools.partial(first_kernel, count, starts),
        jax.ShapeDtypeStruct((2 * rows, columns), BF16),
        [ANY] * (1 + 4 * count),
        [
            pltpu.VMEM((2 * rows, size), BF16),
            pltpu.VMEM((size, columns), BF16),
            pltpu.VMEM((TAIL, columns), BF16),
            pltpu.SemaphoreType.DMA((1 + 4 * count,)),
        ],
        "first",
        10**10,
    )(pair, *parts, *density_near, *density_far)
    parts, starts = plane_parts(products, 0)
    parts, margin_near = lax.optimization_barrier((parts, margin_near))
    fock_far = [moves.core(value) for value in fock_near]
    margin_far = [moves.core(value) for value in margin_near]

    generator = call(
        functools.partial(generator_kernel, count, starts),
        block,
        [ANY] * (2 * count + 2 + 4 * (count - 1)),
        [
            pltpu.VMEM((2, rows, size), BF16),
            pltpu.VMEM((2, size, columns), BF16),
            pltpu.VMEM((TAIL, columns), BF16),
            pltpu.SemaphoreType.DMA((1 + 6 * count,)),
        ],
        "generator",
    )(*parts, pair, pair_far, *fock_near, *fock_far, *margin_near, *margin_far)
    tails = [pair, *fock_near, pair_far, *fock_far]

    lines = [generator] + moves.line(generator)
    lines[1 : half + 1] = lax.optimization_barrier(lines[1 : half + 1])
    groups = []
    for first in (0, half):
        held = tuple(range(first, first + half))
        groups.append((held, jnp.stack([lines[k] for k in held])))
    layout, pieces = [], []

    def keep(held, s, value):
        layout.extend([(held, s, 0), (held, s, 1)])
        pieces.extend([value, moves.core(value)])

    corners = []
    for held, group in groups:
        group, *corners = lax.optimization_barrier((group, *corners))
        for s, value in enumerate(corners):
            keep(before[s : s + 1], 3, value)
        before = held
        keep(held, 0, group)
        planes = {s: moves.in_plane(group, s) for s in slots if not (count == 4 and s == 3)}
        for s, value in planes.items():
            keep(held, s, value)
        if count == 4:
            corners = [moves.in_plane(planes[2][:1], 1), moves.in_plane(planes[1][1:], 2)]
    for s, value in enumerate(corners):
        keep(before[s : s + 1], 3, value)

    panel, mine = call(
        functools.partial(series_kernel, layout, count),
        [jax.ShapeDtypeStruct((rows, size), BF16), block],
        [ANY] * (len(layout) + 2 * count) + [INSMEM],
        [
            pltpu.VMEM((size, size), BF16),
            pltpu.VMEM((size, size), BF16),
            pltpu.VMEM((mesh_rows, TAIL, columns), BF16),
            pltpu.VMEM((128, size), F32),
            pltpu.SemaphoreType.DMA((mesh_rows * mesh_cols + 2 * count,)),
        ],
        "series",
    )(*pieces, *tails, owner_order)

    near = [mine] + [moves.in_plane(mine, s) for s in slots]
    far = [moves.core(value) for value in near]
    square = call(
        functools.partial(square_kernel, count),
        block,
        [ANY] * (2 * count) + [INVMEM, ANY, ANY],
        [
            pltpu.VMEM((size, columns), BF16),
            pltpu.VMEM((2, TAIL, columns), BF16),
            pltpu.SemaphoreType.DMA((2 + 2 * count,)),
        ],
        "square",
    )(*near, *far, panel, pair, pair_far)

    line_near = [square] + moves.line(square)
    line_far = [moves.core(value) for value in line_near]
    plane_near = [square] + [moves.in_plane(square, s) for s in slots]
    plane_far = [line_far[0]] + [moves.core(value) for value in plane_near[1:]]
    evolved = call(
        functools.partial(evolve_kernel, count),
        block,
        [ANY] * (4 * count + 2),
        [
            pltpu.VMEM((columns, size), BF16),
            pltpu.VMEM((size, columns), BF16),
            pltpu.VMEM((2, TAIL, columns), BF16),
            pltpu.SemaphoreType.DMA((2 + 4 * count,)),
        ],
        "evolve",
    )(*line_near, *line_far, *plane_near, *plane_far, pair, pair_far)
    return moves.relabel(evolved)


def solution(mesh):
    return jax.shard_map(
        functools.partial(on_device, mesh.shape["row"], mesh.shape["col"]),
        mesh=mesh,
        in_specs=(
            P("row", "col"),
            P("row", "col"),
            P("row", "col"),
            P(None, "row", "col"),
            P(None, "row", "col"),
            P(),
            P(None, "row", "col"),
        ),
        out_specs=P("row", "col"),
        check_vma=False,
    )
```

```python
import functools

import jax
import jax.numpy as jnp
from jax import lax
from jax.experimental import pallas as pl
from jax.experimental.pallas import tpu as pltpu
from jax.sharding import PartitionSpec as P

BLK = 32
TERMS = 6
SQUARINGS = 2
FIRST = 3
AXES = ("row", "col")
F32 = jnp.float32
BF16 = jnp.bfloat16
TAIL = 16
MEGABYTE = 1024 * 1024


def coordinates(r, c):
    return r // 2, r % 2, c // 2, c % 2


def permutation(rows, cols, source):
    pairs = []
    for r in range(rows):
        for c in range(cols):
            sr, sc = source(*coordinates(r, c))
            pairs.append((sr * cols + sc, r * cols + c))
    return pairs


class Moves:
    def __init__(self, rows, cols):
        self.rows, self.cols = rows, cols

    def move(self, value, source):
        return lax.ppermute(value, AXES, permutation(self.rows, self.cols, source))

    def relabel(self, value, k=0):
        return self.move(value, lambda z, y, x, e: (2 * (z ^ k) + e, 2 * x + y))

    def along_z(self, value, k):
        return self.move(value, lambda z, y, x, e: (2 * (z ^ k) + y, 2 * x + e))

    def line(self, value, relabel=False):
        bits = [1 << b for b in range((self.rows // 2).bit_length() - 1)]
        held = {0: value}
        for bit in reversed(bits):
            for k, part in list(held.items()):
                if k == 0 and relabel:
                    held[bit] = self.relabel(value, bit)
                else:
                    held[k | bit] = self.along_z(part, bit)
        return [held[k] for k in range(1, self.rows // 2)]

    def in_plane(self, value, s):
        return self.move(value, lambda z, y, x, e: (2 * z + (y ^ (s & 1)), 2 * (x ^ (s >> 1)) + e))

    def core(self, value):
        return self.move(value, lambda z, y, x, e: (2 * z + y, 2 * x + 1 - e))


def place():
    r, c = lax.axis_index("row"), lax.axis_index("col")
    z, y, x, e = r // 2, r % 2, c // 2, c % 2
    return z, 2 * x + y, e


def iota(shape, axis):
    return lax.broadcasted_iota(jnp.int32, shape, axis)


def dot(a, b):
    return jnp.dot(a, b, preferred_element_type=F32)


def repeat_rows(rows, blocks):
    return (iota((rows, blocks), 0) // BLK == iota((rows, blocks), 1)).astype(BF16)


def repeat_columns(blocks, columns, first=0):
    return (iota((blocks, columns), 0) == iota((blocks, columns), 1) // BLK + first).astype(BF16)


def block_mask(tail, number, rows, columns):
    blocks = columns // BLK
    wide = dot(repeat_rows(rows, tail.shape[0]), tail).astype(BF16)
    return dot(wide, repeat_columns(tail.shape[1], columns, number * blocks))


def call(kernel, outs, ins, scratch, name, flops=1000, room=16):
    return pl.pallas_call(
        kernel,
        out_shape=outs,
        in_specs=ins,
        out_specs=jax.tree.map(lambda _: pl.BlockSpec(memory_space=pltpu.VMEM), outs),
        scratch_shapes=scratch,
        name=name,
        compiler_params=pltpu.CompilerParams(vmem_limit_bytes=room * MEGABYTE),
        cost_estimate=pl.CostEstimate(flops=flops, bytes_accessed=1000, transcendentals=0),
    )


ANY = pl.BlockSpec(memory_space=pl.ANY)
INVMEM = pl.BlockSpec(memory_space=pltpu.VMEM)
INSMEM = pl.BlockSpec(memory_space=pltpu.SMEM)


def masked(ref, fill):
    rows, columns = ref.shape
    tall = repeat_rows(rows, fill.shape[0])
    wide = repeat_columns(fill.shape[1], columns)
    mask = dot(dot(tall, fill.astype(BF16)).astype(BF16), wide)
    return (ref[...].astype(F32) * mask).astype(BF16)


def density_kernel(density, fills, out):
    out[...] = masked(density, fills[1])


def pair_kernel(fock, margin, fills, firsts, seconds, pair):
    rows, columns = fock.shape
    row_blocks, column_blocks = rows // BLK, columns // BLK
    pair[TAIL : TAIL + rows, :] = masked(fock, fills[0])
    pair[TAIL + rows :, :] = masked(margin, fills[2])
    top = (iota((TAIL, row_blocks), 0) == iota((TAIL, row_blocks), 1)).astype(BF16)
    tail = jnp.zeros((TAIL, columns), F32)
    for number in range(firsts.shape[0] + seconds.shape[0]):
        ref = firsts[number] if number < FIRST else seconds[number - FIRST]
        column = iota((column_blocks, columns), 1) - number * column_blocks
        spread = (iota((column_blocks, columns), 0) == column).astype(BF16)
        tail += dot(dot(top, ref.astype(BF16)).astype(BF16), spread)
    pair[:TAIL, :] = tail.astype(BF16)


def chunk(index, length):
    return pl.ds(pl.multiple_of(index * length, length), length)


def start_all(copies):
    for one in copies:
        one.start()


def wait_all(copies):
    for one in copies:
        one.wait()


def repeat(times, body, unrolled):
    if unrolled:
        for t in range(times):
            body(t)
    else:

        def step(t, carry):
            body(t)
            return carry

        lax.fori_loop(0, times, step, 0)


def tail_of(copy, tail):
    copy.wait()
    return tail[...]


def first_kernel(count, starts, *refs):
    pair, parts = refs[0], refs[1 : 1 + 2 * count]
    near, far = refs[1 + 2 * count : 1 + 3 * count], refs[1 + 3 * count : 1 + 4 * count]
    out, left, right, tail, sems = refs[1 + 4 * count :]
    z, q, e = place()
    rows, columns = near[0].shape
    copies = [pltpu.make_async_copy(pair.at[:TAIL], tail, sems.at[0])]

    def bring(source, target):
        copies.append(pltpu.make_async_copy(source, target, sems.at[len(copies)]))

    for s in range(count):
        for half in range(2):
            bring(
                parts[2 * s + half].at[pl.ds(starts[s][half], rows)],
                left.at[pl.ds(half * rows, rows), chunk(q ^ s, columns)],
            )
        bring(near[s], right.at[chunk(2 * (z ^ s) + e, rows)])
        bring(far[s], right.at[chunk(2 * (z ^ s) + 1 - e, rows)])
    start_all(copies)
    filters = tail_of(copies[0], tail)
    masks = [block_mask(filters, n, rows, columns) for n in range(2)]
    wait_all(copies[1:])
    total = dot(left[...], right[...])
    for n in range(2):
        part = slice(n * rows, (n + 1) * rows)
        out[part, :] = (total[part] * masks[n]).astype(BF16)


def generator_kernel(count, starts, *refs):
    parts = refs[: 2 * count]
    near, far = refs[2 * count : 3 * count], refs[3 * count : 4 * count]
    out, left, right, tail, sems = refs[4 * count :]
    z, q, e = place()
    rows, columns = out.shape
    copies = [pltpu.make_async_copy(near[0].at[:TAIL], tail, sems.at[0])]

    def bring(source, target):
        copies.append(pltpu.make_async_copy(source, target, sems.at[len(copies)]))

    for half in range(2):
        part = pl.ds(TAIL + half * rows, rows)
        for s in range(count):
            bring(
                parts[2 * s + half].at[pl.ds(starts[s][half], rows)],
                left.at[half, :, chunk(q ^ s, columns)],
            )
            bring(near[s].at[part], right.at[1 - half, chunk(2 * (z ^ s) + e, rows)])
            bring(far[s].at[part], right.at[1 - half, chunk(2 * (z ^ s) + 1 - e, rows)])
    start_all(copies)
    mask = block_mask(tail_of(copies[0], tail), 2, rows, columns)
    wait_all(copies[1:])
    plus = dot(left[0], right[0])
    minus = dot(left[1], right[1])
    generator = ((plus - minus) * mask).astype(BF16)
    out[...] = (generator.astype(F32) * 0.25).astype(BF16)


def series_kernel(layout, count, *refs):
    pieces = refs[: len(layout)]
    tails = refs[len(layout) : len(layout) + 2 * count]
    order = refs[len(layout) + 2 * count]
    panel, mine, whole, turned, wides, spread, sems = refs[len(layout) + 2 * count + 1 :]
    z, q, e = place()
    rows, columns = mine.shape
    size = panel.shape[1]
    row_blocks, column_blocks, blocks = rows // BLK, columns // BLK, size // BLK
    copies, early = [], []
    for ref, (runs, plane, lane) in zip(pieces, layout):
        core = e if lane == 0 else 1 - e
        for row, k, inner, length in runs:
            target = pl.multiple_of((2 * (z ^ k) + core) * rows + inner, BLK)
            copies.append(
                pltpu.make_async_copy(
                    ref.at[pl.ds(row, length)],
                    whole.at[pl.ds(target, length), chunk(q ^ plane, columns)],
                    sems.at[len(copies)],
                )
            )
    for index, ref in enumerate(tails):
        core = e if index < count else 1 - e
        early.append(
            pltpu.make_async_copy(
                ref.at[:TAIL],
                wides.at[2 * (z ^ (index % count)) + core],
                sems.at[len(copies) + len(early)],
            )
        )
    start_all(early)
    start_all(copies)
    wait_all(early)
    filters = jnp.zeros((128, size), F32)
    for p in range(2 * count):
        column = iota((TAIL, size), 1) // BLK
        row = iota((TAIL, size), 0)
        near = ((row < row_blocks) & (column == row + p * row_blocks)).astype(BF16)
        filters += lax.dot_general(
            wides[p][:, :128], near, (((0,), (0,)), ((), ())), preferred_element_type=F32
        )
    spread[...] = filters

    wait_all(copies)
    small = size <= 1536

    def turn(t):
        tile = jnp.concatenate(
            [whole[chunk(order[t * column_blocks + a], BLK), :] for a in range(column_blocks)],
            axis=0,
        )
        turned[:, chunk(t, columns)] = tile.T

    def place_rows(b):
        whole[chunk(b, BLK), :] = turned[chunk(order[b], BLK), :]

    repeat(count, turn, small)
    repeat(blocks, place_rows, small)

    first = (2 * q + e) * rows
    unit = (iota((rows, size), 1) == iota((rows, size), 0) + first).astype(F32)
    own = unit + whole[chunk(2 * q + e, rows), :].astype(F32) / TERMS
    panel[...] = own.astype(BF16)
    width = size if small else 512
    for number in range(1, TERMS):
        current = panel[...]
        base = (FIRST + number - 1) * column_blocks + e * row_blocks

        def advance(t):
            part = chunk(t, width)
            product = dot(current, whole[:, part])
            mask = jnp.concatenate(
                [
                    jnp.broadcast_to(spread[pl.ds(base + b, 1), part], (BLK, width))
                    for b in range(row_blocks)
                ],
                axis=0,
            )
            here = iota((rows, width), 1) + t * width == iota((rows, width), 0) + first
            panel[:, part] = (here.astype(F32) + product * mask / (TERMS - number)).astype(BF16)

        repeat(size // width, advance, small)
    mine[...] = panel[:, chunk(z, columns)]


def turned_mask(tails, number, e, rows, columns):
    row_blocks, column_blocks = rows // BLK, columns // BLK
    pick = iota((rows, 128), 0) // BLK + number * column_blocks + e * row_blocks
    pick = (pick == iota((rows, 128), 1)).astype(BF16)
    mask = jnp.zeros((rows, columns), F32)
    for core in range(2):
        row = iota((TAIL, columns), 0)
        near = (row < row_blocks) & (iota((TAIL, columns), 1) // BLK == row + core * row_blocks)
        chosen = lax.dot_general(
            pick, tails[core][:, :128], (((1,), (1,)), ((), ())), preferred_element_type=F32
        )
        mask += dot(chosen.astype(BF16), near.astype(BF16))
    return mask


def square_kernel(count, *refs):
    near, far = refs[:count], refs[count : 2 * count]
    panel, pair, other, out, left, right, tails, sems = refs[2 * count :]
    z, q, e = place()
    rows, columns = out.shape
    copies = [
        pltpu.make_async_copy(pair.at[:TAIL], tails.at[e], sems.at[0]),
        pltpu.make_async_copy(other.at[:TAIL], tails.at[1 - e], sems.at[1]),
        pltpu.make_async_copy(panel, left, sems.at[2]),
    ]
    for s in range(count):
        for ref, core in ((near[s], e), (far[s], 1 - e)):
            copies.append(
                pltpu.make_async_copy(
                    ref, right.at[chunk(2 * (q ^ s) + core, rows)], sems.at[len(copies)]
                )
            )
    start_all(copies)
    wait_all(copies[:2])
    mask = turned_mask(tails, FIRST + TERMS - 1, e, rows, columns)
    wait_all(copies[2:])
    out[...] = (dot(left[...], right[...]) * mask).astype(BF16)


def evolve_kernel(count, *refs):
    groups = [refs[n * count : (n + 1) * count] for n in range(4)]
    line_near, line_far, plane_near, plane_far = groups
    pair, other, out, left, right, tails, sems = refs[4 * count :]
    z, q, e = place()
    rows, columns = out.shape
    copies = [
        pltpu.make_async_copy(pair.at[:TAIL], tails.at[e], sems.at[0]),
        pltpu.make_async_copy(other.at[:TAIL], tails.at[1 - e], sems.at[1]),
    ]
    for s in range(count):
        for ref, core in ((line_near[s], e), (line_far[s], 1 - e)):
            copies.append(
                pltpu.make_async_copy(
                    ref, left.at[chunk(core, rows), chunk(z ^ s, columns)], sems.at[len(copies)]
                )
            )
        for ref, core in ((plane_near[s], e), (plane_far[s], 1 - e)):
            copies.append(
                pltpu.make_async_copy(
                    ref, right.at[chunk(2 * (q ^ s) + core, rows)], sems.at[len(copies)]
                )
            )
    start_all(copies)
    wait_all(copies[:2])
    mask = block_mask(tails[pl.ds(e, 1)][0], FIRST + TERMS, rows, columns)
    wait_all(copies[2:])
    total = dot(left[...], right[...]).T
    chosen = jnp.where(e == 0, total[:rows], total[rows:])
    out[...] = (chosen * mask).astype(BF16)


def on_device(
    mesh_rows,
    mesh_cols,
    fock_matrix,
    density,
    margin,
    fill_patterns,
    first_filters,
    owner_order,
    second_filters,
):
    moves = Moves(mesh_rows, mesh_cols)
    count = mesh_cols
    slots = range(1, count)
    half = count // 2
    rows, columns = fock_matrix.shape
    size = rows * mesh_rows
    block = jax.ShapeDtypeStruct((rows, columns), BF16)

    masked_density = call(density_kernel, block, [INVMEM] * 2, [], "density")(
        density, fill_patterns
    )
    masked_density, fock_matrix = lax.optimization_barrier((masked_density, fock_matrix))
    pair = call(
        pair_kernel,
        jax.ShapeDtypeStruct((TAIL + 2 * rows, columns), BF16),
        [INVMEM] * 5,
        [],
        "pair",
        10**10,
    )(fock_matrix, margin, fill_patterns, first_filters, second_filters)

    def plane_parts(value, first):
        parts = [value, value]
        starts = [(first, first + rows)]
        planes = {}
        for s in slots:
            if count == 4 and s == 3:
                top, bottom = planes[2][:rows], planes[1][rows:]
                parts += [moves.in_plane(top, 1), moves.in_plane(bottom, 2)]
                starts.append((0, 0))
            else:
                planes[s] = moves.in_plane(value[first : first + 2 * rows], s)
                parts += [planes[s], planes[s]]
                starts.append((0, rows))
        return parts, starts

    density_near = [moves.relabel(masked_density)] + moves.line(masked_density, True)
    pair = moves.relabel(pair)
    soon, density_near[half] = lax.optimization_barrier((pair, density_near[half]))
    parts, starts = plane_parts(soon, TAIL)
    pair_near = moves.line(soon)
    density_far = [moves.core(value) for value in density_near]
    pair_far = [moves.core(pair)]
    parts, pair_far[0], pair_near[:half] = lax.optimization_barrier(
        (parts, pair_far[0], pair_near[:half])
    )

    products = call(
        functools.partial(first_kernel, count, starts),
        jax.ShapeDtypeStruct((2 * rows, columns), BF16),
        [ANY] * (1 + 4 * count),
        [
            pltpu.VMEM((2 * rows, size), BF16),
            pltpu.VMEM((size, columns), BF16),
            pltpu.VMEM((TAIL, columns), BF16),
            pltpu.SemaphoreType.DMA((1 + 4 * count,)),
        ],
        "first",
        10**10,
    )(pair, *parts, *density_near, *density_far)
    parts, starts = plane_parts(products, 0)
    parts, pair_near = lax.optimization_barrier((parts, pair_near))
    pair_near = [pair] + pair_near
    pair_far += [moves.core(value) for value in pair_near[1:]]

    generator = call(
        functools.partial(generator_kernel, count, starts),
        block,
        [ANY] * (4 * count),
        [
            pltpu.VMEM((2, rows, size), BF16),
            pltpu.VMEM((2, size, columns), BF16),
            pltpu.VMEM((TAIL, columns), BF16),
            pltpu.SemaphoreType.DMA((1 + 6 * count,)),
        ],
        "generator",
    )(*parts, *pair_near, *pair_far)

    lines = [generator] + moves.line(generator)
    groups = [((0,), generator), (tuple(slots), jnp.concatenate(lines[1:], axis=0))]
    layout, pieces = [], []

    def keep(held, s, value, first=0):
        runs, row = [], 0
        while row < value.shape[0]:
            index, inner = divmod(first + row, rows)
            length = min(rows - inner, value.shape[0] - row)
            runs.append((row, held[index], inner, length))
            row += length
        layout.extend([(runs, s, 0), (runs, s, 1)])
        pieces.extend([value, moves.core(value)])

    def corner(held, planes):
        cut = planes[1].shape[0] // 2
        keep(held, 3, moves.in_plane(planes[2][:cut], 1))
        keep(held, 3, moves.in_plane(planes[1][cut:], 2), cut)

    planes = {}
    for held, group in groups:
        group, planes = lax.optimization_barrier((group, planes))
        for s, value in planes.items():
            keep(before, s, value)
        if planes and count == 4:
            corner(before, planes)
        before = held
        keep(held, 0, group)
        planes = {s: moves.in_plane(group, s) for s in slots if not (count == 4 and s == 3)}
    for s, value in planes.items():
        keep(before, s, value)
    if count == 4:
        corner(before, planes)
    runs = sum(len(part[0]) for part in layout)

    panel, mine = call(
        functools.partial(series_kernel, layout, count),
        [jax.ShapeDtypeStruct((rows, size), BF16), block],
        [ANY] * (len(layout) + 2 * count) + [INSMEM],
        [
            pltpu.VMEM((size, size), BF16),
            pltpu.VMEM((size, size), BF16),
            pltpu.VMEM((mesh_rows, TAIL, columns), BF16),
            pltpu.VMEM((128, size), F32),
            pltpu.SemaphoreType.DMA((runs + 2 * count,)),
        ],
        "series",
        room=16 + 4 * size * size // MEGABYTE,
    )(*pieces, *pair_near, *pair_far, owner_order)

    near = [mine] + [moves.in_plane(mine, s) for s in slots]
    far = [moves.core(value) for value in near]
    square = call(
        functools.partial(square_kernel, count),
        block,
        [ANY] * (2 * count + 3),
        [
            pltpu.VMEM((rows, size), BF16),
            pltpu.VMEM((size, columns), BF16),
            pltpu.VMEM((2, TAIL, columns), BF16),
            pltpu.SemaphoreType.DMA((3 + 2 * count,)),
        ],
        "square",
    )(*near, *far, panel, pair, pair_far[0])

    line_near = [square] + moves.line(square)
    line_far = [moves.core(value) for value in line_near]
    plane_near = [square] + [moves.in_plane(square, s) for s in slots]
    plane_far = [line_far[0]] + [moves.core(value) for value in plane_near[1:]]
    evolved = call(
        functools.partial(evolve_kernel, count),
        block,
        [ANY] * (4 * count + 2),
        [
            pltpu.VMEM((columns, size), BF16),
            pltpu.VMEM((size, columns), BF16),
            pltpu.VMEM((2, TAIL, columns), BF16),
            pltpu.SemaphoreType.DMA((2 + 4 * count,)),
        ],
        "evolve",
    )(*line_near, *line_far, *plane_near, *plane_far, pair, pair_far[0])
    return moves.relabel(evolved)


def solution(mesh):
    return jax.shard_map(
        functools.partial(on_device, mesh.shape["row"], mesh.shape["col"]),
        mesh=mesh,
        in_specs=(
            P("row", "col"),
            P("row", "col"),
            P("row", "col"),
            P(None, "row", "col"),
            P(None, "row", "col"),
            P(),
            P(None, "row", "col"),
        ),
        out_specs=P("row", "col"),
        check_vma=False,
    )
```

```python
import functools

import jax
import jax.numpy as jnp
from jax import lax
from jax.experimental import pallas as pl
from jax.experimental.pallas import tpu as pltpu
from jax.sharding import PartitionSpec as P

BLK = 32
TERMS = 6
SQUARINGS = 2
FIRST = 3
AXES = ("row", "col")
F32 = jnp.float32
BF16 = jnp.bfloat16
TAIL = 16
MEGABYTE = 1024 * 1024


def coordinates(r, c):
    return r // 2, r % 2, c // 2, c % 2


def permutation(rows, cols, source):
    pairs = []
    for r in range(rows):
        for c in range(cols):
            sr, sc = source(*coordinates(r, c))
            pairs.append((sr * cols + sc, r * cols + c))
    return pairs


class Moves:
    def __init__(self, rows, cols):
        self.rows, self.cols = rows, cols

    def move(self, value, source):
        return lax.ppermute(value, AXES, permutation(self.rows, self.cols, source))

    def relabel(self, value, k=0):
        return self.move(value, lambda z, y, x, e: (2 * (z ^ k) + e, 2 * x + y))

    def along_z(self, value, k):
        return self.move(value, lambda z, y, x, e: (2 * (z ^ k) + y, 2 * x + e))

    def line(self, value, relabel=False):
        bits = [1 << b for b in range((self.rows // 2).bit_length() - 1)]
        held = {0: value}
        for bit in reversed(bits):
            for k, part in list(held.items()):
                if k == 0 and relabel:
                    held[bit] = self.relabel(value, bit)
                else:
                    held[k | bit] = self.along_z(part, bit)
        return [held[k] for k in range(1, self.rows // 2)]

    def in_plane(self, value, s):
        return self.move(value, lambda z, y, x, e: (2 * z + (y ^ (s & 1)), 2 * (x ^ (s >> 1)) + e))

    def core(self, value):
        return self.move(value, lambda z, y, x, e: (2 * z + y, 2 * x + 1 - e))


def place():
    r, c = lax.axis_index("row"), lax.axis_index("col")
    z, y, x, e = r // 2, r % 2, c // 2, c % 2
    return z, 2 * x + y, e


def iota(shape, axis):
    return lax.broadcasted_iota(jnp.int32, shape, axis)


def dot(a, b):
    return jnp.dot(a, b, preferred_element_type=F32)


def repeat_rows(rows, blocks):
    return (iota((rows, blocks), 0) // BLK == iota((rows, blocks), 1)).astype(BF16)


def repeat_columns(blocks, columns, first=0):
    return (iota((blocks, columns), 0) == iota((blocks, columns), 1) // BLK + first).astype(BF16)


def block_mask(tail, number, rows, columns):
    blocks = columns // BLK
    wide = dot(repeat_rows(rows, tail.shape[0]), tail).astype(BF16)
    return dot(wide, repeat_columns(tail.shape[1], columns, number * blocks))


def call(kernel, outs, ins, scratch, name, flops=1000, room=16):
    return pl.pallas_call(
        kernel,
        out_shape=outs,
        in_specs=ins,
        out_specs=jax.tree.map(lambda _: pl.BlockSpec(memory_space=pltpu.VMEM), outs),
        scratch_shapes=scratch,
        name=name,
        compiler_params=pltpu.CompilerParams(vmem_limit_bytes=room * MEGABYTE),
        cost_estimate=pl.CostEstimate(flops=flops, bytes_accessed=1000, transcendentals=0),
    )


ANY = pl.BlockSpec(memory_space=pl.ANY)
INVMEM = pl.BlockSpec(memory_space=pltpu.VMEM)
INSMEM = pl.BlockSpec(memory_space=pltpu.SMEM)


def masked(ref, fill):
    rows, columns = ref.shape
    tall = repeat_rows(rows, fill.shape[0])
    wide = repeat_columns(fill.shape[1], columns)
    mask = dot(dot(tall, fill.astype(BF16)).astype(BF16), wide)
    return (ref[...].astype(F32) * mask).astype(BF16)


def density_kernel(density, fills, out):
    out[...] = masked(density, fills[1])


def pair_kernel(fock, margin, fills, firsts, seconds, pair):
    rows, columns = fock.shape
    row_blocks, column_blocks = rows // BLK, columns // BLK
    pair[TAIL : TAIL + rows, :] = masked(fock, fills[0])
    pair[TAIL + rows :, :] = masked(margin, fills[2])
    top = (iota((TAIL, row_blocks), 0) == iota((TAIL, row_blocks), 1)).astype(BF16)
    tail = jnp.zeros((TAIL, columns), F32)
    for number in range(firsts.shape[0] + seconds.shape[0]):
        ref = firsts[number] if number < FIRST else seconds[number - FIRST]
        column = iota((column_blocks, columns), 1) - number * column_blocks
        spread = (iota((column_blocks, columns), 0) == column).astype(BF16)
        tail += dot(dot(top, ref.astype(BF16)).astype(BF16), spread)
    pair[:TAIL, :] = tail.astype(BF16)


def chunk(index, length):
    return pl.ds(pl.multiple_of(index * length, length), length)


def start_all(copies):
    for one in copies:
        one.start()


def wait_all(copies):
    for one in copies:
        one.wait()


def repeat(times, body, unrolled):
    if unrolled:
        for t in range(times):
            body(t)
    else:

        def step(t, carry):
            body(t)
            return carry

        lax.fori_loop(0, times, step, 0)


def in_order(near, far, e):
    low = jnp.where(e == 0, near, far)
    high = jnp.where(e == 0, far, near)
    return jnp.concatenate([low, high], axis=0)


def first_kernel(count, starts, *refs):
    pair, parts = refs[0], refs[1 : 1 + 2 * count]
    near, far = refs[1 + 2 * count : 1 + 3 * count], refs[1 + 3 * count : 1 + 4 * count]
    out, left = refs[1 + 4 * count :]
    z, q, e = place()
    rows, columns = near[0].shape
    for s in range(count):
        for half in range(2):
            first = starts[s][half]
            left[q ^ s, half * rows : (half + 1) * rows, :] = parts[2 * s + half][
                first : first + rows, :
            ]
    masks = [block_mask(pair[:TAIL, :], n, rows, columns) for n in range(2)]
    total = jnp.zeros((2 * rows, columns), F32)
    for s in range(count):
        total += dot(left[z ^ s], in_order(near[s][...], far[s][...], e))
    for n in range(2):
        part = slice(n * rows, (n + 1) * rows)
        out[part, :] = (total[part] * masks[n]).astype(BF16)


def generator_kernel(count, starts, *refs):
    parts = refs[: 2 * count]
    near, far = refs[2 * count : 3 * count], refs[3 * count : 4 * count]
    out, left = refs[4 * count :]
    z, q, e = place()
    rows, columns = out.shape
    for half in range(2):
        for s in range(count):
            first = starts[s][half]
            left[half, q ^ s] = parts[2 * s + half][first : first + rows, :]
    mask = block_mask(near[0][:TAIL, :], 2, rows, columns)
    total = jnp.zeros((rows, columns), F32)
    for half in range(2):
        first = TAIL + (1 - half) * rows
        for s in range(count):
            right = in_order(
                near[s][first : first + rows, :], far[s][first : first + rows, :], e
            )
            product = dot(left[half, z ^ s], right)
            total = total + product if half == 0 else total - product
    generator = (total * mask).astype(BF16)
    out[...] = (generator.astype(F32) * 0.25).astype(BF16)


def series_kernel(layout, count, *refs):
    pieces = refs[: len(layout)]
    tails = refs[len(layout) : len(layout) + 2 * count]
    order = refs[len(layout) + 2 * count]
    panel, mine, whole, turned, wides, spread, sems = refs[len(layout) + 2 * count + 1 :]
    z, q, e = place()
    rows, columns = mine.shape
    size = panel.shape[1]
    row_blocks, column_blocks, blocks = rows // BLK, columns // BLK, size // BLK
    small = size <= 1536
    copies = []
    for ref, (runs, plane, lane) in zip(pieces, layout):
        core = e if lane == 0 else 1 - e
        for row, k, inner, length in runs:
            into = pl.ds(pl.multiple_of((2 * (z ^ k) + core) * rows + inner, BLK), length)
            copies.append(
                pltpu.make_async_copy(
                    ref.at[pl.ds(row, length)],
                    whole.at[into, chunk(q ^ plane, columns)],
                    sems.at[len(copies)],
                )
            )
    start_all(copies)
    for index, ref in enumerate(tails):
        core = e if index < count else 1 - e
        wides[2 * (z ^ (index % count)) + core] = ref[:TAIL, :]
    filters = jnp.zeros((128, size), F32)
    for p in range(2 * count):
        column = iota((TAIL, size), 1) // BLK
        row = iota((TAIL, size), 0)
        near = ((row < row_blocks) & (column == row + p * row_blocks)).astype(BF16)
        filters += lax.dot_general(
            wides[p][:, :128], near, (((0,), (0,)), ((), ())), preferred_element_type=F32
        )
    spread[...] = filters

    wait_all(copies)

    def turn(t):
        tile = jnp.concatenate(
            [whole[chunk(order[t * column_blocks + a], BLK), :] for a in range(column_blocks)],
            axis=0,
        )
        turned[:, chunk(t, columns)] = tile.T

    def place_rows(b):
        whole[chunk(b, BLK), :] = turned[chunk(order[b], BLK), :]

    repeat(count, turn, small)
    repeat(blocks, place_rows, small)

    first = (2 * q + e) * rows
    unit = (iota((rows, size), 1) == iota((rows, size), 0) + first).astype(F32)
    own = unit + whole[chunk(2 * q + e, rows), :].astype(F32) / TERMS
    panel[...] = own.astype(BF16)
    width = size if small else 512
    for number in range(1, TERMS):
        current = panel[...]
        base = (FIRST + number - 1) * column_blocks + e * row_blocks

        def advance(t):
            part = chunk(t, width)
            product = dot(current, whole[:, part])
            mask = jnp.concatenate(
                [
                    jnp.broadcast_to(spread[pl.ds(base + b, 1), part], (BLK, width))
                    for b in range(row_blocks)
                ],
                axis=0,
            )
            here = iota((rows, width), 1) + t * width == iota((rows, width), 0) + first
            panel[:, part] = (here.astype(F32) + product * mask / (TERMS - number)).astype(BF16)

        repeat(size // width, advance, small)
    mine[...] = panel[:, chunk(z, columns)]


def turned_mask(tails, number, e, rows, columns):
    row_blocks, column_blocks = rows // BLK, columns // BLK
    pick = iota((rows, 128), 0) // BLK + number * column_blocks + e * row_blocks
    pick = (pick == iota((rows, 128), 1)).astype(BF16)
    mask = jnp.zeros((rows, columns), F32)
    for core in range(2):
        row = iota((TAIL, columns), 0)
        near = (row < row_blocks) & (iota((TAIL, columns), 1) // BLK == row + core * row_blocks)
        chosen = lax.dot_general(
            pick, tails[core][:, :128], (((1,), (1,)), ((), ())), preferred_element_type=F32
        )
        mask += dot(chosen.astype(BF16), near.astype(BF16))
    return mask


def square_kernel(count, *refs):
    near, far = refs[:count], refs[count : 2 * count]
    panel, pair, other, out = refs[2 * count :]
    z, q, e = place()
    rows, columns = out.shape
    tails = in_order(pair[:TAIL, :], other[:TAIL, :], e)
    tails = [tails[:TAIL], tails[TAIL:]]
    mask = turned_mask(tails, FIRST + TERMS - 1, e, rows, columns)
    total = jnp.zeros((rows, columns), F32)
    for s in range(count):
        total += dot(panel[:, chunk(q ^ s, columns)], in_order(near[s][...], far[s][...], e))
    out[...] = (total * mask).astype(BF16)


def evolve_kernel(count, *refs):
    groups = [refs[n * count : (n + 1) * count] for n in range(4)]
    line_near, line_far, plane_near, plane_far = groups
    pair, out, right = refs[4 * count :]
    z, q, e = place()
    rows, columns = out.shape
    for s in range(count):
        right[q ^ s] = in_order(plane_near[s][...], plane_far[s][...], e)
    mask = block_mask(pair[:TAIL, :], FIRST + TERMS, rows, columns)
    total = jnp.zeros((columns, columns), F32)
    for s in range(count):
        total += dot(in_order(line_near[s][...], line_far[s][...], e), right[z ^ s])
    total = total.T
    chosen = jnp.where(e == 0, total[:rows], total[rows:])
    out[...] = (chosen * mask).astype(BF16)


def on_device(
    mesh_rows,
    mesh_cols,
    fock_matrix,
    density,
    margin,
    fill_patterns,
    first_filters,
    owner_order,
    second_filters,
):
    moves = Moves(mesh_rows, mesh_cols)
    count = mesh_cols
    slots = range(1, count)
    half = count // 2
    rows, columns = fock_matrix.shape
    size = rows * mesh_rows
    block = jax.ShapeDtypeStruct((rows, columns), BF16)

    masked_density = call(density_kernel, block, [INVMEM] * 2, [], "density")(
        density, fill_patterns
    )
    masked_density, fock_matrix, second_filters = lax.optimization_barrier(
        (masked_density, fock_matrix, second_filters)
    )
    pair = call(
        pair_kernel,
        jax.ShapeDtypeStruct((TAIL + 2 * rows, columns), BF16),
        [INVMEM] * 5,
        [],
        "pair",
        10**10,
    )(fock_matrix, margin, fill_patterns, first_filters, second_filters)

    def plane_parts(value, first):
        parts = [value, value]
        starts = [(first, first + rows)]
        planes = {}
        for s in slots:
            if count == 4 and s == 3:
                top, bottom = planes[2][:rows], planes[1][rows:]
                parts += [moves.in_plane(top, 1), moves.in_plane(bottom, 2)]
                starts.append((0, 0))
            else:
                planes[s] = moves.in_plane(value[first : first + 2 * rows], s)
                parts += [planes[s], planes[s]]
                starts.append((0, rows))
        return parts, starts

    density_near = [moves.relabel(masked_density)] + moves.line(masked_density, True)
    pair = moves.relabel(pair)
    soon, density_near[half] = lax.optimization_barrier((pair, density_near[half]))
    parts, starts = plane_parts(soon, TAIL)
    pair, *density_near = lax.optimization_barrier((pair, *density_near))
    pair_near = moves.line(pair)
    density_far = [moves.core(value) for value in density_near]
    pair_far = [moves.core(pair)]
    parts, pair_far[0], pair_near[:half] = lax.optimization_barrier(
        (parts, pair_far[0], pair_near[:half])
    )

    products = call(
        functools.partial(first_kernel, count, starts),
        jax.ShapeDtypeStruct((2 * rows, columns), BF16),
        [INVMEM] * (1 + 4 * count),
        [pltpu.VMEM((count, 2 * rows, columns), BF16)],
        "first",
        10**10,
    )(pair, *parts, *density_near, *density_far)
    parts, starts = plane_parts(products, 0)
    parts, pair_near = lax.optimization_barrier((parts, pair_near))
    pair_near = [pair] + pair_near
    pair_far += [moves.core(value) for value in pair_near[1:]]

    generator = call(
        functools.partial(generator_kernel, count, starts),
        block,
        [INVMEM] * (4 * count),
        [pltpu.VMEM((2, count, rows, columns), BF16)],
        "generator",
    )(*parts, *pair_near, *pair_far)

    layout, pieces = [], []

    def keep(held, s, value, first=0):
        runs, row = [], 0
        while row < value.shape[0]:
            index, inner = divmod(first + row, rows)
            length = min(rows - inner, value.shape[0] - row)
            runs.append((row, held[index], inner, length))
            row += length
        layout.extend([(runs, s, 0), (runs, s, 1)])
        pieces.extend([value, moves.core(value)])

    def planes_of(group):
        return {s: moves.in_plane(group, s) for s in slots if not (count == 4 and s == 3)}

    def corners_of(planes):
        if count != 4:
            return []
        cut = planes[1].shape[0] // 2
        return [moves.in_plane(planes[2][:cut], 1), moves.in_plane(planes[1][cut:], 2)]

    def keep_all(held, group, planes, corners):
        keep(held, 0, group)
        for s, value in planes.items():
            keep(held, s, value)
        first = 0
        for value in corners:
            keep(held, 3, value, first)
            first += value.shape[0]

    planes = planes_of(generator)
    if count == 4:
        near, far = moves.along_z(generator, 1), moves.along_z(generator, 2)
        far, planes = lax.optimization_barrier((far, planes))
        corners = corners_of(planes)
        last = moves.along_z(far, 1)
        middle = jnp.concatenate([near, far], axis=0)
        later = planes_of(middle)
        last, corners, later = lax.optimization_barrier((last, corners, later))
        keep_all((0,), generator, planes, corners)
        final = planes_of(last)
        keep_all((1, 2), middle, later, corners_of(later))
        keep_all((3,), last, final, corners_of(final))
    else:
        keep_all((0,), generator, planes, [])
        rest = jnp.concatenate(moves.line(generator), axis=0)
        keep_all(tuple(slots), rest, planes_of(rest), [])
    runs = sum(len(part[0]) for part in layout)

    panel, mine = call(
        functools.partial(series_kernel, layout, count),
        [jax.ShapeDtypeStruct((rows, size), BF16), block],
        [ANY] * len(layout) + [INVMEM] * (2 * count) + [INSMEM],
        [
            pltpu.VMEM((size, size), BF16),
            pltpu.VMEM((size, size), BF16),
            pltpu.VMEM((mesh_rows, TAIL, columns), BF16),
            pltpu.VMEM((128, size), F32),
            pltpu.SemaphoreType.DMA((runs,)),
        ],
        "series",
        room=16 + 4 * size * size // MEGABYTE,
    )(*pieces, *pair_near, *pair_far, owner_order)

    near = [mine] + [moves.in_plane(mine, s) for s in slots]
    far = [moves.core(value) for value in near]
    square = call(
        functools.partial(square_kernel, count),
        block,
        [INVMEM] * (2 * count + 3),
        [],
        "square",
    )(*near, *far, panel, pair, pair_far[0])

    line_near = [square] + moves.line(square)
    soon, line_near[1] = lax.optimization_barrier((square, line_near[1]))
    plane_near = [square] + [moves.in_plane(soon, s) for s in slots]
    line_far = [moves.core(value) for value in line_near]
    plane_far = [line_far[0]] + [moves.core(value) for value in plane_near[1:]]
    evolved = call(
        functools.partial(evolve_kernel, count),
        block,
        [INVMEM] * (4 * count + 1),
        [pltpu.VMEM((count, columns, columns), BF16)],
        "evolve",
    )(*line_near, *line_far, *plane_near, *plane_far, pair)
    return moves.relabel(evolved)


def solution(mesh):
    return jax.shard_map(
        functools.partial(on_device, mesh.shape["row"], mesh.shape["col"]),
        mesh=mesh,
        in_specs=(
            P("row", "col"),
            P("row", "col"),
            P("row", "col"),
            P(None, "row", "col"),
            P(None, "row", "col"),
            P(),
            P(None, "row", "col"),
        ),
        out_specs=P("row", "col"),
        check_vma=False,
    )
```

```python
import functools

import jax
import jax.numpy as jnp
from jax import lax
from jax.experimental import pallas as pl
from jax.experimental.pallas import tpu as pltpu
from jax.sharding import PartitionSpec as P

BLK = 32
TERMS = 6
SQUARINGS = 2
FIRST = 3
AXES = ("row", "col")
F32 = jnp.float32
BF16 = jnp.bfloat16
TAIL = 16
MEGABYTE = 1024 * 1024


def coordinates(r, c):
    return r // 2, r % 2, c // 2, c % 2


def permutation(rows, cols, source):
    pairs = []
    for r in range(rows):
        for c in range(cols):
            sr, sc = source(*coordinates(r, c))
            pairs.append((sr * cols + sc, r * cols + c))
    return pairs


class Moves:
    def __init__(self, rows, cols):
        self.rows, self.cols = rows, cols

    def move(self, value, source):
        return lax.ppermute(value, AXES, permutation(self.rows, self.cols, source))

    def relabel(self, value, k=0):
        return self.move(value, lambda z, y, x, e: (2 * (z ^ k) + e, 2 * x + y))

    def along_z(self, value, k):
        return self.move(value, lambda z, y, x, e: (2 * (z ^ k) + y, 2 * x + e))

    def line(self, value, relabel=False, gate=None):
        bits = [1 << b for b in range((self.rows // 2).bit_length() - 1)]
        held = {0: value}
        for bit in reversed(bits):
            for k, part in list(held.items()):
                if k == 0 and relabel:
                    held[bit] = self.relabel(value, bit)
                else:
                    if k and gate is not None:
                        part, _ = lax.optimization_barrier((part, gate))
                    held[k | bit] = self.along_z(part, bit)
        return [held[k] for k in range(1, self.rows // 2)]

    def in_plane(self, value, s):
        return self.move(value, lambda z, y, x, e: (2 * z + (y ^ (s & 1)), 2 * (x ^ (s >> 1)) + e))

    def plane(self, value, relabel=False):
        if relabel:
            return [
                self.move(value, lambda z, y, x, e: (2 * z + e, 2 * (x ^ (s >> 1)) + (y ^ (s & 1))))
                for s in range(1, self.cols)
            ]
        return [self.in_plane(value, s) for s in range(1, self.cols)]

    def core(self, value):
        return self.move(value, lambda z, y, x, e: (2 * z + y, 2 * x + 1 - e))

    def cores(self, values):
        length = values[0].shape[0]
        far = self.core(jnp.concatenate(values, axis=0) if len(values) > 1 else values[0])
        return [(far, n * length) for n in range(len(values))]


def place():
    r, c = lax.axis_index("row"), lax.axis_index("col")
    z, y, x, e = r // 2, r % 2, c // 2, c % 2
    return z, 2 * x + y, e


def iota(shape, axis):
    return lax.broadcasted_iota(jnp.int32, shape, axis)


def dot(a, b):
    return jnp.dot(a, b, preferred_element_type=F32)


def repeat_rows(rows, blocks):
    return (iota((rows, blocks), 0) // BLK == iota((rows, blocks), 1)).astype(BF16)


def repeat_columns(blocks, columns, first=0):
    return (iota((blocks, columns), 0) == iota((blocks, columns), 1) // BLK + first).astype(BF16)


def block_mask(tail, number, rows, columns):
    blocks = columns // BLK
    wide = dot(repeat_rows(rows, tail.shape[0]), tail).astype(BF16)
    return dot(wide, repeat_columns(tail.shape[1], columns, number * blocks))


def call(kernel, outs, ins, scratch, name, flops=1000, room=16):
    return pl.pallas_call(
        kernel,
        out_shape=outs,
        in_specs=ins,
        out_specs=jax.tree.map(lambda _: pl.BlockSpec(memory_space=pltpu.VMEM), outs),
        scratch_shapes=scratch,
        name=name,
        compiler_params=pltpu.CompilerParams(vmem_limit_bytes=room * MEGABYTE),
        cost_estimate=pl.CostEstimate(flops=flops, bytes_accessed=1000, transcendentals=0),
    )


def views_call(kernel, views, outs, scratch, name, flops=1000, extra=()):
    arrays, spec = [], {}
    for key, items in views.items():
        spec[key] = []
        for value, first in items:
            known = [n for n, other in enumerate(arrays) if other is value]
            if not known:
                arrays.append(value)
            spec[key].append((known[0] if known else len(arrays) - 1, first))

    def body(*refs):
        def take(key, n, length, shift=0):
            index, first = spec[key][n]
            return refs[index][first + shift : first + shift + length, :]

        kernel(take, *refs[len(arrays) :])

    operands = [*arrays, *extra]
    return call(body, outs, [INVMEM] * len(operands), scratch, name, flops)(*operands)


ANY = pl.BlockSpec(memory_space=pl.ANY)
INVMEM = pl.BlockSpec(memory_space=pltpu.VMEM)
INSMEM = pl.BlockSpec(memory_space=pltpu.SMEM)


def masked(ref, fill):
    rows, columns = ref.shape
    tall = repeat_rows(rows, fill.shape[0])
    wide = repeat_columns(fill.shape[1], columns)
    mask = dot(dot(tall, fill.astype(BF16)).astype(BF16), wide)
    return (ref[...].astype(F32) * mask).astype(BF16)


def density_kernel(density, fills, out):
    out[...] = masked(density, fills[1])


def pair_kernel(fock, margin, density, fills, firsts, seconds, duo, trio):
    rows, columns = fock.shape
    row_blocks, column_blocks = rows // BLK, columns // BLK
    for half, (ref, number) in enumerate(((fock, 0), (margin, 2))):
        value = masked(ref, fills[number])
        duo[half * rows : (half + 1) * rows, :] = value
        trio[TAIL + half * rows : TAIL + (half + 1) * rows, :] = value
    trio[TAIL + 2 * rows :, :] = density[...]
    top = (iota((TAIL, row_blocks), 0) == iota((TAIL, row_blocks), 1)).astype(BF16)
    tail = jnp.zeros((TAIL, columns), F32)
    for number in range(firsts.shape[0] + seconds.shape[0]):
        ref = firsts[number] if number < FIRST else seconds[number - FIRST]
        column = iota((column_blocks, columns), 1) - number * column_blocks
        spread = (iota((column_blocks, columns), 0) == column).astype(BF16)
        tail += dot(dot(top, ref.astype(BF16)).astype(BF16), spread)
    trio[:TAIL, :] = tail.astype(BF16)


def chunk(index, length):
    return pl.ds(pl.multiple_of(index * length, length), length)


def start_all(copies):
    for one in copies:
        one.start()


def wait_all(copies):
    for one in copies:
        one.wait()


def repeat(times, body, unrolled):
    if unrolled:
        for t in range(times):
            body(t)
    else:

        def step(t, carry):
            body(t)
            return carry

        lax.fori_loop(0, times, step, 0)


def in_order(near, far, e):
    low = jnp.where(e == 0, near, far)
    high = jnp.where(e == 0, far, near)
    return jnp.concatenate([low, high], axis=0)


def first_kernel(count, take, out, left):
    z, q, e = place()
    rows, columns = out.shape[0] // 2, out.shape[1]
    for s in range(count):
        left[q ^ s] = take("plane", s, 2 * rows)
    tail = take("tail", 0, TAIL)
    masks = [block_mask(tail, n, rows, columns) for n in range(2)]
    total = jnp.zeros((2 * rows, columns), F32)
    for s in range(count):
        total += dot(left[z ^ s], in_order(take("near", s, rows), take("far", s, rows), e))
    for n in range(2):
        part = slice(n * rows, (n + 1) * rows)
        out[part, :] = (total[part] * masks[n]).astype(BF16)


def generator_kernel(count, take, out, left):
    z, q, e = place()
    rows, columns = out.shape
    for s in range(count):
        for half in range(2):
            left[half, q ^ s] = take("plane", s, rows, half * rows)
    mask = block_mask(take("tail", 0, TAIL), 2, rows, columns)
    total = jnp.zeros((rows, columns), F32)
    for half in range(2):
        shift = (1 - half) * rows
        for s in range(count):
            right = in_order(take("near", s, rows, shift), take("far", s, rows, shift), e)
            product = dot(left[half, z ^ s], right)
            total = total + product if half == 0 else total - product
    generator = (total * mask).astype(BF16)
    out[...] = (generator.astype(F32) * 0.25).astype(BF16)


def series_kernel(layout, count, pieces, *refs):
    arrays, tails, order = refs[:pieces], refs[pieces : pieces + 2 * count], refs[pieces + 2 * count]
    panel, mine, whole, turned, wides, spread, sems = refs[pieces + 2 * count + 1 :]
    z, q, e = place()
    rows, columns = mine.shape
    size = panel.shape[1]
    row_blocks, column_blocks, blocks = rows // BLK, columns // BLK, size // BLK
    small = size <= 1536
    copies = []
    for index, first, k, plane, lane in layout:
        core = e if lane == 0 else 1 - e
        copies.append(
            pltpu.make_async_copy(
                arrays[index].at[pl.ds(first, rows)],
                whole.at[chunk(2 * (z ^ k) + core, rows), chunk(q ^ plane, columns)],
                sems.at[len(copies)],
            )
        )
    start_all(copies)
    for index, ref in enumerate(tails):
        core = e if index < count else 1 - e
        wides[2 * (z ^ (index % count)) + core] = ref[...]
    filters = jnp.zeros((128, size), F32)
    for p in range(2 * count):
        column = iota((TAIL, size), 1) // BLK
        row = iota((TAIL, size), 0)
        near = ((row < row_blocks) & (column == row + p * row_blocks)).astype(BF16)
        filters += lax.dot_general(
            wides[p][:, :128], near, (((0,), (0,)), ((), ())), preferred_element_type=F32
        )
    spread[...] = filters

    wait_all(copies)

    def turn(t):
        tile = jnp.concatenate(
            [whole[chunk(order[t * column_blocks + a], BLK), :] for a in range(column_blocks)],
            axis=0,
        )
        turned[:, chunk(t, columns)] = tile.T

    def place_rows(b):
        whole[chunk(b, BLK), :] = turned[chunk(order[b], BLK), :]

    repeat(count, turn, small)
    repeat(blocks, place_rows, small)

    first = (2 * q + e) * rows
    unit = (iota((rows, size), 1) == iota((rows, size), 0) + first).astype(F32)
    own = unit + whole[chunk(2 * q + e, rows), :].astype(F32) / TERMS
    panel[...] = own.astype(BF16)
    width = size if small else 512
    for number in range(1, TERMS):
        current = panel[...]
        base = (FIRST + number - 1) * column_blocks + e * row_blocks

        def advance(t):
            part = chunk(t, width)
            product = dot(current, whole[:, part])
            mask = jnp.concatenate(
                [
                    jnp.broadcast_to(spread[pl.ds(base + b, 1), part], (BLK, width))
                    for b in range(row_blocks)
                ],
                axis=0,
            )
            here = iota((rows, width), 1) + t * width == iota((rows, width), 0) + first
            panel[:, part] = (here.astype(F32) + product * mask / (TERMS - number)).astype(BF16)

        repeat(size // width, advance, small)
    mine[...] = panel[:, chunk(z, columns)]


def turned_mask(tails, number, e, rows, columns):
    row_blocks, column_blocks = rows // BLK, columns // BLK
    pick = iota((rows, 128), 0) // BLK + number * column_blocks + e * row_blocks
    pick = (pick == iota((rows, 128), 1)).astype(BF16)
    mask = jnp.zeros((rows, columns), F32)
    for core in range(2):
        row = iota((TAIL, columns), 0)
        near = (row < row_blocks) & (iota((TAIL, columns), 1) // BLK == row + core * row_blocks)
        chosen = lax.dot_general(
            pick, tails[core][:, :128], (((1,), (1,)), ((), ())), preferred_element_type=F32
        )
        mask += dot(chosen.astype(BF16), near.astype(BF16))
    return mask


def square_kernel(count, take, panel, out):
    z, q, e = place()
    rows, columns = out.shape
    tails = in_order(take("tail", 0, TAIL), take("tail", 1, TAIL), e)
    mask = turned_mask([tails[:TAIL], tails[TAIL:]], FIRST + TERMS - 1, e, rows, columns)
    total = jnp.zeros((rows, columns), F32)
    for s in range(count):
        right = in_order(take("near", s, rows), take("far", s, rows), e)
        total += dot(panel[:, chunk(q ^ s, columns)], right)
    out[...] = (total * mask).astype(BF16)


def evolve_kernel(count, take, out, right):
    z, q, e = place()
    rows, columns = out.shape
    for s in range(count):
        right[q ^ s] = in_order(take("plane_near", s, rows), take("plane_far", s, rows), e)
    mask = block_mask(take("tail", 0, TAIL), FIRST + TERMS, rows, columns)
    total = jnp.zeros((columns, columns), F32)
    for s in range(count):
        total += dot(
            in_order(take("line_near", s, rows), take("line_far", s, rows), e), right[z ^ s]
        )
    total = total.T
    chosen = jnp.where(e == 0, total[:rows], total[rows:])
    out[...] = (chosen * mask).astype(BF16)


def on_device(
    mesh_rows,
    mesh_cols,
    fock_matrix,
    density,
    margin,
    fill_patterns,
    first_filters,
    owner_order,
    second_filters,
):
    moves = Moves(mesh_rows, mesh_cols)
    count = mesh_cols
    half = count // 2
    rows, columns = fock_matrix.shape
    size = rows * mesh_rows
    block = jax.ShapeDtypeStruct((rows, columns), BF16)
    barrier = lax.optimization_barrier

    def whole(values):
        return [(value, 0) for value in values]

    masked_density = call(density_kernel, block, [INVMEM] * 2, [], "density")(
        density, fill_patterns
    )
    later, fock_matrix, second_filters = barrier((masked_density, fock_matrix, second_filters))
    duo, trio = call(
        pair_kernel,
        [
            jax.ShapeDtypeStruct((2 * rows, columns), BF16),
            jax.ShapeDtypeStruct((TAIL + 3 * rows, columns), BF16),
        ],
        [INVMEM] * 6,
        [],
        "pair",
        10**10,
    )(fock_matrix, margin, later, fill_patterns, first_filters, second_filters)

    trio = moves.relabel(trio)
    fock_rows = moves.plane(duo, True)
    density_line = moves.line(masked_density, True)
    density_near = [(trio, TAIL + 2 * rows)] + whole(density_line)
    density_line = list(barrier((*density_line, *fock_rows))[: count - 1])
    trio_far = moves.core(trio)
    density_far = [(trio_far, TAIL + 2 * rows)] + moves.cores(density_line)
    pair, *_ = barrier((trio[: TAIL + 2 * rows], *density_line, *fock_rows))

    products = views_call(
        functools.partial(first_kernel, count),
        {
            "plane": [(trio, TAIL)] + whole(fock_rows),
            "tail": [(trio, 0)],
            "near": density_near,
            "far": density_far,
        },
        jax.ShapeDtypeStruct((2 * rows, columns), BF16),
        [pltpu.VMEM((count, 2 * rows, columns), BF16)],
        "first",
        10**10,
    )
    product_rows = [products] + moves.plane(products)
    pair_line = moves.line(pair, gate=products)
    pair_line = list(barrier((*pair_line, *product_rows[1:]))[: count - 1])
    pair_far = [(trio_far, 0)] + moves.cores(pair_line[:half]) + moves.cores(pair_line[half:])
    pair_near = [(trio, 0)] + whole(pair_line)

    generator = views_call(
        functools.partial(generator_kernel, count),
        {
            "plane": whole(product_rows),
            "tail": [(trio, 0)],
            "near": [(value, first + TAIL) for value, first in pair_near],
            "far": [(value, first + TAIL) for value, first in pair_far],
        },
        block,
        [pltpu.VMEM((2, count, rows, columns), BF16)],
        "generator",
    )

    lines = [generator] + moves.line(generator)
    arrays, layout, planes = [], [], []
    for held in (range(1), range(1, half + 1), range(half + 1, count)):
        group = jnp.concatenate([lines[k] for k in held], axis=0) if len(held) > 1 else lines[held[0]]
        if len(held) > 1:
            group, *planes = barrier((group, *planes))
        planes = [group] + moves.plane(group)
        ready = planes
        if 1 < len(held) < count - 1:
            *ready, _ = barrier((*planes, *lines[half + 1 :]))[: count + 1]
        far = moves.cores(ready)
        for s, value in enumerate(planes):
            for lane, (array, start) in enumerate(((value, 0), far[s])):
                if not any(other is array for other in arrays):
                    arrays.append(array)
                index = [n for n, other in enumerate(arrays) if other is array][0]
                for n, k in enumerate(held):
                    layout.append((index, start + n * rows, k, s, lane))
    tails = [value[first : first + TAIL] for value, first in pair_near + pair_far]

    panel, mine = call(
        functools.partial(series_kernel, layout, count, len(arrays)),
        [jax.ShapeDtypeStruct((rows, size), BF16), block],
        [ANY] * len(arrays) + [INVMEM] * (2 * count) + [INSMEM],
        [
            pltpu.VMEM((size, size), BF16),
            pltpu.VMEM((size, size), BF16),
            pltpu.VMEM((mesh_rows, TAIL, columns), BF16),
            pltpu.VMEM((128, size), F32),
            pltpu.SemaphoreType.DMA((len(layout),)),
        ],
        "series",
        room=16 + 4 * size * size // MEGABYTE,
    )(*arrays, *tails, owner_order)

    near = [mine] + moves.plane(mine)
    square = views_call(
        functools.partial(square_kernel, count),
        {"near": whole(near), "far": moves.cores(near), "tail": [(trio, 0), (trio_far, 0)]},
        block,
        [],
        "square",
        extra=[panel],
    )

    line = moves.line(square)
    plane_near = [square] + moves.plane(square)
    plane_far = moves.cores(plane_near)
    evolved = views_call(
        functools.partial(evolve_kernel, count),
        {
            "plane_near": whole(plane_near),
            "plane_far": plane_far,
            "line_near": whole([square] + line),
            "line_far": plane_far[:1] + moves.cores(line),
            "tail": [(trio, 0)],
        },
        block,
        [pltpu.VMEM((count, columns, columns), BF16)],
        "evolve",
    )
    return moves.relabel(evolved)


def solution(mesh):
    return jax.shard_map(
        functools.partial(on_device, mesh.shape["row"], mesh.shape["col"]),
        mesh=mesh,
        in_specs=(
            P("row", "col"),
            P("row", "col"),
            P("row", "col"),
            P(None, "row", "col"),
            P(None, "row", "col"),
            P(),
            P(None, "row", "col"),
        ),
        out_specs=P("row", "col"),
        check_vma=False,
    )
```

```python
import functools

import jax
import jax.numpy as jnp
from jax import lax
from jax.experimental import pallas as pl
from jax.experimental.pallas import tpu as pltpu
from jax.sharding import PartitionSpec as P

BLK = 32
TERMS = 6
SQUARINGS = 2
FIRST = 3
AXES = ("row", "col")
F32 = jnp.float32
BF16 = jnp.bfloat16
TAIL = 16
MEGABYTE = 1024 * 1024


def coordinates(r, c):
    return r // 2, r % 2, c // 2, c % 2


def permutation(rows, cols, source):
    pairs = []
    for r in range(rows):
        for c in range(cols):
            sr, sc = source(*coordinates(r, c))
            pairs.append((sr * cols + sc, r * cols + c))
    return pairs


class Moves:
    def __init__(self, rows, cols):
        self.rows, self.cols = rows, cols

    def move(self, value, source):
        return lax.ppermute(value, AXES, permutation(self.rows, self.cols, source))

    def relabel(self, value, k=0):
        return self.move(value, lambda z, y, x, e: (2 * (z ^ k) + e, 2 * x + y))

    def along_z(self, value, k):
        return self.move(value, lambda z, y, x, e: (2 * (z ^ k) + y, 2 * x + e))

    def line(self, value, relabel=False, second=None, gate=None):
        bits = [1 << b for b in range((self.rows // 2).bit_length() - 1)]
        held = {0: value}
        for bit in reversed(bits):
            for k, part in list(held.items()):
                if k == 0 and relabel:
                    held[bit] = self.relabel(value, bit)
                else:
                    if k and gate is not None:
                        part, _ = lax.optimization_barrier((part, gate))
                    held[k | bit] = self.along_z(part, bit)
            if second is not None:
                held[0] = second
        return [held[k] for k in range(1, self.rows // 2)]

    def in_plane(self, value, s):
        return self.move(value, lambda z, y, x, e: (2 * z + (y ^ (s & 1)), 2 * (x ^ (s >> 1)) + e))

    def plane(self, value, relabel=False):
        if relabel:
            return [
                self.move(value, lambda z, y, x, e: (2 * z + e, 2 * (x ^ (s >> 1)) + (y ^ (s & 1))))
                for s in range(1, self.cols)
            ]
        return [self.in_plane(value, s) for s in range(1, self.cols)]

    def core(self, value):
        return self.move(value, lambda z, y, x, e: (2 * z + y, 2 * x + 1 - e))

    def cores(self, values):
        length = values[0].shape[0]
        far = self.core(jnp.concatenate(values, axis=0) if len(values) > 1 else values[0])
        return [(far, n * length) for n in range(len(values))]


def place():
    r, c = lax.axis_index("row"), lax.axis_index("col")
    z, y, x, e = r // 2, r % 2, c // 2, c % 2
    return z, 2 * x + y, e


def iota(shape, axis):
    return lax.broadcasted_iota(jnp.int32, shape, axis)


def dot(a, b):
    return jnp.dot(a, b, preferred_element_type=F32)


def repeat_rows(rows, blocks):
    return (iota((rows, blocks), 0) // BLK == iota((rows, blocks), 1)).astype(BF16)


def repeat_columns(blocks, columns, first=0):
    return (iota((blocks, columns), 0) == iota((blocks, columns), 1) // BLK + first).astype(BF16)


def block_mask(tail, number, rows, columns):
    blocks = columns // BLK
    wide = dot(repeat_rows(rows, tail.shape[0]), tail).astype(BF16)
    return dot(wide, repeat_columns(tail.shape[1], columns, number * blocks))


def call(kernel, outs, ins, scratch, name, flops=1000, room=16):
    return pl.pallas_call(
        kernel,
        out_shape=outs,
        in_specs=ins,
        out_specs=jax.tree.map(lambda _: pl.BlockSpec(memory_space=pltpu.VMEM), outs),
        scratch_shapes=scratch,
        name=name,
        compiler_params=pltpu.CompilerParams(vmem_limit_bytes=room * MEGABYTE),
        cost_estimate=pl.CostEstimate(flops=flops, bytes_accessed=1000, transcendentals=0),
    )


def views_call(kernel, views, outs, scratch, name, flops=1000, extra=()):
    arrays, spec = [], {}
    for key, items in views.items():
        spec[key] = []
        for value, first in items:
            known = [n for n, other in enumerate(arrays) if other is value]
            if not known:
                arrays.append(value)
            spec[key].append((known[0] if known else len(arrays) - 1, first))

    def body(*refs):
        def take(key, n, length, shift=0):
            index, first = spec[key][n]
            return refs[index][first + shift : first + shift + length, :]

        kernel(take, *refs[len(arrays) :])

    operands = [*arrays, *extra]
    return call(body, outs, [INVMEM] * len(operands), scratch, name, flops)(*operands)


ANY = pl.BlockSpec(memory_space=pl.ANY)
INVMEM = pl.BlockSpec(memory_space=pltpu.VMEM)
INSMEM = pl.BlockSpec(memory_space=pltpu.SMEM)


def masked(ref, fill):
    rows, columns = ref.shape
    tall = repeat_rows(rows, fill.shape[0])
    wide = repeat_columns(fill.shape[1], columns)
    mask = dot(dot(tall, fill.astype(BF16)).astype(BF16), wide)
    return (ref[...].astype(F32) * mask).astype(BF16)


def density_kernel(density, fills, out):
    out[...] = masked(density, fills[1])


def pair_kernel(fock, margin, density, fills, firsts, seconds, duo, trio):
    rows, columns = fock.shape
    row_blocks, column_blocks = rows // BLK, columns // BLK
    for half, (ref, number) in enumerate(((fock, 0), (margin, 2))):
        value = masked(ref, fills[number])
        duo[half * rows : (half + 1) * rows, :] = value
        trio[TAIL + half * rows : TAIL + (half + 1) * rows, :] = value
    trio[TAIL + 2 * rows :, :] = density[...]
    top = (iota((TAIL, row_blocks), 0) == iota((TAIL, row_blocks), 1)).astype(BF16)
    tail = jnp.zeros((TAIL, columns), F32)
    for number in range(firsts.shape[0] + seconds.shape[0]):
        ref = firsts[number] if number < FIRST else seconds[number - FIRST]
        column = iota((column_blocks, columns), 1) - number * column_blocks
        spread = (iota((column_blocks, columns), 0) == column).astype(BF16)
        tail += dot(dot(top, ref.astype(BF16)).astype(BF16), spread)
    trio[:TAIL, :] = tail.astype(BF16)


def chunk(index, length):
    return pl.ds(pl.multiple_of(index * length, length), length)


def start_all(copies):
    for one in copies:
        one.start()


def wait_all(copies):
    for one in copies:
        one.wait()


def repeat(times, body, unrolled):
    if unrolled:
        for t in range(times):
            body(t)
    else:

        def step(t, carry):
            body(t)
            return carry

        lax.fori_loop(0, times, step, 0)


def in_order(near, far, e):
    low = jnp.where(e == 0, near, far)
    high = jnp.where(e == 0, far, near)
    return jnp.concatenate([low, high], axis=0)


def first_kernel(count, take, out, left):
    z, q, e = place()
    rows, columns = out.shape[0] // 2, out.shape[1]
    for s in range(count):
        left[q ^ s] = take("plane", s, 2 * rows)
    tail = take("tail", 0, TAIL)
    masks = [block_mask(tail, n, rows, columns) for n in range(2)]
    total = jnp.zeros((2 * rows, columns), F32)
    for s in range(count):
        total += dot(left[z ^ s], in_order(take("near", s, rows), take("far", s, rows), e))
    for n in range(2):
        part = slice(n * rows, (n + 1) * rows)
        out[part, :] = (total[part] * masks[n]).astype(BF16)


def generator_kernel(count, take, out, left):
    z, q, e = place()
    rows, columns = out.shape
    for s in range(count):
        for half in range(2):
            left[half, q ^ s] = take("plane", s, rows, half * rows)
    mask = block_mask(take("tail", 0, TAIL), 2, rows, columns)
    total = jnp.zeros((rows, columns), F32)
    for half in range(2):
        shift = (1 - half) * rows
        for s in range(count):
            right = in_order(take("near", s, rows, shift), take("far", s, rows, shift), e)
            product = dot(left[half, z ^ s], right)
            total = total + product if half == 0 else total - product
    generator = (total * mask).astype(BF16)
    out[...] = (generator.astype(F32) * 0.25).astype(BF16)


def series_kernel(layout, count, pieces, *refs):
    arrays, tails, order = refs[:pieces], refs[pieces : pieces + 2 * count], refs[pieces + 2 * count]
    panel, mine, whole, turned, wides, spread, sems = refs[pieces + 2 * count + 1 :]
    z, q, e = place()
    rows, columns = mine.shape
    size = panel.shape[1]
    row_blocks, column_blocks, blocks = rows // BLK, columns // BLK, size // BLK
    small = size <= 1536
    copies = []
    for index, first, k, plane, lane in layout:
        core = e if lane == 0 else 1 - e
        copies.append(
            pltpu.make_async_copy(
                arrays[index].at[pl.ds(first, rows)],
                whole.at[chunk(2 * (z ^ k) + core, rows), chunk(q ^ plane, columns)],
                sems.at[len(copies)],
            )
        )
    start_all(copies)
    for index, ref in enumerate(tails):
        core = e if index < count else 1 - e
        wides[2 * (z ^ (index % count)) + core] = ref[...]
    filters = jnp.zeros((128, size), F32)
    for p in range(2 * count):
        column = iota((TAIL, size), 1) // BLK
        row = iota((TAIL, size), 0)
        near = ((row < row_blocks) & (column == row + p * row_blocks)).astype(BF16)
        filters += lax.dot_general(
            wides[p][:, :128], near, (((0,), (0,)), ((), ())), preferred_element_type=F32
        )
    spread[...] = filters

    wait_all(copies)

    def turn(t):
        tile = jnp.concatenate(
            [whole[chunk(order[t * column_blocks + a], BLK), :] for a in range(column_blocks)],
            axis=0,
        )
        turned[:, chunk(t, columns)] = tile.T

    def place_rows(b):
        whole[chunk(b, BLK), :] = turned[chunk(order[b], BLK), :]

    repeat(count, turn, small)
    repeat(blocks, place_rows, small)

    first = (2 * q + e) * rows
    unit = (iota((rows, size), 1) == iota((rows, size), 0) + first).astype(F32)
    own = unit + whole[chunk(2 * q + e, rows), :].astype(F32) / TERMS
    panel[...] = own.astype(BF16)
    width = size if small else 512
    for number in range(1, TERMS):
        current = panel[...]
        base = (FIRST + number - 1) * column_blocks + e * row_blocks

        def advance(t):
            part = chunk(t, width)
            product = dot(current, whole[:, part])
            mask = jnp.concatenate(
                [
                    jnp.broadcast_to(spread[pl.ds(base + b, 1), part], (BLK, width))
                    for b in range(row_blocks)
                ],
                axis=0,
            )
            here = iota((rows, width), 1) + t * width == iota((rows, width), 0) + first
            panel[:, part] = (here.astype(F32) + product * mask / (TERMS - number)).astype(BF16)

        repeat(size // width, advance, small)
    mine[...] = panel[:, chunk(z, columns)]


def turned_mask(tails, number, e, rows, columns):
    row_blocks, column_blocks = rows // BLK, columns // BLK
    pick = iota((rows, 128), 0) // BLK + number * column_blocks + e * row_blocks
    pick = (pick == iota((rows, 128), 1)).astype(BF16)
    mask = jnp.zeros((rows, columns), F32)
    for core in range(2):
        row = iota((TAIL, columns), 0)
        near = (row < row_blocks) & (iota((TAIL, columns), 1) // BLK == row + core * row_blocks)
        chosen = lax.dot_general(
            pick, tails[core][:, :128], (((1,), (1,)), ((), ())), preferred_element_type=F32
        )
        mask += dot(chosen.astype(BF16), near.astype(BF16))
    return mask


def square_kernel(count, take, panel, out):
    z, q, e = place()
    rows, columns = out.shape
    tails = in_order(take("tail", 0, TAIL), take("tail", 1, TAIL), e)
    mask = turned_mask([tails[:TAIL], tails[TAIL:]], FIRST + TERMS - 1, e, rows, columns)
    total = jnp.zeros((rows, columns), F32)
    for s in range(count):
        right = in_order(take("near", s, rows), take("far", s, rows), e)
        total += dot(panel[:, chunk(q ^ s, columns)], right)
    out[...] = (total * mask).astype(BF16)


def evolve_kernel(count, take, out, right):
    z, q, e = place()
    rows, columns = out.shape
    for s in range(count):
        right[q ^ s] = in_order(take("plane_near", s, rows), take("plane_far", s, rows), e)
    mask = block_mask(take("tail", 0, TAIL), FIRST + TERMS, rows, columns)
    total = jnp.zeros((columns, columns), F32)
    for s in range(count):
        total += dot(
            in_order(take("line_near", s, rows), take("line_far", s, rows), e), right[z ^ s]
        )
    total = total.T
    chosen = jnp.where(e == 0, total[:rows], total[rows:])
    out[...] = (chosen * mask).astype(BF16)


def on_device(
    mesh_rows,
    mesh_cols,
    fock_matrix,
    density,
    margin,
    fill_patterns,
    first_filters,
    owner_order,
    second_filters,
):
    moves = Moves(mesh_rows, mesh_cols)
    count = mesh_cols
    half = count // 2
    rows, columns = fock_matrix.shape
    size = rows * mesh_rows
    block = jax.ShapeDtypeStruct((rows, columns), BF16)
    barrier = lax.optimization_barrier

    def whole(values):
        return [(value, 0) for value in values]

    masked_density = call(density_kernel, block, [INVMEM] * 2, [], "density")(
        density, fill_patterns
    )
    later, second_filters = barrier((masked_density, second_filters))
    duo, trio = call(
        pair_kernel,
        [
            jax.ShapeDtypeStruct((2 * rows, columns), BF16),
            jax.ShapeDtypeStruct((TAIL + 3 * rows, columns), BF16),
        ],
        [INVMEM] * 6,
        [],
        "pair",
        10**10,
    )(fock_matrix, margin, later, fill_patterns, first_filters, second_filters)

    trio = moves.relabel(trio)
    fock_rows = moves.plane(duo, True)
    density_line = moves.line(masked_density, True, gate=trio)
    density_near = [(trio, TAIL + 2 * rows)] + whole(density_line)
    pair = trio[: TAIL + 2 * rows]
    pair_second, *_ = barrier((pair, *density_line))
    pair_line = moves.line(pair, second=pair_second)
    early = (*density_line, *fock_rows, pair_line[half - 1])
    *density_line, pair_line[half - 1] = [
        value for n, value in enumerate(barrier(early)) if n < count - 1 or n == len(early) - 1
    ]
    trio_far = moves.core(trio)
    density_far = [(trio_far, TAIL + 2 * rows)] + moves.cores(density_line)

    products = views_call(
        functools.partial(first_kernel, count),
        {
            "plane": [(trio, TAIL)] + whole(fock_rows),
            "tail": [(trio, 0)],
            "near": density_near,
            "far": density_far,
        },
        jax.ShapeDtypeStruct((2 * rows, columns), BF16),
        [pltpu.VMEM((count, 2 * rows, columns), BF16)],
        "first",
        10**10,
    )
    product_rows = [products] + moves.plane(products)
    pair_line = list(barrier((*pair_line, *product_rows[1:]))[: count - 1])
    pair_far = [(trio_far, 0)] + moves.cores(pair_line[:half]) + moves.cores(pair_line[half:])
    pair_near = [(trio, 0)] + whole(pair_line)

    generator = views_call(
        functools.partial(generator_kernel, count),
        {
            "plane": whole(product_rows),
            "tail": [(trio, 0)],
            "near": [(value, first + TAIL) for value, first in pair_near],
            "far": [(value, first + TAIL) for value, first in pair_far],
        },
        block,
        [pltpu.VMEM((2, count, rows, columns), BF16)],
        "generator",
    )

    lines = [generator] + moves.line(generator)
    arrays, layout, planes, done = [], [], [], []
    for held in (range(1), range(1, half + 1), range(half + 1, count)):
        group = lines[held[0]]
        if len(held) > 1:
            group = jnp.concatenate([lines[k] for k in held], axis=0)
        if held[0] == 1:
            group, *planes = barrier((group, *planes))
        planes = [group] + moves.plane(group)
        done.append((held, planes))
    done[1] = (done[1][0], list(barrier((*done[1][1], *done[2][1][1:]))[:count]))
    for held, planes in done:
        far = moves.cores(planes)
        for s, value in enumerate(planes):
            for lane, (array, start) in enumerate(((value, 0), far[s])):
                if not any(other is array for other in arrays):
                    arrays.append(array)
                index = [n for n, other in enumerate(arrays) if other is array][0]
                for n, k in enumerate(held):
                    layout.append((index, start + n * rows, k, s, lane))
    tails = [value[first : first + TAIL] for value, first in pair_near + pair_far]

    panel, mine = call(
        functools.partial(series_kernel, layout, count, len(arrays)),
        [jax.ShapeDtypeStruct((rows, size), BF16), block],
        [ANY] * len(arrays) + [INVMEM] * (2 * count) + [INSMEM],
        [
            pltpu.VMEM((size, size), BF16),
            pltpu.VMEM((size, size), BF16),
            pltpu.VMEM((mesh_rows, TAIL, columns), BF16),
            pltpu.VMEM((128, size), F32),
            pltpu.SemaphoreType.DMA((len(layout),)),
        ],
        "series",
        room=16 + 4 * size * size // MEGABYTE,
    )(*arrays, *tails, owner_order)

    near = [mine] + moves.plane(mine)
    square = views_call(
        functools.partial(square_kernel, count),
        {"near": whole(near), "far": moves.cores(near), "tail": [(trio, 0), (trio_far, 0)]},
        block,
        [],
        "square",
        extra=[panel],
    )

    line = moves.line(square)
    plane_near = [square] + moves.plane(square)
    plane_far = moves.cores(plane_near)
    evolved = views_call(
        functools.partial(evolve_kernel, count),
        {
            "plane_near": whole(plane_near),
            "plane_far": plane_far,
            "line_near": whole([square] + line),
            "line_far": plane_far[:1] + moves.cores(line),
            "tail": [(trio, 0)],
        },
        block,
        [pltpu.VMEM((count, columns, columns), BF16)],
        "evolve",
    )
    return moves.relabel(evolved)


def solution(mesh):
    return jax.shard_map(
        functools.partial(on_device, mesh.shape["row"], mesh.shape["col"]),
        mesh=mesh,
        in_specs=(
            P("row", "col"),
            P("row", "col"),
            P("row", "col"),
            P(None, "row", "col"),
            P(None, "row", "col"),
            P(),
            P(None, "row", "col"),
        ),
        out_specs=P("row", "col"),
        check_vma=False,
    )
```

```python
import functools

import jax
import jax.numpy as jnp
from jax import lax
from jax.experimental import pallas as pl
from jax.experimental.pallas import tpu as pltpu
from jax.sharding import PartitionSpec as P

BLK = 32
TERMS = 6
SQUARINGS = 2
FIRST = 3
AXES = ("row", "col")
F32 = jnp.float32
BF16 = jnp.bfloat16
TAIL = 16
MEGABYTE = 1024 * 1024


def coordinates(r, c):
    return r // 2, r % 2, c // 2, c % 2


def permutation(rows, cols, source):
    pairs = []
    for r in range(rows):
        for c in range(cols):
            sr, sc = source(*coordinates(r, c))
            pairs.append((sr * cols + sc, r * cols + c))
    return pairs


class Moves:
    def __init__(self, rows, cols):
        self.rows, self.cols = rows, cols

    def move(self, value, source):
        return lax.ppermute(value, AXES, permutation(self.rows, self.cols, source))

    def relabel(self, value, k=0):
        return self.move(value, lambda z, y, x, e: (2 * (z ^ k) + e, 2 * x + y))

    def along_z(self, value, k):
        return self.move(value, lambda z, y, x, e: (2 * (z ^ k) + y, 2 * x + e))

    def line(self, value, relabel=False, second=None, gate=None):
        bits = [1 << b for b in range((self.rows // 2).bit_length() - 1)]
        held = {0: value}
        for bit in reversed(bits):
            for k, part in list(held.items()):
                if k == 0 and relabel:
                    held[bit] = self.relabel(value, bit)
                else:
                    if k and gate is not None:
                        part, _ = lax.optimization_barrier((part, gate))
                    held[k | bit] = self.along_z(part, bit)
            if second is not None:
                held[0] = second
        return [held[k] for k in range(1, self.rows // 2)]

    def in_plane(self, value, s):
        return self.move(value, lambda z, y, x, e: (2 * z + (y ^ (s & 1)), 2 * (x ^ (s >> 1)) + e))

    def plane(self, value, relabel=False):
        if relabel:
            return [
                self.move(value, lambda z, y, x, e: (2 * z + e, 2 * (x ^ (s >> 1)) + (y ^ (s & 1))))
                for s in range(1, self.cols)
            ]
        return [self.in_plane(value, s) for s in range(1, self.cols)]

    def core(self, value):
        return self.move(value, lambda z, y, x, e: (2 * z + y, 2 * x + 1 - e))

    def cores(self, values):
        length = values[0].shape[0]
        far = self.core(jnp.concatenate(values, axis=0) if len(values) > 1 else values[0])
        return [(far, n * length) for n in range(len(values))]


def place():
    r, c = lax.axis_index("row"), lax.axis_index("col")
    z, y, x, e = r // 2, r % 2, c // 2, c % 2
    return z, 2 * x + y, e


def iota(shape, axis):
    return lax.broadcasted_iota(jnp.int32, shape, axis)


def dot(a, b):
    return jnp.dot(a, b, preferred_element_type=F32)


def repeat_rows(rows, blocks):
    return (iota((rows, blocks), 0) // BLK == iota((rows, blocks), 1)).astype(BF16)


def repeat_columns(blocks, columns, first=0):
    return (iota((blocks, columns), 0) == iota((blocks, columns), 1) // BLK + first).astype(BF16)


def block_mask(tail, number, rows, columns):
    blocks = columns // BLK
    wide = dot(repeat_rows(rows, tail.shape[0]), tail).astype(BF16)
    return dot(wide, repeat_columns(tail.shape[1], columns, number * blocks))


def call(kernel, outs, ins, scratch, name, flops=1000, room=16):
    return pl.pallas_call(
        kernel,
        out_shape=outs,
        in_specs=ins,
        out_specs=jax.tree.map(lambda _: pl.BlockSpec(memory_space=pltpu.VMEM), outs),
        scratch_shapes=scratch,
        name=name,
        compiler_params=pltpu.CompilerParams(vmem_limit_bytes=room * MEGABYTE),
        cost_estimate=pl.CostEstimate(flops=flops, bytes_accessed=1000, transcendentals=0),
    )


def views_call(kernel, views, outs, scratch, name, flops=1000, extra=()):
    arrays, spec = [], {}
    for key, items in views.items():
        spec[key] = []
        for value, first in items:
            known = [n for n, other in enumerate(arrays) if other is value]
            if not known:
                arrays.append(value)
            spec[key].append((known[0] if known else len(arrays) - 1, first))

    def body(*refs):
        def take(key, n, length, shift=0):
            index, first = spec[key][n]
            return refs[index][first + shift : first + shift + length, :]

        kernel(take, *refs[len(arrays) :])

    operands = [*arrays, *extra]
    return call(body, outs, [INVMEM] * len(operands), scratch, name, flops)(*operands)


ANY = pl.BlockSpec(memory_space=pl.ANY)
INVMEM = pl.BlockSpec(memory_space=pltpu.VMEM)
INSMEM = pl.BlockSpec(memory_space=pltpu.SMEM)


def mask_kernel(inputs, *refs):
    sources, (tailed, duo) = refs[:inputs], refs[inputs : inputs + 2]
    held, sems = refs[inputs + 2 : -1], refs[-1]
    copies = [
        pltpu.make_async_copy(source, target, sems.at[n])
        for n, (source, target) in enumerate(zip(sources, held))
    ]
    fills, density, fock, margin, firsts, seconds = held
    rows, columns = density.shape
    row_blocks, column_blocks = rows // BLK, columns // BLK
    start_all(copies)
    tall = repeat_rows(rows, row_blocks)
    wide = repeat_columns(column_blocks, columns)

    def masked(ref, number):
        mask = dot(dot(tall, fills[number].astype(BF16)).astype(BF16), wide)
        return (ref[...].astype(F32) * mask).astype(BF16)

    wait_all(copies[:2])
    tailed[TAIL:, :] = masked(density, 1)
    wait_all(copies[2:])
    duo[:rows, :] = masked(fock, 0)
    duo[rows:, :] = masked(margin, 2)
    top = (iota((TAIL, row_blocks), 0) == iota((TAIL, row_blocks), 1)).astype(BF16)
    tail = jnp.zeros((TAIL, columns), F32)
    for number in range(FIRST + seconds.shape[1]):
        block = firsts[number] if number < FIRST else seconds[:, number - FIRST, :]
        column = iota((column_blocks, columns), 1) - number * column_blocks
        spread = (iota((column_blocks, columns), 0) == column).astype(BF16)
        tail += dot(dot(top, block.astype(BF16)).astype(BF16), spread)
    tailed[:TAIL, :] = tail.astype(BF16)


def chunk(index, length):
    return pl.ds(pl.multiple_of(index * length, length), length)


def start_all(copies):
    for one in copies:
        one.start()


def wait_all(copies):
    for one in copies:
        one.wait()


def repeat(times, body, unrolled):
    if unrolled:
        for t in range(times):
            body(t)
    else:

        def step(t, carry):
            body(t)
            return carry

        lax.fori_loop(0, times, step, 0)


def in_order(near, far, e):
    low = jnp.where(e == 0, near, far)
    high = jnp.where(e == 0, far, near)
    return jnp.concatenate([low, high], axis=0)


def first_kernel(count, take, out, left):
    z, q, e = place()
    rows, columns = out.shape[0] // 2, out.shape[1]
    for s in range(count):
        left[q ^ s] = take("plane", s, 2 * rows)
    tail = take("tail", 0, TAIL)
    masks = [block_mask(tail, n, rows, columns) for n in range(2)]
    total = jnp.zeros((2 * rows, columns), F32)
    for s in range(count):
        total += dot(left[z ^ s], in_order(take("near", s, rows), take("far", s, rows), e))
    for n in range(2):
        part = slice(n * rows, (n + 1) * rows)
        out[part, :] = (total[part] * masks[n]).astype(BF16)


def generator_kernel(count, take, out, left):
    z, q, e = place()
    rows, columns = out.shape
    for s in range(count):
        for half in range(2):
            left[half, q ^ s] = take("plane", s, rows, half * rows)
    mask = block_mask(take("tail", 0, TAIL), 2, rows, columns)
    total = jnp.zeros((rows, columns), F32)
    for half in range(2):
        shift = (1 - half) * rows
        for s in range(count):
            right = in_order(take("near", s, rows, shift), take("far", s, rows, shift), e)
            product = dot(left[half, z ^ s], right)
            total = total + product if half == 0 else total - product
    generator = (total * mask).astype(BF16)
    out[...] = (generator.astype(F32) * 0.25).astype(BF16)


def series_kernel(layout, count, pieces, *refs):
    arrays, tails, order = refs[:pieces], refs[pieces : pieces + 2 * count], refs[pieces + 2 * count]
    panel, mine, whole, turned, wides, spread, sems = refs[pieces + 2 * count + 1 :]
    z, q, e = place()
    rows, columns = mine.shape
    size = panel.shape[1]
    row_blocks, column_blocks, blocks = rows // BLK, columns // BLK, size // BLK
    small = size <= 1536
    copies = []
    for index, first, k, plane, lane in layout:
        core = e if lane == 0 else 1 - e
        copies.append(
            pltpu.make_async_copy(
                arrays[index].at[pl.ds(first, rows)],
                whole.at[chunk(2 * (z ^ k) + core, rows), chunk(q ^ plane, columns)],
                sems.at[len(copies)],
            )
        )
    start_all(copies)
    for index, ref in enumerate(tails):
        core = e if index < count else 1 - e
        wides[2 * (z ^ (index % count)) + core] = ref[...]
    filters = jnp.zeros((128, size), F32)
    for p in range(2 * count):
        column = iota((TAIL, size), 1) // BLK
        row = iota((TAIL, size), 0)
        near = ((row < row_blocks) & (column == row + p * row_blocks)).astype(BF16)
        filters += lax.dot_general(
            wides[p][:, :128], near, (((0,), (0,)), ((), ())), preferred_element_type=F32
        )
    spread[...] = filters

    wait_all(copies)

    def turn(t):
        tile = jnp.concatenate(
            [whole[chunk(order[t * column_blocks + a], BLK), :] for a in range(column_blocks)],
            axis=0,
        )
        turned[:, chunk(t, columns)] = tile.T

    def place_rows(b):
        whole[chunk(b, BLK), :] = turned[chunk(order[b], BLK), :]

    repeat(count, turn, small)
    repeat(blocks, place_rows, small)

    first = (2 * q + e) * rows
    unit = (iota((rows, size), 1) == iota((rows, size), 0) + first).astype(F32)
    own = unit + whole[chunk(2 * q + e, rows), :].astype(F32) / TERMS
    panel[...] = own.astype(BF16)
    width = size if small else 512
    for number in range(1, TERMS):
        current = panel[...]
        base = (FIRST + number - 1) * column_blocks + e * row_blocks

        def advance(t):
            part = chunk(t, width)
            product = dot(current, whole[:, part])
            mask = jnp.concatenate(
                [
                    jnp.broadcast_to(spread[pl.ds(base + b, 1), part], (BLK, width))
                    for b in range(row_blocks)
                ],
                axis=0,
            )
            here = iota((rows, width), 1) + t * width == iota((rows, width), 0) + first
            panel[:, part] = (here.astype(F32) + product * mask / (TERMS - number)).astype(BF16)

        repeat(size // width, advance, small)
    mine[...] = panel[:, chunk(z, columns)]


def turned_mask(tails, number, e, rows, columns):
    row_blocks, column_blocks = rows // BLK, columns // BLK
    pick = iota((rows, 128), 0) // BLK + number * column_blocks + e * row_blocks
    pick = (pick == iota((rows, 128), 1)).astype(BF16)
    mask = jnp.zeros((rows, columns), F32)
    for core in range(2):
        row = iota((TAIL, columns), 0)
        near = (row < row_blocks) & (iota((TAIL, columns), 1) // BLK == row + core * row_blocks)
        chosen = lax.dot_general(
            pick, tails[core][:, :128], (((1,), (1,)), ((), ())), preferred_element_type=F32
        )
        mask += dot(chosen.astype(BF16), near.astype(BF16))
    return mask


def square_kernel(count, take, panel, out):
    z, q, e = place()
    rows, columns = out.shape
    tails = in_order(take("tail", 0, TAIL), take("tail", 1, TAIL), e)
    mask = turned_mask([tails[:TAIL], tails[TAIL:]], FIRST + TERMS - 1, e, rows, columns)
    total = jnp.zeros((rows, columns), F32)
    for s in range(count):
        right = in_order(take("near", s, rows), take("far", s, rows), e)
        total += dot(panel[:, chunk(q ^ s, columns)], right)
    out[...] = (total * mask).astype(BF16)


def evolve_kernel(count, take, out, right):
    z, q, e = place()
    rows, columns = out.shape
    for s in range(count):
        right[q ^ s] = in_order(take("plane_near", s, rows), take("plane_far", s, rows), e)
    mask = block_mask(take("tail", 0, TAIL), FIRST + TERMS, rows, columns)
    total = jnp.zeros((columns, columns), F32)
    for s in range(count):
        total += dot(
            in_order(take("line_near", s, rows), take("line_far", s, rows), e), right[z ^ s]
        )
    total = total.T
    chosen = jnp.where(e == 0, total[:rows], total[rows:])
    out[...] = (chosen * mask).astype(BF16)


def on_device(
    mesh_rows,
    mesh_cols,
    fock_matrix,
    density,
    margin,
    fill_patterns,
    first_filters,
    owner_order,
    second_filters,
):
    moves = Moves(mesh_rows, mesh_cols)
    count = mesh_cols
    half = count // 2
    rows, columns = fock_matrix.shape
    size = rows * mesh_rows
    block = jax.ShapeDtypeStruct((rows, columns), BF16)
    barrier = lax.optimization_barrier

    def whole(values):
        return [(value, 0) for value in values]

    inputs = (
        fill_patterns,
        density,
        fock_matrix,
        margin,
        first_filters,
        second_filters.transpose(1, 0, 2),
    )
    tailed, duo = call(
        functools.partial(mask_kernel, len(inputs)),
        [
            jax.ShapeDtypeStruct((TAIL + rows, columns), BF16),
            jax.ShapeDtypeStruct((2 * rows, columns), BF16),
        ],
        [pl.BlockSpec(memory_space=pltpu.HBM)] * len(inputs),
        [pltpu.VMEM(value.shape, value.dtype) for value in inputs]
        + [pltpu.SemaphoreType.DMA((len(inputs),))],
        "mask",
    )(*inputs)

    pair = moves.relabel(duo)
    fock_rows = moves.plane(duo, True)
    density_line = [moves.relabel(tailed)] + moves.line(tailed, True)
    pair_second, *_ = barrier((pair, *density_line))
    pair_line = moves.line(pair, second=pair_second)
    ready = list(barrier((*density_line, *fock_rows, pair))[:count])
    density_far = moves.cores(ready)
    density_near = whole(density_line)
    other = moves.core(pair)

    products = views_call(
        functools.partial(first_kernel, count),
        {
            "plane": whole([pair] + fock_rows),
            "tail": density_near,
            "near": [(value, first + TAIL) for value, first in density_near],
            "far": [(value, first + TAIL) for value, first in density_far],
        },
        jax.ShapeDtypeStruct((2 * rows, columns), BF16),
        [pltpu.VMEM((count, 2 * rows, columns), BF16)],
        "first",
        10**10,
    )
    product_rows = [products] + moves.plane(products)
    pair_line = list(barrier((*pair_line, *product_rows[1:]))[: count - 1])
    pair_far = [(other, 0)] + moves.cores(pair_line[:half]) + moves.cores(pair_line[half:])
    pair_near = whole([pair] + pair_line)

    generator = views_call(
        functools.partial(generator_kernel, count),
        {
            "plane": whole(product_rows),
            "tail": density_near,
            "near": pair_near,
            "far": pair_far,
        },
        block,
        [pltpu.VMEM((2, count, rows, columns), BF16)],
        "generator",
    )

    lines = [generator] + moves.line(generator)
    arrays, layout, done, own_far = [], [], [], []
    for held in (range(1), range(1, half + 1), range(half + 1, count)):
        group = lines[held[0]]
        if len(held) > 1:
            group = jnp.concatenate([lines[k] for k in held], axis=0)
        if held[0] == 1:
            group, *_ = barrier((group, *done[0][1]))
        if held[0] > 1:
            group, _ = barrier((group, own_far[0][0]))
        planes = [group] + moves.plane(group)
        if held[0] == 0:
            own_far = moves.cores(planes)
        done.append((held, planes))
    done[1] = (done[1][0], list(barrier((*done[1][1], *done[2][1][1:]))[:count]))
    for held, planes in done:
        far = own_far if held[0] == 0 else moves.cores(planes)
        for s, value in enumerate(planes):
            for lane, (array, start) in enumerate(((value, 0), far[s])):
                if not any(other is array for other in arrays):
                    arrays.append(array)
                index = [n for n, other in enumerate(arrays) if other is array][0]
                for n, k in enumerate(held):
                    layout.append((index, start + n * rows, k, s, lane))
    tails = [value[first : first + TAIL] for value, first in density_near + density_far]

    panel, mine = call(
        functools.partial(series_kernel, layout, count, len(arrays)),
        [jax.ShapeDtypeStruct((rows, size), BF16), block],
        [ANY] * len(arrays) + [INVMEM] * (2 * count) + [INSMEM],
        [
            pltpu.VMEM((size, size), BF16),
            pltpu.VMEM((size, size), BF16),
            pltpu.VMEM((mesh_rows, TAIL, columns), BF16),
            pltpu.VMEM((128, size), F32),
            pltpu.SemaphoreType.DMA((len(layout),)),
        ],
        "series",
        room=16 + 4 * size * size // MEGABYTE,
    )(*arrays, *tails, owner_order)

    near = [mine] + moves.plane(mine)
    square = views_call(
        functools.partial(square_kernel, count),
        {"near": whole(near), "far": moves.cores(near), "tail": [density_near[0], density_far[0]]},
        block,
        [],
        "square",
        extra=[panel],
    )

    line = moves.line(square)
    plane_near = [square] + moves.plane(square)
    plane_far = moves.cores(plane_near)
    evolved = views_call(
        functools.partial(evolve_kernel, count),
        {
            "plane_near": whole(plane_near),
            "plane_far": plane_far,
            "line_near": whole([square] + line),
            "line_far": plane_far[:1] + moves.cores(line),
            "tail": density_near,
        },
        block,
        [pltpu.VMEM((count, columns, columns), BF16)],
        "evolve",
    )
    return moves.relabel(evolved)


def solution(mesh):
    return jax.shard_map(
        functools.partial(on_device, mesh.shape["row"], mesh.shape["col"]),
        mesh=mesh,
        in_specs=(
            P("row", "col"),
            P("row", "col"),
            P("row", "col"),
            P(None, "row", "col"),
            P(None, "row", "col"),
            P(),
            P(None, "row", "col"),
        ),
        out_specs=P("row", "col"),
        check_vma=False,
    )
```

```python
import functools

import jax
import jax.numpy as jnp
from jax import lax
from jax.experimental import pallas as pl
from jax.experimental.pallas import tpu as pltpu
from jax.sharding import PartitionSpec as P

BLK = 32
TERMS = 6
SQUARINGS = 2
FIRST = 3
AXES = ("row", "col")
F32 = jnp.float32
BF16 = jnp.bfloat16
TAIL = 16
MEGABYTE = 1024 * 1024


def coordinates(r, c):
    return r // 2, r % 2, c // 2, c % 2


def permutation(rows, cols, source):
    pairs = []
    for r in range(rows):
        for c in range(cols):
            sr, sc = source(*coordinates(r, c))
            pairs.append((sr * cols + sc, r * cols + c))
    return pairs


class Moves:
    def __init__(self, rows, cols):
        self.rows, self.cols = rows, cols

    def move(self, value, source):
        return lax.ppermute(value, AXES, permutation(self.rows, self.cols, source))

    def relabel(self, value, k=0):
        return self.move(value, lambda z, y, x, e: (2 * (z ^ k) + e, 2 * x + y))

    def along_z(self, value, k):
        return self.move(value, lambda z, y, x, e: (2 * (z ^ k) + y, 2 * x + e))

    def line(self, value, relabel=False, second=None, gate=None):
        bits = [1 << b for b in range((self.rows // 2).bit_length() - 1)]
        held = {0: value}
        for bit in reversed(bits):
            for k, part in list(held.items()):
                if k == 0 and relabel:
                    held[bit] = self.relabel(value, bit)
                else:
                    if k and gate is not None:
                        part, _ = lax.optimization_barrier((part, gate))
                    held[k | bit] = self.along_z(part, bit)
            if second is not None:
                held[0] = second
        return [held[k] for k in range(1, self.rows // 2)]

    def in_plane(self, value, s):
        return self.move(value, lambda z, y, x, e: (2 * z + (y ^ (s & 1)), 2 * (x ^ (s >> 1)) + e))

    def plane(self, value, relabel=False):
        if relabel:
            return [
                self.move(value, lambda z, y, x, e: (2 * z + e, 2 * (x ^ (s >> 1)) + (y ^ (s & 1))))
                for s in range(1, self.cols)
            ]
        return [self.in_plane(value, s) for s in range(1, self.cols)]

    def core(self, value):
        return self.move(value, lambda z, y, x, e: (2 * z + y, 2 * x + 1 - e))

    def cores(self, values):
        length = values[0].shape[0]
        far = self.core(jnp.concatenate(values, axis=0) if len(values) > 1 else values[0])
        return [(far, n * length) for n in range(len(values))]


def place():
    r, c = lax.axis_index("row"), lax.axis_index("col")
    z, y, x, e = r // 2, r % 2, c // 2, c % 2
    return z, 2 * x + y, e


def iota(shape, axis):
    return lax.broadcasted_iota(jnp.int32, shape, axis)


def dot(a, b):
    return jnp.dot(a, b, preferred_element_type=F32)


def repeat_rows(rows, blocks):
    return (iota((rows, blocks), 0) // BLK == iota((rows, blocks), 1)).astype(BF16)


def repeat_columns(blocks, columns, first=0):
    return (iota((blocks, columns), 0) == iota((blocks, columns), 1) // BLK + first).astype(BF16)


def block_mask(tail, number, rows, columns):
    blocks = columns // BLK
    wide = dot(repeat_rows(rows, tail.shape[0]), tail).astype(BF16)
    return dot(wide, repeat_columns(tail.shape[1], columns, number * blocks))


def call(kernel, outs, ins, scratch, name, flops=1000, room=16):
    return pl.pallas_call(
        kernel,
        out_shape=outs,
        in_specs=ins,
        out_specs=jax.tree.map(lambda _: pl.BlockSpec(memory_space=pltpu.VMEM), outs),
        scratch_shapes=scratch,
        name=name,
        compiler_params=pltpu.CompilerParams(vmem_limit_bytes=room * MEGABYTE),
        cost_estimate=pl.CostEstimate(flops=flops, bytes_accessed=1000, transcendentals=0),
    )


def views_call(kernel, views, outs, scratch, name, flops=1000, extra=()):
    arrays, spec = [], {}
    for key, items in views.items():
        spec[key] = []
        for value, first in items:
            known = [n for n, other in enumerate(arrays) if other is value]
            if not known:
                arrays.append(value)
            spec[key].append((known[0] if known else len(arrays) - 1, first))

    def body(*refs):
        def take(key, n, length, shift=0):
            index, first = spec[key][n]
            return refs[index][first + shift : first + shift + length, :]

        kernel(take, *refs[len(arrays) :])

    operands = [*arrays, *extra]
    return call(body, outs, [INVMEM] * len(operands), scratch, name, flops)(*operands)


ANY = pl.BlockSpec(memory_space=pl.ANY)
INVMEM = pl.BlockSpec(memory_space=pltpu.VMEM)
INSMEM = pl.BlockSpec(memory_space=pltpu.SMEM)


def mask_kernel(inputs, *refs):
    sources, (masked_density, duo, trio) = refs[:inputs], refs[inputs : inputs + 3]
    held, sems = refs[inputs + 3 : -1], refs[-1]
    copies = [
        pltpu.make_async_copy(source, target, sems.at[n])
        for n, (source, target) in enumerate(zip(sources, held))
    ]
    fills, density, fock, margin, firsts, seconds = held
    rows, columns = density.shape
    row_blocks, column_blocks = rows // BLK, columns // BLK
    start_all(copies)
    tall = repeat_rows(rows, row_blocks)
    wide = repeat_columns(column_blocks, columns)

    def masked(ref, number):
        mask = dot(dot(tall, fills[number].astype(BF16)).astype(BF16), wide)
        return (ref[...].astype(F32) * mask).astype(BF16)

    wait_all(copies)
    value = masked(density, 1)
    masked_density[...] = value
    trio[TAIL + 2 * rows :, :] = value
    for half, (ref, number) in enumerate(((fock, 0), (margin, 2))):
        value = masked(ref, number)
        duo[half * rows : (half + 1) * rows, :] = value
        trio[TAIL + half * rows : TAIL + (half + 1) * rows, :] = value
    top = (iota((TAIL, row_blocks), 0) == iota((TAIL, row_blocks), 1)).astype(BF16)
    tail = jnp.zeros((TAIL, columns), F32)
    for number in range(FIRST + seconds.shape[1]):
        block = firsts[number] if number < FIRST else seconds[:, number - FIRST, :]
        column = iota((column_blocks, columns), 1) - number * column_blocks
        spread = (iota((column_blocks, columns), 0) == column).astype(BF16)
        tail += dot(dot(top, block.astype(BF16)).astype(BF16), spread)
    trio[:TAIL, :] = tail.astype(BF16)


def chunk(index, length):
    return pl.ds(pl.multiple_of(index * length, length), length)


def start_all(copies):
    for one in copies:
        one.start()


def wait_all(copies):
    for one in copies:
        one.wait()


def repeat(times, body, unrolled):
    if unrolled:
        for t in range(times):
            body(t)
    else:

        def step(t, carry):
            body(t)
            return carry

        lax.fori_loop(0, times, step, 0)


def in_order(near, far, e):
    low = jnp.where(e == 0, near, far)
    high = jnp.where(e == 0, far, near)
    return jnp.concatenate([low, high], axis=0)


def first_kernel(count, take, out, left):
    z, q, e = place()
    rows, columns = out.shape[0] // 2, out.shape[1]
    for s in range(count):
        left[q ^ s] = take("plane", s, 2 * rows)
    tail = take("tail", 0, TAIL)
    masks = [block_mask(tail, n, rows, columns) for n in range(2)]
    total = jnp.zeros((2 * rows, columns), F32)
    for s in range(count):
        total += dot(left[z ^ s], in_order(take("near", s, rows), take("far", s, rows), e))
    for n in range(2):
        part = slice(n * rows, (n + 1) * rows)
        out[part, :] = (total[part] * masks[n]).astype(BF16)


def generator_kernel(count, take, out, left):
    z, q, e = place()
    rows, columns = out.shape
    for s in range(count):
        for half in range(2):
            left[half, q ^ s] = take("plane", s, rows, half * rows)
    mask = block_mask(take("tail", 0, TAIL), 2, rows, columns)
    total = jnp.zeros((rows, columns), F32)
    for half in range(2):
        shift = (1 - half) * rows
        for s in range(count):
            right = in_order(take("near", s, rows, shift), take("far", s, rows, shift), e)
            product = dot(left[half, z ^ s], right)
            total = total + product if half == 0 else total - product
    generator = (total * mask).astype(BF16)
    out[...] = (generator.astype(F32) * 0.25).astype(BF16)


def series_kernel(layout, count, pieces, *refs):
    arrays, tails, order = refs[:pieces], refs[pieces : pieces + 2 * count], refs[pieces + 2 * count]
    panel, mine, whole, turned, wides, spread, sems = refs[pieces + 2 * count + 1 :]
    z, q, e = place()
    rows, columns = mine.shape
    size = panel.shape[1]
    row_blocks, column_blocks, blocks = rows // BLK, columns // BLK, size // BLK
    small = size <= 1536
    copies = []
    for index, first, k, plane, lane in layout:
        core = e if lane == 0 else 1 - e
        copies.append(
            pltpu.make_async_copy(
                arrays[index].at[pl.ds(first, rows)],
                whole.at[chunk(2 * (z ^ k) + core, rows), chunk(q ^ plane, columns)],
                sems.at[len(copies)],
            )
        )
    start_all(copies)
    for index, ref in enumerate(tails):
        core = e if index < count else 1 - e
        wides[2 * (z ^ (index % count)) + core] = ref[...]
    filters = jnp.zeros((128, size), F32)
    for p in range(2 * count):
        column = iota((TAIL, size), 1) // BLK
        row = iota((TAIL, size), 0)
        near = ((row < row_blocks) & (column == row + p * row_blocks)).astype(BF16)
        filters += lax.dot_general(
            wides[p][:, :128], near, (((0,), (0,)), ((), ())), preferred_element_type=F32
        )
    spread[...] = filters

    wait_all(copies)

    def turn(t):
        tile = jnp.concatenate(
            [whole[chunk(order[t * column_blocks + a], BLK), :] for a in range(column_blocks)],
            axis=0,
        )
        turned[:, chunk(t, columns)] = tile.T

    def place_rows(b):
        whole[chunk(b, BLK), :] = turned[chunk(order[b], BLK), :]

    repeat(count, turn, small)
    repeat(blocks, place_rows, small)

    first = (2 * q + e) * rows
    unit = (iota((rows, size), 1) == iota((rows, size), 0) + first).astype(F32)
    own = unit + whole[chunk(2 * q + e, rows), :].astype(F32) / TERMS
    panel[...] = own.astype(BF16)
    width = size if small else 512
    for number in range(1, TERMS):
        current = panel[...]
        base = (FIRST + number - 1) * column_blocks + e * row_blocks

        def advance(t):
            part = chunk(t, width)
            product = dot(current, whole[:, part])
            mask = jnp.concatenate(
                [
                    jnp.broadcast_to(spread[pl.ds(base + b, 1), part], (BLK, width))
                    for b in range(row_blocks)
                ],
                axis=0,
            )
            here = iota((rows, width), 1) + t * width == iota((rows, width), 0) + first
            panel[:, part] = (here.astype(F32) + product * mask / (TERMS - number)).astype(BF16)

        repeat(size // width, advance, small)
    mine[...] = panel[:, chunk(z, columns)]


def turned_mask(tails, number, e, rows, columns):
    row_blocks, column_blocks = rows // BLK, columns // BLK
    pick = iota((rows, 128), 0) // BLK + number * column_blocks + e * row_blocks
    pick = (pick == iota((rows, 128), 1)).astype(BF16)
    mask = jnp.zeros((rows, columns), F32)
    for core in range(2):
        row = iota((TAIL, columns), 0)
        near = (row < row_blocks) & (iota((TAIL, columns), 1) // BLK == row + core * row_blocks)
        chosen = lax.dot_general(
            pick, tails[core][:, :128], (((1,), (1,)), ((), ())), preferred_element_type=F32
        )
        mask += dot(chosen.astype(BF16), near.astype(BF16))
    return mask


def square_kernel(count, take, panel, out):
    z, q, e = place()
    rows, columns = out.shape
    tails = in_order(take("tail", 0, TAIL), take("tail", 1, TAIL), e)
    mask = turned_mask([tails[:TAIL], tails[TAIL:]], FIRST + TERMS - 1, e, rows, columns)
    total = jnp.zeros((rows, columns), F32)
    for s in range(count):
        right = in_order(take("near", s, rows), take("far", s, rows), e)
        total += dot(panel[:, chunk(q ^ s, columns)], right)
    out[...] = (total * mask).astype(BF16)


def evolve_kernel(count, take, out, right):
    z, q, e = place()
    rows, columns = out.shape
    for s in range(count):
        right[q ^ s] = in_order(take("plane_near", s, rows), take("plane_far", s, rows), e)
    mask = block_mask(take("tail", 0, TAIL), FIRST + TERMS, rows, columns)
    total = jnp.zeros((columns, columns), F32)
    for s in range(count):
        total += dot(
            in_order(take("line_near", s, rows), take("line_far", s, rows), e), right[z ^ s]
        )
    total = total.T
    chosen = jnp.where(e == 0, total[:rows], total[rows:])
    out[...] = (chosen * mask).astype(BF16)


def on_device(
    mesh_rows,
    mesh_cols,
    fock_matrix,
    density,
    margin,
    fill_patterns,
    first_filters,
    owner_order,
    second_filters,
):
    moves = Moves(mesh_rows, mesh_cols)
    count = mesh_cols
    half = count // 2
    rows, columns = fock_matrix.shape
    size = rows * mesh_rows
    block = jax.ShapeDtypeStruct((rows, columns), BF16)
    barrier = lax.optimization_barrier

    def whole(values):
        return [(value, 0) for value in values]

    inputs = (
        fill_patterns,
        density,
        fock_matrix,
        margin,
        first_filters,
        second_filters.transpose(1, 0, 2),
    )
    masked_density, duo, trio = call(
        functools.partial(mask_kernel, len(inputs)),
        [
            block,
            jax.ShapeDtypeStruct((2 * rows, columns), BF16),
            jax.ShapeDtypeStruct((TAIL + 3 * rows, columns), BF16),
        ],
        [ANY] * len(inputs),
        [pltpu.VMEM(value.shape, value.dtype) for value in inputs]
        + [pltpu.SemaphoreType.DMA((len(inputs),))],
        "mask",
        room=60,
    )(*inputs)

    trio = moves.relabel(trio)
    fock_rows = moves.plane(duo, True)
    density_line = moves.line(masked_density, True, gate=(trio, *fock_rows))
    density_near = [(trio, TAIL + 2 * rows)] + whole(density_line)
    pair = trio[: TAIL + 2 * rows]
    pair_second, *_ = barrier((pair, *density_line))
    pair_line = moves.line(pair, second=pair_second)
    density_line = list(barrier((*density_line, *fock_rows))[: count - 1])
    trio_far = moves.core(trio)
    density_far = [(trio_far, TAIL + 2 * rows)] + moves.cores(density_line)
    early_far = moves.cores(pair_line[half - 1 : half])
    trio, early, _ = barrier((trio, early_far[0][0], pair_line[half - 1]))
    early_far = [(early, 0)]

    products = views_call(
        functools.partial(first_kernel, count),
        {
            "plane": [(trio, TAIL)] + whole(fock_rows),
            "tail": [(trio, 0)],
            "near": density_near,
            "far": density_far,
        },
        jax.ShapeDtypeStruct((2 * rows, columns), BF16),
        [pltpu.VMEM((count, 2 * rows, columns), BF16)],
        "first",
        10**10,
    )
    product_rows = [products] + moves.plane(products)
    pair_line = list(barrier((*pair_line, *product_rows[1:]))[: count - 1])
    rest = pair_line[: half - 1] + pair_line[half:]
    rest_far = moves.cores(rest)
    pair_far = [(trio_far, 0)] + rest_far[: half - 1] + early_far + rest_far[half - 1 :]
    pair_near = [(trio, 0)] + whole(pair_line)

    generator = views_call(
        functools.partial(generator_kernel, count),
        {
            "plane": whole(product_rows),
            "tail": [(trio, 0)],
            "near": [(value, first + TAIL) for value, first in pair_near],
            "far": [(value, first + TAIL) for value, first in pair_far],
        },
        block,
        [pltpu.VMEM((2, count, rows, columns), BF16)],
        "generator",
    )

    lines = [generator] + moves.line(generator)
    arrays, layout, planes, done = [], [], [], []
    for held in (range(1), range(1, half + 1), range(half + 1, count)):
        group = lines[held[0]]
        if len(held) > 1:
            group = jnp.concatenate([lines[k] for k in held], axis=0)
        if held[0] == 1:
            group, *planes = barrier((group, *planes))
        planes = [group] + moves.plane(group)
        done.append((held, planes))
    done[1] = (done[1][0], list(barrier((*done[1][1], *done[2][1][1:]))[:count]))
    for held, planes in done:
        far = moves.cores(planes)
        for s, value in enumerate(planes):
            for lane, (array, start) in enumerate(((value, 0), far[s])):
                if not any(other is array for other in arrays):
                    arrays.append(array)
                index = [n for n, other in enumerate(arrays) if other is array][0]
                for n, k in enumerate(held):
                    layout.append((index, start + n * rows, k, s, lane))
    tails = [value[first : first + TAIL] for value, first in pair_near + pair_far]

    panel, mine = call(
        functools.partial(series_kernel, layout, count, len(arrays)),
        [jax.ShapeDtypeStruct((rows, size), BF16), block],
        [ANY] * len(arrays) + [INVMEM] * (2 * count) + [INSMEM],
        [
            pltpu.VMEM((size, size), BF16),
            pltpu.VMEM((size, size), BF16),
            pltpu.VMEM((mesh_rows, TAIL, columns), BF16),
            pltpu.VMEM((128, size), F32),
            pltpu.SemaphoreType.DMA((len(layout),)),
        ],
        "series",
        room=16 + 4 * size * size // MEGABYTE,
    )(*arrays, *tails, owner_order)

    near = [mine] + moves.plane(mine)
    square = views_call(
        functools.partial(square_kernel, count),
        {"near": whole(near), "far": moves.cores(near), "tail": [(trio, 0), (trio_far, 0)]},
        block,
        [],
        "square",
        extra=[panel],
    )

    line = moves.line(square)
    plane_near = [square] + moves.plane(square)
    plane_far = moves.cores(plane_near)
    evolved = views_call(
        functools.partial(evolve_kernel, count),
        {
            "plane_near": whole(plane_near),
            "plane_far": plane_far,
            "line_near": whole([square] + line),
            "line_far": plane_far[:1] + moves.cores(line),
            "tail": [(trio, 0)],
        },
        block,
        [pltpu.VMEM((count, columns, columns), BF16)],
        "evolve",
    )
    return moves.relabel(evolved)


def solution(mesh):
    return jax.shard_map(
        functools.partial(on_device, mesh.shape["row"], mesh.shape["col"]),
        mesh=mesh,
        in_specs=(
            P("row", "col"),
            P("row", "col"),
            P("row", "col"),
            P(None, "row", "col"),
            P(None, "row", "col"),
            P(),
            P(None, "row", "col"),
        ),
        out_specs=P("row", "col"),
        check_vma=False,
    )
```

```python
import functools

import jax
import jax.numpy as jnp
from jax import lax
from jax.experimental import pallas as pl
from jax.experimental.pallas import tpu as pltpu
from jax.sharding import PartitionSpec as P

BLK = 32
TERMS = 6
SQUARINGS = 2
FIRST = 3
AXES = ("row", "col")
F32 = jnp.float32
BF16 = jnp.bfloat16
TAIL = 16
MEGABYTE = 1024 * 1024


def coordinates(r, c):
    return r // 2, r % 2, c // 2, c % 2


def permutation(rows, cols, source):
    pairs = []
    for r in range(rows):
        for c in range(cols):
            sr, sc = source(*coordinates(r, c))
            pairs.append((sr * cols + sc, r * cols + c))
    return pairs


class Moves:
    def __init__(self, rows, cols):
        self.rows, self.cols = rows, cols

    def move(self, value, source):
        return lax.ppermute(value, AXES, permutation(self.rows, self.cols, source))

    def relabel(self, value, k=0):
        return self.move(value, lambda z, y, x, e: (2 * (z ^ k) + e, 2 * x + y))

    def along_z(self, value, k):
        return self.move(value, lambda z, y, x, e: (2 * (z ^ k) + y, 2 * x + e))

    def line(self, value, relabel=False, second=None, gate=None):
        bits = [1 << b for b in range((self.rows // 2).bit_length() - 1)]
        held = {0: value}
        for bit in reversed(bits):
            for k, part in list(held.items()):
                if k == 0 and relabel and (second is None or bit == bits[-1]):
                    held[bit] = self.relabel(value, bit)
                else:
                    if k and gate is not None:
                        part, _ = lax.optimization_barrier((part, gate))
                    held[k | bit] = self.along_z(part, bit)
            if second is not None:
                held[0] = second
        return [held[k] for k in range(1, self.rows // 2)]

    def in_plane(self, value, s):
        return self.move(value, lambda z, y, x, e: (2 * z + (y ^ (s & 1)), 2 * (x ^ (s >> 1)) + e))

    def plane(self, value, relabel=False):
        if relabel:
            return [
                self.move(value, lambda z, y, x, e: (2 * z + e, 2 * (x ^ (s >> 1)) + (y ^ (s & 1))))
                for s in range(1, self.cols)
            ]
        return [self.in_plane(value, s) for s in range(1, self.cols)]

    def core(self, value):
        return self.move(value, lambda z, y, x, e: (2 * z + y, 2 * x + 1 - e))

    def cores(self, values):
        length = values[0].shape[0]
        far = self.core(jnp.concatenate(values, axis=0) if len(values) > 1 else values[0])
        return [(far, n * length) for n in range(len(values))]


def place():
    r, c = lax.axis_index("row"), lax.axis_index("col")
    z, y, x, e = r // 2, r % 2, c // 2, c % 2
    return z, 2 * x + y, e


def iota(shape, axis):
    return lax.broadcasted_iota(jnp.int32, shape, axis)


def dot(a, b):
    return jnp.dot(a, b, preferred_element_type=F32)


def repeat_rows(rows, blocks):
    return (iota((rows, blocks), 0) // BLK == iota((rows, blocks), 1)).astype(BF16)


def repeat_columns(blocks, columns, first=0):
    return (iota((blocks, columns), 0) == iota((blocks, columns), 1) // BLK + first).astype(BF16)


def block_mask(tail, number, rows, columns):
    blocks = columns // BLK
    wide = dot(repeat_rows(rows, tail.shape[0]), tail).astype(BF16)
    return dot(wide, repeat_columns(tail.shape[1], columns, number * blocks))


def call(kernel, outs, ins, scratch, name, flops=1000, room=16):
    return pl.pallas_call(
        kernel,
        out_shape=outs,
        in_specs=ins,
        out_specs=jax.tree.map(lambda _: pl.BlockSpec(memory_space=pltpu.VMEM), outs),
        scratch_shapes=scratch,
        name=name,
        compiler_params=pltpu.CompilerParams(vmem_limit_bytes=room * MEGABYTE),
        cost_estimate=pl.CostEstimate(flops=flops, bytes_accessed=1000, transcendentals=0),
    )


def views_call(kernel, views, outs, scratch, name, flops=1000, extra=()):
    arrays, spec = [], {}
    for key, items in views.items():
        spec[key] = []
        for value, first in items:
            known = [n for n, other in enumerate(arrays) if other is value]
            if not known:
                arrays.append(value)
            spec[key].append((known[0] if known else len(arrays) - 1, first))

    def body(*refs):
        def take(key, n, length, shift=0):
            index, first = spec[key][n]
            return refs[index][first + shift : first + shift + length, :]

        kernel(take, *refs[len(arrays) :])

    operands = [*arrays, *extra]
    return call(body, outs, [INVMEM] * len(operands), scratch, name, flops)(*operands)


ANY = pl.BlockSpec(memory_space=pl.ANY)
INVMEM = pl.BlockSpec(memory_space=pltpu.VMEM)
INSMEM = pl.BlockSpec(memory_space=pltpu.SMEM)


def mask_kernel(inputs, *refs):
    sources, (masked_density, duo, trio) = refs[:inputs], refs[inputs : inputs + 3]
    held, sems = refs[inputs + 3 : -1], refs[-1]
    copies = [
        pltpu.make_async_copy(source, target, sems.at[n])
        for n, (source, target) in enumerate(zip(sources, held))
    ]
    fills, density, fock, margin, firsts, seconds = held
    rows, columns = density.shape
    row_blocks, column_blocks = rows // BLK, columns // BLK
    start_all(copies)
    tall = repeat_rows(rows, row_blocks)
    wide = repeat_columns(column_blocks, columns)

    def masked(ref, number):
        mask = dot(dot(tall, fills[number].astype(BF16)).astype(BF16), wide)
        return (ref[...].astype(F32) * mask).astype(BF16)

    wait_all(copies)
    value = masked(density, 1)
    masked_density[...] = value
    trio[TAIL + 2 * rows :, :] = value
    for half, (ref, number) in enumerate(((fock, 0), (margin, 2))):
        value = masked(ref, number)
        duo[half * rows : (half + 1) * rows, :] = value
        trio[TAIL + half * rows : TAIL + (half + 1) * rows, :] = value
    top = (iota((TAIL, row_blocks), 0) == iota((TAIL, row_blocks), 1)).astype(BF16)
    tail = jnp.zeros((TAIL, columns), F32)
    for number in range(FIRST + seconds.shape[1]):
        block = firsts[number] if number < FIRST else seconds[:, number - FIRST, :]
        column = iota((column_blocks, columns), 1) - number * column_blocks
        spread = (iota((column_blocks, columns), 0) == column).astype(BF16)
        tail += dot(dot(top, block.astype(BF16)).astype(BF16), spread)
    trio[:TAIL, :] = tail.astype(BF16)


def chunk(index, length):
    return pl.ds(pl.multiple_of(index * length, length), length)


def start_all(copies):
    for one in copies:
        one.start()


def wait_all(copies):
    for one in copies:
        one.wait()


def repeat(times, body, unrolled):
    if unrolled:
        for t in range(times):
            body(t)
    else:

        def step(t, carry):
            body(t)
            return carry

        lax.fori_loop(0, times, step, 0)


def in_order(near, far, e):
    low = jnp.where(e == 0, near, far)
    high = jnp.where(e == 0, far, near)
    return jnp.concatenate([low, high], axis=0)


def first_kernel(count, take, out, left):
    z, q, e = place()
    rows, columns = out.shape[0] // 2, out.shape[1]
    for s in range(count):
        left[q ^ s] = take("plane", s, 2 * rows)
    tail = take("tail", 0, TAIL)
    masks = [block_mask(tail, n, rows, columns) for n in range(2)]
    total = jnp.zeros((2 * rows, columns), F32)
    for s in range(count):
        total += dot(left[z ^ s], in_order(take("near", s, rows), take("far", s, rows), e))
    for n in range(2):
        part = slice(n * rows, (n + 1) * rows)
        out[part, :] = (total[part] * masks[n]).astype(BF16)


def generator_kernel(count, take, out, left):
    z, q, e = place()
    rows, columns = out.shape
    for s in range(count):
        for half in range(2):
            left[half, q ^ s] = take("plane", s, rows, half * rows)
    mask = block_mask(take("tail", 0, TAIL), 2, rows, columns)
    total = jnp.zeros((rows, columns), F32)
    for half in range(2):
        shift = (1 - half) * rows
        for s in range(count):
            right = in_order(take("near", s, rows, shift), take("far", s, rows, shift), e)
            product = dot(left[half, z ^ s], right)
            total = total + product if half == 0 else total - product
    generator = (total * mask).astype(BF16)
    out[...] = (generator.astype(F32) * 0.25).astype(BF16)


def series_kernel(layout, count, pieces, *refs):
    arrays, tails, order = refs[:pieces], refs[pieces : pieces + 2 * count], refs[pieces + 2 * count]
    panel, mine, whole, turned, wides, spread, sems = refs[pieces + 2 * count + 1 :]
    z, q, e = place()
    rows, columns = mine.shape
    size = panel.shape[1]
    row_blocks, column_blocks, blocks = rows // BLK, columns // BLK, size // BLK
    small = size <= 1536
    copies = []
    for index, first, k, plane, lane in layout:
        core = e if lane == 0 else 1 - e
        copies.append(
            pltpu.make_async_copy(
                arrays[index].at[pl.ds(first, rows)],
                whole.at[chunk(2 * (z ^ k) + core, rows), chunk(q ^ plane, columns)],
                sems.at[len(copies)],
            )
        )
    start_all(copies)
    for index, ref in enumerate(tails):
        core = e if index < count else 1 - e
        wides[2 * (z ^ (index % count)) + core] = ref[...]
    filters = jnp.zeros((128, size), F32)
    for p in range(2 * count):
        column = iota((TAIL, size), 1) // BLK
        row = iota((TAIL, size), 0)
        near = ((row < row_blocks) & (column == row + p * row_blocks)).astype(BF16)
        filters += lax.dot_general(
            wides[p][:, :128], near, (((0,), (0,)), ((), ())), preferred_element_type=F32
        )
    spread[...] = filters

    wait_all(copies)

    def turn(t):
        tile = jnp.concatenate(
            [whole[chunk(order[t * column_blocks + a], BLK), :] for a in range(column_blocks)],
            axis=0,
        )
        turned[:, chunk(t, columns)] = tile.T

    def place_rows(b):
        whole[chunk(b, BLK), :] = turned[chunk(order[b], BLK), :]

    repeat(count, turn, small)
    repeat(blocks, place_rows, small)

    first = (2 * q + e) * rows
    unit = (iota((rows, size), 1) == iota((rows, size), 0) + first).astype(F32)
    own = unit + whole[chunk(2 * q + e, rows), :].astype(F32) / TERMS
    panel[...] = own.astype(BF16)
    width = size if small else 512
    for number in range(1, TERMS):
        current = panel[...]
        base = (FIRST + number - 1) * column_blocks + e * row_blocks

        def advance(t):
            part = chunk(t, width)
            product = dot(current, whole[:, part])
            mask = jnp.concatenate(
                [
                    jnp.broadcast_to(spread[pl.ds(base + b, 1), part], (BLK, width))
                    for b in range(row_blocks)
                ],
                axis=0,
            )
            here = iota((rows, width), 1) + t * width == iota((rows, width), 0) + first
            panel[:, part] = (here.astype(F32) + product * mask / (TERMS - number)).astype(BF16)

        repeat(size // width, advance, small)
    mine[...] = panel[:, chunk(z, columns)]


def turned_mask(tails, number, e, rows, columns):
    row_blocks, column_blocks = rows // BLK, columns // BLK
    pick = iota((rows, 128), 0) // BLK + number * column_blocks + e * row_blocks
    pick = (pick == iota((rows, 128), 1)).astype(BF16)
    mask = jnp.zeros((rows, columns), F32)
    for core in range(2):
        row = iota((TAIL, columns), 0)
        near = (row < row_blocks) & (iota((TAIL, columns), 1) // BLK == row + core * row_blocks)
        chosen = lax.dot_general(
            pick, tails[core][:, :128], (((1,), (1,)), ((), ())), preferred_element_type=F32
        )
        mask += dot(chosen.astype(BF16), near.astype(BF16))
    return mask


def square_kernel(count, take, panel, out):
    z, q, e = place()
    rows, columns = out.shape
    tails = in_order(take("tail", 0, TAIL), take("tail", 1, TAIL), e)
    mask = turned_mask([tails[:TAIL], tails[TAIL:]], FIRST + TERMS - 1, e, rows, columns)
    total = jnp.zeros((rows, columns), F32)
    for s in range(count):
        right = in_order(take("near", s, rows), take("far", s, rows), e)
        total += dot(panel[:, chunk(q ^ s, columns)], right)
    out[...] = (total * mask).astype(BF16)


def evolve_kernel(count, take, out, right):
    z, q, e = place()
    rows, columns = out.shape
    for s in range(count):
        right[q ^ s] = in_order(take("plane_near", s, rows), take("plane_far", s, rows), e)
    mask = block_mask(take("tail", 0, TAIL), FIRST + TERMS, rows, columns)
    total = jnp.zeros((columns, columns), F32)
    for s in range(count):
        total += dot(
            in_order(take("line_near", s, rows), take("line_far", s, rows), e), right[z ^ s]
        )
    total = total.T
    chosen = jnp.where(e == 0, total[:rows], total[rows:])
    out[...] = (chosen * mask).astype(BF16)


def on_device(
    mesh_rows,
    mesh_cols,
    fock_matrix,
    density,
    margin,
    fill_patterns,
    first_filters,
    owner_order,
    second_filters,
):
    moves = Moves(mesh_rows, mesh_cols)
    count = mesh_cols
    half = count // 2
    rows, columns = fock_matrix.shape
    size = rows * mesh_rows
    block = jax.ShapeDtypeStruct((rows, columns), BF16)
    barrier = lax.optimization_barrier

    def whole(values):
        return [(value, 0) for value in values]

    inputs = (
        fill_patterns,
        density,
        fock_matrix,
        margin,
        first_filters,
        second_filters.transpose(1, 0, 2),
    )
    masked_density, duo, trio = call(
        functools.partial(mask_kernel, len(inputs)),
        [
            block,
            jax.ShapeDtypeStruct((2 * rows, columns), BF16),
            jax.ShapeDtypeStruct((TAIL + 3 * rows, columns), BF16),
        ],
        [ANY] * len(inputs),
        [pltpu.VMEM(value.shape, value.dtype) for value in inputs]
        + [pltpu.SemaphoreType.DMA((len(inputs),))],
        "mask",
        room=60,
    )(*inputs)

    home = trio
    trio = moves.relabel(home)
    fock_rows = moves.plane(duo, True)
    density_line = moves.line(masked_density, True)
    density_near = [(trio, TAIL + 2 * rows)] + whole(density_line)
    span = TAIL + 2 * rows
    pair_second, *_ = barrier((trio[:span], *density_line))
    pair_line = moves.line(home[:span], True, second=pair_second)
    early = barrier((*density_line, trio, pair_line[half - 1], *fock_rows))
    density_line, trio, pair_line[half - 1] = list(early[: count - 1]), early[count - 1], early[count]
    trio_far = moves.core(trio)
    density_far = [(trio_far, TAIL + 2 * rows)] + moves.cores(density_line)

    products = views_call(
        functools.partial(first_kernel, count),
        {
            "plane": [(trio, TAIL)] + whole(fock_rows),
            "tail": [(trio, 0)],
            "near": density_near,
            "far": density_far,
        },
        jax.ShapeDtypeStruct((2 * rows, columns), BF16),
        [pltpu.VMEM((count, 2 * rows, columns), BF16)],
        "first",
        10**10,
    )
    product_rows = [products] + moves.plane(products)
    pair_line = list(barrier((*pair_line, *product_rows[1:]))[: count - 1])
    pair_far = [(trio_far, 0)] + moves.cores(pair_line[:half]) + moves.cores(pair_line[half:])
    pair_near = [(trio, 0)] + whole(pair_line)

    generator = views_call(
        functools.partial(generator_kernel, count),
        {
            "plane": whole(product_rows),
            "tail": [(trio, 0)],
            "near": [(value, first + TAIL) for value, first in pair_near],
            "far": [(value, first + TAIL) for value, first in pair_far],
        },
        block,
        [pltpu.VMEM((2, count, rows, columns), BF16)],
        "generator",
    )

    lines = [generator] + moves.line(generator)
    arrays, layout, planes, done = [], [], [], []
    for held in (range(1), range(1, half + 1), range(half + 1, count)):
        group = lines[held[0]]
        if len(held) > 1:
            group = jnp.concatenate([lines[k] for k in held], axis=0)
        if held[0] == 1:
            group, *planes = barrier((group, *planes))
        planes = [group] + moves.plane(group)
        done.append((held, planes))
    done[1] = (done[1][0], list(barrier((*done[1][1], *done[2][1][1:]))[:count]))
    for held, planes in done:
        far = moves.cores(planes)
        for s, value in enumerate(planes):
            for lane, (array, start) in enumerate(((value, 0), far[s])):
                if not any(other is array for other in arrays):
                    arrays.append(array)
                index = [n for n, other in enumerate(arrays) if other is array][0]
                for n, k in enumerate(held):
                    layout.append((index, start + n * rows, k, s, lane))
    tails = [value[first : first + TAIL] for value, first in pair_near + pair_far]

    panel, mine = call(
        functools.partial(series_kernel, layout, count, len(arrays)),
        [jax.ShapeDtypeStruct((rows, size), BF16), block],
        [ANY] * len(arrays) + [INVMEM] * (2 * count) + [INSMEM],
        [
            pltpu.VMEM((size, size), BF16),
            pltpu.VMEM((size, size), BF16),
            pltpu.VMEM((mesh_rows, TAIL, columns), BF16),
            pltpu.VMEM((128, size), F32),
            pltpu.SemaphoreType.DMA((len(layout),)),
        ],
        "series",
        room=16 + 4 * size * size // MEGABYTE,
    )(*arrays, *tails, owner_order)

    near = [mine] + moves.plane(mine)
    square = views_call(
        functools.partial(square_kernel, count),
        {"near": whole(near), "far": moves.cores(near), "tail": [(trio, 0), (trio_far, 0)]},
        block,
        [],
        "square",
        extra=[panel],
    )

    line = moves.line(square)
    plane_near = [square] + moves.plane(square)
    plane_far = moves.cores(plane_near)
    evolved = views_call(
        functools.partial(evolve_kernel, count),
        {
            "plane_near": whole(plane_near),
            "plane_far": plane_far,
            "line_near": whole([square] + line),
            "line_far": plane_far[:1] + moves.cores(line),
            "tail": [(trio, 0)],
        },
        block,
        [pltpu.VMEM((count, columns, columns), BF16)],
        "evolve",
    )
    return moves.relabel(evolved)


def solution(mesh):
    return jax.shard_map(
        functools.partial(on_device, mesh.shape["row"], mesh.shape["col"]),
        mesh=mesh,
        in_specs=(
            P("row", "col"),
            P("row", "col"),
            P("row", "col"),
            P(None, "row", "col"),
            P(None, "row", "col"),
            P(),
            P(None, "row", "col"),
        ),
        out_specs=P("row", "col"),
        check_vma=False,
    )
```

```python
import functools

import jax
import jax.numpy as jnp
from jax import lax
from jax.experimental import pallas as pl
from jax.experimental.pallas import tpu as pltpu
from jax.sharding import PartitionSpec as P

BLK = 32
TERMS = 6
SQUARINGS = 2
FIRST = 3
AXES = ("row", "col")
F32 = jnp.float32
BF16 = jnp.bfloat16
TAIL = 16
MEGABYTE = 1024 * 1024


def coordinates(r, c):
    return r // 2, r % 2, c // 2, c % 2


def permutation(rows, cols, source):
    pairs = []
    for r in range(rows):
        for c in range(cols):
            sr, sc = source(*coordinates(r, c))
            pairs.append((sr * cols + sc, r * cols + c))
    return pairs


class Moves:
    def __init__(self, rows, cols):
        self.rows, self.cols = rows, cols

    def move(self, value, source):
        return lax.ppermute(value, AXES, permutation(self.rows, self.cols, source))

    def relabel(self, value, k=0):
        return self.move(value, lambda z, y, x, e: (2 * (z ^ k) + e, 2 * x + y))

    def along_z(self, value, k):
        return self.move(value, lambda z, y, x, e: (2 * (z ^ k) + y, 2 * x + e))

    def line(self, value, relabel=False, second=None, gate=None):
        bits = [1 << b for b in range((self.rows // 2).bit_length() - 1)]
        held = {0: value}
        for bit in reversed(bits):
            for k, part in list(held.items()):
                if k == 0 and relabel and (second is None or bit == bits[-1]):
                    held[bit] = self.relabel(value, bit)
                else:
                    if k and gate is not None:
                        part, _ = lax.optimization_barrier((part, gate))
                    held[k | bit] = self.along_z(part, bit)
            if second is not None:
                held[0] = second
        return [held[k] for k in range(1, self.rows // 2)]

    def in_plane(self, value, s):
        return self.move(value, lambda z, y, x, e: (2 * z + (y ^ (s & 1)), 2 * (x ^ (s >> 1)) + e))

    def plane(self, value, relabel=False):
        if relabel:
            return [
                self.move(value, lambda z, y, x, e: (2 * z + e, 2 * (x ^ (s >> 1)) + (y ^ (s & 1))))
                for s in range(1, self.cols)
            ]
        return [self.in_plane(value, s) for s in range(1, self.cols)]

    def core(self, value):
        return self.move(value, lambda z, y, x, e: (2 * z + y, 2 * x + 1 - e))

    def cores(self, values):
        length = values[0].shape[0]
        far = self.core(jnp.concatenate(values, axis=0) if len(values) > 1 else values[0])
        return [(far, n * length) for n in range(len(values))]


def place():
    r, c = lax.axis_index("row"), lax.axis_index("col")
    z, y, x, e = r // 2, r % 2, c // 2, c % 2
    return z, 2 * x + y, e


def iota(shape, axis):
    return lax.broadcasted_iota(jnp.int32, shape, axis)


def dot(a, b):
    return jnp.dot(a, b, preferred_element_type=F32)


def repeat_rows(rows, blocks):
    return (iota((rows, blocks), 0) // BLK == iota((rows, blocks), 1)).astype(BF16)


def repeat_columns(blocks, columns, first=0):
    return (iota((blocks, columns), 0) == iota((blocks, columns), 1) // BLK + first).astype(BF16)


def block_mask(tail, number, rows, columns):
    blocks = columns // BLK
    wide = dot(repeat_rows(rows, tail.shape[0]), tail).astype(BF16)
    return dot(wide, repeat_columns(tail.shape[1], columns, number * blocks))


def call(kernel, outs, ins, scratch, name, flops=1000, room=16):
    return pl.pallas_call(
        kernel,
        out_shape=outs,
        in_specs=ins,
        out_specs=jax.tree.map(lambda _: pl.BlockSpec(memory_space=pltpu.VMEM), outs),
        scratch_shapes=scratch,
        name=name,
        compiler_params=pltpu.CompilerParams(vmem_limit_bytes=room * MEGABYTE),
        cost_estimate=pl.CostEstimate(flops=flops, bytes_accessed=1000, transcendentals=0),
    )


def views_call(kernel, views, outs, scratch, name, flops=1000, extra=()):
    arrays, spec = [], {}
    for key, items in views.items():
        spec[key] = []
        for value, first in items:
            known = [n for n, other in enumerate(arrays) if other is value]
            if not known:
                arrays.append(value)
            spec[key].append((known[0] if known else len(arrays) - 1, first))

    def body(*refs):
        def take(key, n, length, shift=0):
            index, first = spec[key][n]
            return refs[index][first + shift : first + shift + length, :]

        kernel(take, *refs[len(arrays) :])

    operands = [*arrays, *extra]
    return call(body, outs, [INVMEM] * len(operands), scratch, name, flops)(*operands)


ANY = pl.BlockSpec(memory_space=pl.ANY)
INVMEM = pl.BlockSpec(memory_space=pltpu.VMEM)
INSMEM = pl.BlockSpec(memory_space=pltpu.SMEM)


def mask_kernel(inputs, *refs):
    sources, (masked_density, duo, trio) = refs[:inputs], refs[inputs : inputs + 3]
    held, sems = refs[inputs + 3 : -1], refs[-1]
    copies = [
        pltpu.make_async_copy(source, target, sems.at[n])
        for n, (source, target) in enumerate(zip(sources, held))
    ]
    fills, density, fock, margin, firsts, seconds = held
    rows, columns = density.shape
    row_blocks, column_blocks = rows // BLK, columns // BLK
    start_all(copies)
    tall = repeat_rows(rows, row_blocks)
    wide = repeat_columns(column_blocks, columns)

    def masked(ref, number):
        mask = dot(dot(tall, fills[number].astype(BF16)).astype(BF16), wide)
        return (ref[...].astype(F32) * mask).astype(BF16)

    wait_all(copies)
    value = masked(density, 1)
    masked_density[...] = value
    trio[TAIL + 2 * rows :, :] = value
    for half, (ref, number) in enumerate(((fock, 0), (margin, 2))):
        value = masked(ref, number)
        duo[half * rows : (half + 1) * rows, :] = value
        trio[TAIL + half * rows : TAIL + (half + 1) * rows, :] = value
    top = (iota((TAIL, row_blocks), 0) == iota((TAIL, row_blocks), 1)).astype(BF16)
    tail = jnp.zeros((TAIL, columns), F32)
    for number in range(FIRST + seconds.shape[1]):
        block = firsts[number] if number < FIRST else seconds[:, number - FIRST, :]
        column = iota((column_blocks, columns), 1) - number * column_blocks
        spread = (iota((column_blocks, columns), 0) == column).astype(BF16)
        tail += dot(dot(top, block.astype(BF16)).astype(BF16), spread)
    trio[:TAIL, :] = tail.astype(BF16)


def chunk(index, length):
    return pl.ds(pl.multiple_of(index * length, length), length)


def start_all(copies):
    for one in copies:
        one.start()


def wait_all(copies):
    for one in copies:
        one.wait()


def repeat(times, body, unrolled):
    if unrolled:
        for t in range(times):
            body(t)
    else:

        def step(t, carry):
            body(t)
            return carry

        lax.fori_loop(0, times, step, 0)


def in_order(near, far, e):
    low = jnp.where(e == 0, near, far)
    high = jnp.where(e == 0, far, near)
    return jnp.concatenate([low, high], axis=0)


def first_kernel(count, take, out, left):
    z, q, e = place()
    rows, columns = out.shape[0] // 2, out.shape[1]
    for s in range(count):
        left[q ^ s] = take("plane", s, 2 * rows)
    tail = take("tail", 0, TAIL)
    masks = [block_mask(tail, n, rows, columns) for n in range(2)]
    total = jnp.zeros((2 * rows, columns), F32)
    for s in range(count):
        total += dot(left[z ^ s], in_order(take("near", s, rows), take("far", s, rows), e))
    for n in range(2):
        part = slice(n * rows, (n + 1) * rows)
        out[part, :] = (total[part] * masks[n]).astype(BF16)


def generator_kernel(count, take, out, left):
    z, q, e = place()
    rows, columns = out.shape
    for s in range(count):
        for half in range(2):
            left[half, q ^ s] = take("plane", s, rows, half * rows)
    mask = block_mask(take("tail", 0, TAIL), 2, rows, columns)
    total = jnp.zeros((rows, columns), F32)
    for half in range(2):
        shift = (1 - half) * rows
        for s in range(count):
            right = in_order(take("near", s, rows, shift), take("far", s, rows, shift), e)
            product = dot(left[half, z ^ s], right)
            total = total + product if half == 0 else total - product
    generator = (total * mask).astype(BF16)
    out[...] = (generator.astype(F32) * 0.25).astype(BF16)


def series_kernel(layout, count, pieces, *refs):
    arrays, tails, order = refs[:pieces], refs[pieces : pieces + 2 * count], refs[pieces + 2 * count]
    panel, mine, whole, turned, wides, spread, sems = refs[pieces + 2 * count + 1 :]
    z, q, e = place()
    rows, columns = mine.shape
    size = panel.shape[1]
    row_blocks, column_blocks, blocks = rows // BLK, columns // BLK, size // BLK
    small = size <= 1536
    copies = []
    for index, first, k, plane, lane in layout:
        core = e if lane == 0 else 1 - e
        copies.append(
            pltpu.make_async_copy(
                arrays[index].at[pl.ds(first, rows)],
                whole.at[chunk(2 * (z ^ k) + core, rows), chunk(q ^ plane, columns)],
                sems.at[len(copies)],
            )
        )
    start_all(copies)
    for index, ref in enumerate(tails):
        core = e if index < count else 1 - e
        wides[2 * (z ^ (index % count)) + core] = ref[...]
    filters = jnp.zeros((128, size), F32)
    for p in range(2 * count):
        column = iota((TAIL, size), 1) // BLK
        row = iota((TAIL, size), 0)
        near = ((row < row_blocks) & (column == row + p * row_blocks)).astype(BF16)
        filters += lax.dot_general(
            wides[p][:, :128], near, (((0,), (0,)), ((), ())), preferred_element_type=F32
        )
    spread[...] = filters

    wait_all(copies)

    def turn(t):
        tile = jnp.concatenate(
            [whole[chunk(order[t * column_blocks + a], BLK), :] for a in range(column_blocks)],
            axis=0,
        )
        turned[:, chunk(t, columns)] = tile.T

    def place_rows(b):
        whole[chunk(b, BLK), :] = turned[chunk(order[b], BLK), :]

    repeat(count, turn, small)
    repeat(blocks, place_rows, small)

    first = (2 * q + e) * rows
    unit = (iota((rows, size), 1) == iota((rows, size), 0) + first).astype(F32)
    own = unit + whole[chunk(2 * q + e, rows), :].astype(F32) / TERMS
    panel[...] = own.astype(BF16)
    width = size if small else 512
    for number in range(1, TERMS):
        current = panel[...]
        base = (FIRST + number - 1) * column_blocks + e * row_blocks

        def advance(t):
            part = chunk(t, width)
            product = dot(current, whole[:, part])
            mask = jnp.concatenate(
                [
                    jnp.broadcast_to(spread[pl.ds(base + b, 1), part], (BLK, width))
                    for b in range(row_blocks)
                ],
                axis=0,
            )
            here = iota((rows, width), 1) + t * width == iota((rows, width), 0) + first
            panel[:, part] = (here.astype(F32) + product * mask / (TERMS - number)).astype(BF16)

        repeat(size // width, advance, small)
    mine[...] = panel[:, chunk(z, columns)]


def turned_mask(tails, number, e, rows, columns):
    row_blocks, column_blocks = rows // BLK, columns // BLK
    pick = iota((rows, 128), 0) // BLK + number * column_blocks + e * row_blocks
    pick = (pick == iota((rows, 128), 1)).astype(BF16)
    mask = jnp.zeros((rows, columns), F32)
    for core in range(2):
        row = iota((TAIL, columns), 0)
        near = (row < row_blocks) & (iota((TAIL, columns), 1) // BLK == row + core * row_blocks)
        chosen = lax.dot_general(
            pick, tails[core][:, :128], (((1,), (1,)), ((), ())), preferred_element_type=F32
        )
        mask += dot(chosen.astype(BF16), near.astype(BF16))
    return mask


def square_kernel(count, take, panel, out):
    z, q, e = place()
    rows, columns = out.shape
    tails = in_order(take("tail", 0, TAIL), take("tail", 1, TAIL), e)
    mask = turned_mask([tails[:TAIL], tails[TAIL:]], FIRST + TERMS - 1, e, rows, columns)
    total = jnp.zeros((rows, columns), F32)
    for s in range(count):
        right = in_order(take("near", s, rows), take("far", s, rows), e)
        total += dot(panel[:, chunk(q ^ s, columns)], right)
    out[...] = (total * mask).astype(BF16)


def evolve_kernel(count, take, out, right):
    z, q, e = place()
    rows, columns = out.shape
    for s in range(count):
        right[q ^ s] = in_order(take("plane_near", s, rows), take("plane_far", s, rows), e)
    mask = block_mask(take("tail", 0, TAIL), FIRST + TERMS, rows, columns)
    total = jnp.zeros((columns, columns), F32)
    for s in range(count):
        total += dot(
            in_order(take("line_near", s, rows), take("line_far", s, rows), e), right[z ^ s]
        )
    total = total.T
    chosen = jnp.where(e == 0, total[:rows], total[rows:])
    out[...] = (chosen * mask).astype(BF16)


def on_device(
    mesh_rows,
    mesh_cols,
    fock_matrix,
    density,
    margin,
    fill_patterns,
    first_filters,
    owner_order,
    second_filters,
):
    moves = Moves(mesh_rows, mesh_cols)
    count = mesh_cols
    half = count // 2
    rows, columns = fock_matrix.shape
    size = rows * mesh_rows
    block = jax.ShapeDtypeStruct((rows, columns), BF16)
    barrier = lax.optimization_barrier

    def whole(values):
        return [(value, 0) for value in values]

    inputs = (
        fill_patterns,
        density,
        fock_matrix,
        margin,
        first_filters,
        second_filters.transpose(1, 0, 2),
    )
    masked_density, duo, trio = call(
        functools.partial(mask_kernel, len(inputs)),
        [
            block,
            jax.ShapeDtypeStruct((2 * rows, columns), BF16),
            jax.ShapeDtypeStruct((TAIL + 3 * rows, columns), BF16),
        ],
        [ANY] * len(inputs),
        [pltpu.VMEM(value.shape, value.dtype) for value in inputs]
        + [pltpu.SemaphoreType.DMA((len(inputs),))],
        "mask",
        room=60,
    )(*inputs)

    home = trio
    trio = moves.relabel(home)
    fock_rows = moves.plane(duo, True)
    density_line = moves.line(masked_density, True, gate=tuple(fock_rows))
    density_near = [(trio, TAIL + 2 * rows)] + whole(density_line)
    span = TAIL + 2 * rows
    pair_second, *_ = barrier((trio[:span], *density_line))
    pair_line = moves.line(home[:span], True, second=pair_second)
    early = barrier((*density_line, trio, pair_line[half - 1], *fock_rows))
    density_line, trio, pair_line[half - 1] = list(early[: count - 1]), early[count - 1], early[count]
    trio_far = moves.core(trio)
    density_far = [(trio_far, TAIL + 2 * rows)] + moves.cores(density_line)

    products = views_call(
        functools.partial(first_kernel, count),
        {
            "plane": [(trio, TAIL)] + whole(fock_rows),
            "tail": [(trio, 0)],
            "near": density_near,
            "far": density_far,
        },
        jax.ShapeDtypeStruct((2 * rows, columns), BF16),
        [pltpu.VMEM((count, 2 * rows, columns), BF16)],
        "first",
        10**10,
    )
    product_rows = [products] + moves.plane(products)
    pair_line = list(barrier((*pair_line, *product_rows[1:]))[: count - 1])
    pair_far = [(trio_far, 0)] + moves.cores(pair_line[:half]) + moves.cores(pair_line[half:])
    pair_near = [(trio, 0)] + whole(pair_line)

    generator = views_call(
        functools.partial(generator_kernel, count),
        {
            "plane": whole(product_rows),
            "tail": [(trio, 0)],
            "near": [(value, first + TAIL) for value, first in pair_near],
            "far": [(value, first + TAIL) for value, first in pair_far],
        },
        block,
        [pltpu.VMEM((2, count, rows, columns), BF16)],
        "generator",
    )

    lines = [generator] + moves.line(generator)
    arrays, layout, planes, done = [], [], [], []
    for held in (range(1), range(1, half + 1), range(half + 1, count)):
        group = lines[held[0]]
        if len(held) > 1:
            group = jnp.concatenate([lines[k] for k in held], axis=0)
        if held[0] == 1:
            group, *planes = barrier((group, *planes))
        planes = [group] + moves.plane(group)
        done.append((held, planes))
    done[1] = (done[1][0], list(barrier((*done[1][1], *done[2][1][1:]))[:count]))
    for held, planes in done:
        far = moves.cores(planes)
        for s, value in enumerate(planes):
            for lane, (array, start) in enumerate(((value, 0), far[s])):
                if not any(other is array for other in arrays):
                    arrays.append(array)
                index = [n for n, other in enumerate(arrays) if other is array][0]
                for n, k in enumerate(held):
                    layout.append((index, start + n * rows, k, s, lane))
    tails = [value[first : first + TAIL] for value, first in pair_near + pair_far]

    panel, mine = call(
        functools.partial(series_kernel, layout, count, len(arrays)),
        [jax.ShapeDtypeStruct((rows, size), BF16), block],
        [ANY] * len(arrays) + [INVMEM] * (2 * count) + [INSMEM],
        [
            pltpu.VMEM((size, size), BF16),
            pltpu.VMEM((size, size), BF16),
            pltpu.VMEM((mesh_rows, TAIL, columns), BF16),
            pltpu.VMEM((128, size), F32),
            pltpu.SemaphoreType.DMA((len(layout),)),
        ],
        "series",
        room=16 + 4 * size * size // MEGABYTE,
    )(*arrays, *tails, owner_order)

    near = [mine] + moves.plane(mine)
    square = views_call(
        functools.partial(square_kernel, count),
        {"near": whole(near), "far": moves.cores(near), "tail": [(trio, 0), (trio_far, 0)]},
        block,
        [],
        "square",
        extra=[panel],
    )

    line = moves.line(square)
    plane_near = [square] + moves.plane(square)
    plane_far = moves.cores(plane_near)
    evolved = views_call(
        functools.partial(evolve_kernel, count),
        {
            "plane_near": whole(plane_near),
            "plane_far": plane_far,
            "line_near": whole([square] + line),
            "line_far": plane_far[:1] + moves.cores(line),
            "tail": [(trio, 0)],
        },
        block,
        [pltpu.VMEM((count, columns, columns), BF16)],
        "evolve",
    )
    return moves.relabel(evolved)


def solution(mesh):
    return jax.shard_map(
        functools.partial(on_device, mesh.shape["row"], mesh.shape["col"]),
        mesh=mesh,
        in_specs=(
            P("row", "col"),
            P("row", "col"),
            P("row", "col"),
            P(None, "row", "col"),
            P(None, "row", "col"),
            P(),
            P(None, "row", "col"),
        ),
        out_specs=P("row", "col"),
        check_vma=False,
    )
```

```python
import functools

import jax
import jax.numpy as jnp
from jax import lax
from jax.experimental import pallas as pl
from jax.experimental.pallas import tpu as pltpu
from jax.sharding import PartitionSpec as P

BLK = 32
TERMS = 6
SQUARINGS = 2
FIRST = 3
AXES = ("row", "col")
F32 = jnp.float32
BF16 = jnp.bfloat16
TAIL = 16
MEGABYTE = 1024 * 1024


def coordinates(r, c):
    return r // 2, r % 2, c // 2, c % 2


def permutation(rows, cols, source):
    pairs = []
    for r in range(rows):
        for c in range(cols):
            sr, sc = source(*coordinates(r, c))
            pairs.append((sr * cols + sc, r * cols + c))
    return pairs


class Moves:
    def __init__(self, rows, cols):
        self.rows, self.cols = rows, cols

    def move(self, value, source):
        return lax.ppermute(value, AXES, permutation(self.rows, self.cols, source))

    def relabel(self, value, k=0):
        return self.move(value, lambda z, y, x, e: (2 * (z ^ k) + e, 2 * x + y))

    def along_z(self, value, k):
        return self.move(value, lambda z, y, x, e: (2 * (z ^ k) + y, 2 * x + e))

    def line(self, value, relabel=False, second=None, gate=None):
        bits = [1 << b for b in range((self.rows // 2).bit_length() - 1)]
        held = {0: value}
        for bit in reversed(bits):
            for k, part in list(held.items()):
                if k == 0 and relabel and (second is None or bit == bits[-1]):
                    held[bit] = self.relabel(value, bit)
                else:
                    if k and gate is not None:
                        part, _ = lax.optimization_barrier((part, (gate, held[bit])))
                    held[k | bit] = self.along_z(part, bit)
            if second is not None:
                held[0] = second
        return [held[k] for k in range(1, self.rows // 2)]

    def in_plane(self, value, s):
        return self.move(value, lambda z, y, x, e: (2 * z + (y ^ (s & 1)), 2 * (x ^ (s >> 1)) + e))

    def plane(self, value, relabel=False):
        if relabel:
            return [
                self.move(value, lambda z, y, x, e: (2 * z + e, 2 * (x ^ (s >> 1)) + (y ^ (s & 1))))
                for s in range(1, self.cols)
            ]
        return [self.in_plane(value, s) for s in range(1, self.cols)]

    def core(self, value):
        return self.move(value, lambda z, y, x, e: (2 * z + y, 2 * x + 1 - e))

    def cores(self, values):
        length = values[0].shape[0]
        far = self.core(jnp.concatenate(values, axis=0) if len(values) > 1 else values[0])
        return [(far, n * length) for n in range(len(values))]


def place():
    r, c = lax.axis_index("row"), lax.axis_index("col")
    z, y, x, e = r // 2, r % 2, c // 2, c % 2
    return z, 2 * x + y, e


def iota(shape, axis):
    return lax.broadcasted_iota(jnp.int32, shape, axis)


def dot(a, b):
    return jnp.dot(a, b, preferred_element_type=F32)


def repeat_rows(rows, blocks):
    return (iota((rows, blocks), 0) // BLK == iota((rows, blocks), 1)).astype(BF16)


def repeat_columns(blocks, columns, first=0):
    return (iota((blocks, columns), 0) == iota((blocks, columns), 1) // BLK + first).astype(BF16)


def block_mask(tail, number, rows, columns):
    blocks = columns // BLK
    wide = dot(repeat_rows(rows, tail.shape[0]), tail).astype(BF16)
    return dot(wide, repeat_columns(tail.shape[1], columns, number * blocks))


def call(kernel, outs, ins, scratch, name, flops=1000, room=16):
    return pl.pallas_call(
        kernel,
        out_shape=outs,
        in_specs=ins,
        out_specs=jax.tree.map(lambda _: pl.BlockSpec(memory_space=pltpu.VMEM), outs),
        scratch_shapes=scratch,
        name=name,
        compiler_params=pltpu.CompilerParams(vmem_limit_bytes=room * MEGABYTE),
        cost_estimate=pl.CostEstimate(flops=flops, bytes_accessed=1000, transcendentals=0),
    )


def views_call(kernel, views, outs, scratch, name, flops=1000, extra=()):
    arrays, spec = [], {}
    for key, items in views.items():
        spec[key] = []
        for value, first in items:
            known = [n for n, other in enumerate(arrays) if other is value]
            if not known:
                arrays.append(value)
            spec[key].append((known[0] if known else len(arrays) - 1, first))

    def body(*refs):
        def take(key, n, length, shift=0):
            index, first = spec[key][n]
            return refs[index][first + shift : first + shift + length, :]

        kernel(take, *refs[len(arrays) :])

    operands = [*arrays, *extra]
    return call(body, outs, [INVMEM] * len(operands), scratch, name, flops)(*operands)


ANY = pl.BlockSpec(memory_space=pl.ANY)
INVMEM = pl.BlockSpec(memory_space=pltpu.VMEM)
INSMEM = pl.BlockSpec(memory_space=pltpu.SMEM)


def mask_kernel(inputs, *refs):
    sources, (masked_density, duo, trio) = refs[:inputs], refs[inputs : inputs + 3]
    held, sems = refs[inputs + 3 : -1], refs[-1]
    copies = [
        pltpu.make_async_copy(source, target, sems.at[n])
        for n, (source, target) in enumerate(zip(sources, held))
    ]
    fills, density, fock, margin, firsts, seconds = held
    rows, columns = density.shape
    row_blocks, column_blocks = rows // BLK, columns // BLK
    start_all(copies)
    tall = repeat_rows(rows, row_blocks)
    wide = repeat_columns(column_blocks, columns)

    def masked(ref, number):
        mask = dot(dot(tall, fills[number].astype(BF16)).astype(BF16), wide)
        return (ref[...].astype(F32) * mask).astype(BF16)

    wait_all(copies)
    value = masked(density, 1)
    masked_density[...] = value
    trio[TAIL + 2 * rows :, :] = value
    for half, (ref, number) in enumerate(((fock, 0), (margin, 2))):
        value = masked(ref, number)
        duo[half * rows : (half + 1) * rows, :] = value
        trio[TAIL + half * rows : TAIL + (half + 1) * rows, :] = value
    top = (iota((TAIL, row_blocks), 0) == iota((TAIL, row_blocks), 1)).astype(BF16)
    tail = jnp.zeros((TAIL, columns), F32)
    for number in range(FIRST + seconds.shape[1]):
        block = firsts[number] if number < FIRST else seconds[:, number - FIRST, :]
        column = iota((column_blocks, columns), 1) - number * column_blocks
        spread = (iota((column_blocks, columns), 0) == column).astype(BF16)
        tail += dot(dot(top, block.astype(BF16)).astype(BF16), spread)
    trio[:TAIL, :] = tail.astype(BF16)


def chunk(index, length):
    return pl.ds(pl.multiple_of(index * length, length), length)


def start_all(copies):
    for one in copies:
        one.start()


def wait_all(copies):
    for one in copies:
        one.wait()


def repeat(times, body, unrolled):
    if unrolled:
        for t in range(times):
            body(t)
    else:

        def step(t, carry):
            body(t)
            return carry

        lax.fori_loop(0, times, step, 0)


def in_order(near, far, e):
    low = jnp.where(e == 0, near, far)
    high = jnp.where(e == 0, far, near)
    return jnp.concatenate([low, high], axis=0)


def first_kernel(count, take, out, left):
    z, q, e = place()
    rows, columns = out.shape[0] // 2, out.shape[1]
    for s in range(count):
        left[q ^ s] = take("plane", s, 2 * rows)
    tail = take("tail", 0, TAIL)
    masks = [block_mask(tail, n, rows, columns) for n in range(2)]
    total = jnp.zeros((2 * rows, columns), F32)
    for s in range(count):
        total += dot(left[z ^ s], in_order(take("near", s, rows), take("far", s, rows), e))
    for n in range(2):
        part = slice(n * rows, (n + 1) * rows)
        out[part, :] = (total[part] * masks[n]).astype(BF16)


def generator_kernel(count, take, out, left):
    z, q, e = place()
    rows, columns = out.shape
    for s in range(count):
        for half in range(2):
            left[half, q ^ s] = take("plane", s, rows, half * rows)
    mask = block_mask(take("tail", 0, TAIL), 2, rows, columns)
    total = jnp.zeros((rows, columns), F32)
    for half in range(2):
        shift = (1 - half) * rows
        for s in range(count):
            right = in_order(take("near", s, rows, shift), take("far", s, rows, shift), e)
            product = dot(left[half, z ^ s], right)
            total = total + product if half == 0 else total - product
    generator = (total * mask).astype(BF16)
    out[...] = (generator.astype(F32) * 0.25).astype(BF16)


def series_kernel(layout, count, pieces, *refs):
    arrays, tails, order = refs[:pieces], refs[pieces : pieces + 2 * count], refs[pieces + 2 * count]
    panel, mine, whole, turned, wides, spread, sems = refs[pieces + 2 * count + 1 :]
    z, q, e = place()
    rows, columns = mine.shape
    size = panel.shape[1]
    row_blocks, column_blocks, blocks = rows // BLK, columns // BLK, size // BLK
    small = size <= 1536
    copies = []
    for index, first, k, plane, lane in layout:
        core = e if lane == 0 else 1 - e
        copies.append(
            pltpu.make_async_copy(
                arrays[index].at[pl.ds(first, rows)],
                whole.at[chunk(2 * (z ^ k) + core, rows), chunk(q ^ plane, columns)],
                sems.at[len(copies)],
            )
        )
    start_all(copies)
    for index, ref in enumerate(tails):
        core = e if index < count else 1 - e
        wides[2 * (z ^ (index % count)) + core] = ref[...]
    filters = jnp.zeros((128, size), F32)
    for p in range(2 * count):
        column = iota((TAIL, size), 1) // BLK
        row = iota((TAIL, size), 0)
        near = ((row < row_blocks) & (column == row + p * row_blocks)).astype(BF16)
        filters += lax.dot_general(
            wides[p][:, :128], near, (((0,), (0,)), ((), ())), preferred_element_type=F32
        )
    spread[...] = filters

    wait_all(copies)

    def turn(t):
        tile = jnp.concatenate(
            [whole[chunk(order[t * column_blocks + a], BLK), :] for a in range(column_blocks)],
            axis=0,
        )
        turned[:, chunk(t, columns)] = tile.T

    def place_rows(b):
        whole[chunk(b, BLK), :] = turned[chunk(order[b], BLK), :]

    repeat(count, turn, small)
    repeat(blocks, place_rows, small)

    first = (2 * q + e) * rows
    unit = (iota((rows, size), 1) == iota((rows, size), 0) + first).astype(F32)
    own = unit + whole[chunk(2 * q + e, rows), :].astype(F32) / TERMS
    panel[...] = own.astype(BF16)
    width = size if small else 512
    for number in range(1, TERMS):
        current = panel[...]
        base = (FIRST + number - 1) * column_blocks + e * row_blocks

        def advance(t):
            part = chunk(t, width)
            product = dot(current, whole[:, part])
            mask = jnp.concatenate(
                [
                    jnp.broadcast_to(spread[pl.ds(base + b, 1), part], (BLK, width))
                    for b in range(row_blocks)
                ],
                axis=0,
            )
            here = iota((rows, width), 1) + t * width == iota((rows, width), 0) + first
            panel[:, part] = (here.astype(F32) + product * mask / (TERMS - number)).astype(BF16)

        repeat(size // width, advance, small)
    mine[...] = panel[:, chunk(z, columns)]


def turned_mask(tails, number, e, rows, columns):
    row_blocks, column_blocks = rows // BLK, columns // BLK
    pick = iota((rows, 128), 0) // BLK + number * column_blocks + e * row_blocks
    pick = (pick == iota((rows, 128), 1)).astype(BF16)
    mask = jnp.zeros((rows, columns), F32)
    for core in range(2):
        row = iota((TAIL, columns), 0)
        near = (row < row_blocks) & (iota((TAIL, columns), 1) // BLK == row + core * row_blocks)
        chosen = lax.dot_general(
            pick, tails[core][:, :128], (((1,), (1,)), ((), ())), preferred_element_type=F32
        )
        mask += dot(chosen.astype(BF16), near.astype(BF16))
    return mask


def square_kernel(count, take, panel, out):
    z, q, e = place()
    rows, columns = out.shape
    tails = in_order(take("tail", 0, TAIL), take("tail", 1, TAIL), e)
    mask = turned_mask([tails[:TAIL], tails[TAIL:]], FIRST + TERMS - 1, e, rows, columns)
    total = jnp.zeros((rows, columns), F32)
    for s in range(count):
        right = in_order(take("near", s, rows), take("far", s, rows), e)
        total += dot(panel[:, chunk(q ^ s, columns)], right)
    out[...] = (total * mask).astype(BF16)


def evolve_kernel(count, take, out, right):
    z, q, e = place()
    rows, columns = out.shape
    for s in range(count):
        right[q ^ s] = in_order(take("plane_near", s, rows), take("plane_far", s, rows), e)
    mask = block_mask(take("tail", 0, TAIL), FIRST + TERMS, rows, columns)
    total = jnp.zeros((columns, columns), F32)
    for s in range(count):
        total += dot(
            in_order(take("line_near", s, rows), take("line_far", s, rows), e), right[z ^ s]
        )
    total = total.T
    chosen = jnp.where(e == 0, total[:rows], total[rows:])
    out[...] = (chosen * mask).astype(BF16)


def on_device(
    mesh_rows,
    mesh_cols,
    fock_matrix,
    density,
    margin,
    fill_patterns,
    first_filters,
    owner_order,
    second_filters,
):
    moves = Moves(mesh_rows, mesh_cols)
    count = mesh_cols
    half = count // 2
    rows, columns = fock_matrix.shape
    size = rows * mesh_rows
    block = jax.ShapeDtypeStruct((rows, columns), BF16)
    barrier = lax.optimization_barrier

    def whole(values):
        return [(value, 0) for value in values]

    inputs = (
        fill_patterns,
        density,
        fock_matrix,
        margin,
        first_filters,
        second_filters.transpose(1, 0, 2),
    )
    masked_density, duo, trio = call(
        functools.partial(mask_kernel, len(inputs)),
        [
            block,
            jax.ShapeDtypeStruct((2 * rows, columns), BF16),
            jax.ShapeDtypeStruct((TAIL + 3 * rows, columns), BF16),
        ],
        [ANY] * len(inputs),
        [pltpu.VMEM(value.shape, value.dtype) for value in inputs]
        + [pltpu.SemaphoreType.DMA((len(inputs),))],
        "mask",
        room=60,
    )(*inputs)

    home = trio
    trio = moves.relabel(home)
    fock_rows = moves.plane(duo, True)
    density_line = moves.line(masked_density, True, gate=tuple(fock_rows[-2:]))
    density_near = [(trio, TAIL + 2 * rows)] + whole(density_line)
    span = TAIL + 2 * rows
    pair_second, *_ = barrier((trio[:span], *density_line))
    gated, _ = barrier((home[:span], density_line[half - 1]))
    pair_line = moves.line(gated, True, second=pair_second)
    early = barrier((*density_line, trio, pair_line[half - 1], *fock_rows))
    density_line, trio, pair_line[half - 1] = list(early[: count - 1]), early[count - 1], early[count]
    trio_far = moves.core(trio)
    density_far = [(trio_far, TAIL + 2 * rows)] + moves.cores(density_line)

    products = views_call(
        functools.partial(first_kernel, count),
        {
            "plane": [(trio, TAIL)] + whole(fock_rows),
            "tail": [(trio, 0)],
            "near": density_near,
            "far": density_far,
        },
        jax.ShapeDtypeStruct((2 * rows, columns), BF16),
        [pltpu.VMEM((count, 2 * rows, columns), BF16)],
        "first",
        10**10,
    )
    product_rows = [products] + moves.plane(products)
    pair_line = list(barrier((*pair_line, *product_rows[1:]))[: count - 1])
    pair_far = [(trio_far, 0)] + moves.cores(pair_line[:half]) + moves.cores(pair_line[half:])
    pair_near = [(trio, 0)] + whole(pair_line)

    generator = views_call(
        functools.partial(generator_kernel, count),
        {
            "plane": whole(product_rows),
            "tail": [(trio, 0)],
            "near": [(value, first + TAIL) for value, first in pair_near],
            "far": [(value, first + TAIL) for value, first in pair_far],
        },
        block,
        [pltpu.VMEM((2, count, rows, columns), BF16)],
        "generator",
    )

    lines = [generator] + moves.line(generator)
    arrays, layout, planes, done = [], [], [], []
    for held in (range(1), range(1, half + 1), range(half + 1, count)):
        group = lines[held[0]]
        if len(held) > 1:
            group = jnp.concatenate([lines[k] for k in held], axis=0)
        if held[0] == 1:
            group, *planes = barrier((group, *planes))
        planes = [group] + moves.plane(group)
        done.append((held, planes))
    done[1] = (done[1][0], list(barrier((*done[1][1], *done[2][1][1:]))[:count]))
    for held, planes in done:
        far = moves.cores(planes)
        for s, value in enumerate(planes):
            for lane, (array, start) in enumerate(((value, 0), far[s])):
                if not any(other is array for other in arrays):
                    arrays.append(array)
                index = [n for n, other in enumerate(arrays) if other is array][0]
                for n, k in enumerate(held):
                    layout.append((index, start + n * rows, k, s, lane))
    tails = [value[first : first + TAIL] for value, first in pair_near + pair_far]

    panel, mine = call(
        functools.partial(series_kernel, layout, count, len(arrays)),
        [jax.ShapeDtypeStruct((rows, size), BF16), block],
        [ANY] * len(arrays) + [INVMEM] * (2 * count) + [INSMEM],
        [
            pltpu.VMEM((size, size), BF16),
            pltpu.VMEM((size, size), BF16),
            pltpu.VMEM((mesh_rows, TAIL, columns), BF16),
            pltpu.VMEM((128, size), F32),
            pltpu.SemaphoreType.DMA((len(layout),)),
        ],
        "series",
        room=16 + 4 * size * size // MEGABYTE,
    )(*arrays, *tails, owner_order)

    near = [mine] + moves.plane(mine)
    square = views_call(
        functools.partial(square_kernel, count),
        {"near": whole(near), "far": moves.cores(near), "tail": [(trio, 0), (trio_far, 0)]},
        block,
        [],
        "square",
        extra=[panel],
    )

    line = moves.line(square)
    plane_near = [square] + moves.plane(square)
    plane_far = moves.cores(plane_near)
    evolved = views_call(
        functools.partial(evolve_kernel, count),
        {
            "plane_near": whole(plane_near),
            "plane_far": plane_far,
            "line_near": whole([square] + line),
            "line_far": plane_far[:1] + moves.cores(line),
            "tail": [(trio, 0)],
        },
        block,
        [pltpu.VMEM((count, columns, columns), BF16)],
        "evolve",
    )
    return moves.relabel(evolved)


def solution(mesh):
    return jax.shard_map(
        functools.partial(on_device, mesh.shape["row"], mesh.shape["col"]),
        mesh=mesh,
        in_specs=(
            P("row", "col"),
            P("row", "col"),
            P("row", "col"),
            P(None, "row", "col"),
            P(None, "row", "col"),
            P(),
            P(None, "row", "col"),
        ),
        out_specs=P("row", "col"),
        check_vma=False,
    )
```

```python
import functools

import jax
import jax.numpy as jnp
from jax import lax
from jax.experimental import pallas as pl
from jax.experimental.pallas import tpu as pltpu
from jax.sharding import PartitionSpec as P

BLK = 32
TERMS = 6
SQUARINGS = 2
FIRST = 3
AXES = ("row", "col")
F32 = jnp.float32
BF16 = jnp.bfloat16
TAIL = 16
MEGABYTE = 1024 * 1024


def coordinates(r, c):
    return r // 2, r % 2, c // 2, c % 2


def permutation(rows, cols, source):
    pairs = []
    for r in range(rows):
        for c in range(cols):
            sr, sc = source(*coordinates(r, c))
            pairs.append((sr * cols + sc, r * cols + c))
    return pairs


class Moves:
    def __init__(self, rows, cols):
        self.rows, self.cols = rows, cols

    def move(self, value, source):
        return lax.ppermute(value, AXES, permutation(self.rows, self.cols, source))

    def relabel(self, value, k=0):
        return self.move(value, lambda z, y, x, e: (2 * (z ^ k) + e, 2 * x + y))

    def along_z(self, value, k):
        return self.move(value, lambda z, y, x, e: (2 * (z ^ k) + y, 2 * x + e))

    def line(self, value, relabel=False, second=None, gate=None):
        bits = [1 << b for b in range((self.rows // 2).bit_length() - 1)]
        held = {0: value}
        for bit in reversed(bits):
            for k, part in list(held.items()):
                if k == 0 and relabel and (second is None or bit == bits[-1]):
                    held[bit] = self.relabel(value, bit)
                else:
                    if k and gate is not None:
                        part, _ = lax.optimization_barrier((part, (gate, held[bit])))
                    held[k | bit] = self.along_z(part, bit)
            if second is not None:
                held[0] = second
        return [held[k] for k in range(1, self.rows // 2)]

    def in_plane(self, value, s):
        return self.move(value, lambda z, y, x, e: (2 * z + (y ^ (s & 1)), 2 * (x ^ (s >> 1)) + e))

    def plane(self, value, relabel=False):
        if relabel:
            return [
                self.move(value, lambda z, y, x, e: (2 * z + e, 2 * (x ^ (s >> 1)) + (y ^ (s & 1))))
                for s in range(1, self.cols)
            ]
        return [self.in_plane(value, s) for s in range(1, self.cols)]

    def core(self, value):
        return self.move(value, lambda z, y, x, e: (2 * z + y, 2 * x + 1 - e))

    def cores(self, values):
        length = values[0].shape[0]
        far = self.core(jnp.concatenate(values, axis=0) if len(values) > 1 else values[0])
        return [(far, n * length) for n in range(len(values))]


def place():
    r, c = lax.axis_index("row"), lax.axis_index("col")
    z, y, x, e = r // 2, r % 2, c // 2, c % 2
    return z, 2 * x + y, e


def iota(shape, axis):
    return lax.broadcasted_iota(jnp.int32, shape, axis)


def dot(a, b):
    return jnp.dot(a, b, preferred_element_type=F32)


def repeat_rows(rows, blocks):
    return (iota((rows, blocks), 0) // BLK == iota((rows, blocks), 1)).astype(BF16)


def repeat_columns(blocks, columns, first=0):
    return (iota((blocks, columns), 0) == iota((blocks, columns), 1) // BLK + first).astype(BF16)


def block_mask(tail, number, rows, columns):
    blocks = columns // BLK
    wide = dot(repeat_rows(rows, tail.shape[0]), tail).astype(BF16)
    return dot(wide, repeat_columns(tail.shape[1], columns, number * blocks))


def call(kernel, outs, ins, scratch, name, flops=1000, room=16):
    return pl.pallas_call(
        kernel,
        out_shape=outs,
        in_specs=ins,
        out_specs=jax.tree.map(lambda _: pl.BlockSpec(memory_space=pltpu.VMEM), outs),
        scratch_shapes=scratch,
        name=name,
        compiler_params=pltpu.CompilerParams(vmem_limit_bytes=room * MEGABYTE),
        cost_estimate=pl.CostEstimate(flops=flops, bytes_accessed=1000, transcendentals=0),
    )


def views_call(kernel, views, outs, scratch, name, flops=1000, extra=()):
    arrays, spec = [], {}
    for key, items in views.items():
        spec[key] = []
        for value, first in items:
            known = [n for n, other in enumerate(arrays) if other is value]
            if not known:
                arrays.append(value)
            spec[key].append((known[0] if known else len(arrays) - 1, first))

    def body(*refs):
        def take(key, n, length, shift=0):
            index, first = spec[key][n]
            return refs[index][first + shift : first + shift + length, :]

        kernel(take, *refs[len(arrays) :])

    operands = [*arrays, *extra]
    return call(body, outs, [INVMEM] * len(operands), scratch, name, flops)(*operands)


ANY = pl.BlockSpec(memory_space=pl.ANY)
INVMEM = pl.BlockSpec(memory_space=pltpu.VMEM)
INSMEM = pl.BlockSpec(memory_space=pltpu.SMEM)


def mask_kernel(inputs, *refs):
    sources, (masked_density, duo, sent, trio) = refs[:inputs], refs[inputs : inputs + 4]
    held, sems = refs[inputs + 4 : -1], refs[-1]
    copies = [
        pltpu.make_async_copy(source, target, sems.at[n])
        for n, (source, target) in enumerate(zip(sources, held))
    ]
    fills, density, fock, margin, firsts, seconds = held
    rows, columns = density.shape
    row_blocks, column_blocks = rows // BLK, columns // BLK
    start_all(copies)
    tall = repeat_rows(rows, row_blocks)
    wide = repeat_columns(column_blocks, columns)

    def masked(ref, number):
        mask = dot(dot(tall, fills[number].astype(BF16)).astype(BF16), wide)
        return (ref[...].astype(F32) * mask).astype(BF16)

    wait_all(copies)
    value = masked(density, 1)
    masked_density[...] = value
    trio[TAIL + 2 * rows :, :] = value
    for half, (ref, number) in enumerate(((fock, 0), (margin, 2))):
        value = masked(ref, number)
        duo[half * rows : (half + 1) * rows, :] = value
        sent[TAIL + half * rows : TAIL + (half + 1) * rows, :] = value
        trio[TAIL + half * rows : TAIL + (half + 1) * rows, :] = value
    top = (iota((TAIL, row_blocks), 0) == iota((TAIL, row_blocks), 1)).astype(BF16)
    tail = jnp.zeros((TAIL, columns), F32)
    for number in range(FIRST + seconds.shape[1]):
        block = firsts[number] if number < FIRST else seconds[:, number - FIRST, :]
        column = iota((column_blocks, columns), 1) - number * column_blocks
        spread = (iota((column_blocks, columns), 0) == column).astype(BF16)
        tail += dot(dot(top, block.astype(BF16)).astype(BF16), spread)
    sent[:TAIL, :] = tail.astype(BF16)
    trio[:TAIL, :] = tail.astype(BF16)


def chunk(index, length):
    return pl.ds(pl.multiple_of(index * length, length), length)


def start_all(copies):
    for one in copies:
        one.start()


def wait_all(copies):
    for one in copies:
        one.wait()


def repeat(times, body, unrolled):
    if unrolled:
        for t in range(times):
            body(t)
    else:

        def step(t, carry):
            body(t)
            return carry

        lax.fori_loop(0, times, step, 0)


def in_order(near, far, e):
    low = jnp.where(e == 0, near, far)
    high = jnp.where(e == 0, far, near)
    return jnp.concatenate([low, high], axis=0)


def first_kernel(count, take, out, left):
    z, q, e = place()
    rows, columns = out.shape[0] // 2, out.shape[1]
    for s in range(count):
        left[q ^ s] = take("plane", s, 2 * rows)
    tail = take("tail", 0, TAIL)
    masks = [block_mask(tail, n, rows, columns) for n in range(2)]
    total = jnp.zeros((2 * rows, columns), F32)
    for s in range(count):
        total += dot(left[z ^ s], in_order(take("near", s, rows), take("far", s, rows), e))
    for n in range(2):
        part = slice(n * rows, (n + 1) * rows)
        out[part, :] = (total[part] * masks[n]).astype(BF16)


def generator_kernel(count, take, out, left):
    z, q, e = place()
    rows, columns = out.shape
    for s in range(count):
        for half in range(2):
            left[half, q ^ s] = take("plane", s, rows, half * rows)
    mask = block_mask(take("tail", 0, TAIL), 2, rows, columns)
    total = jnp.zeros((rows, columns), F32)
    for half in range(2):
        shift = (1 - half) * rows
        for s in range(count):
            right = in_order(take("near", s, rows, shift), take("far", s, rows, shift), e)
            product = dot(left[half, z ^ s], right)
            total = total + product if half == 0 else total - product
    generator = (total * mask).astype(BF16)
    out[...] = (generator.astype(F32) * 0.25).astype(BF16)


def series_kernel(layout, count, pieces, *refs):
    arrays, tails, order = refs[:pieces], refs[pieces : pieces + 2 * count], refs[pieces + 2 * count]
    panel, mine, whole, turned, wides, spread, sems = refs[pieces + 2 * count + 1 :]
    z, q, e = place()
    rows, columns = mine.shape
    size = panel.shape[1]
    row_blocks, column_blocks, blocks = rows // BLK, columns // BLK, size // BLK
    small = size <= 1536
    copies = []
    for index, first, k, plane, lane in layout:
        core = e if lane == 0 else 1 - e
        copies.append(
            pltpu.make_async_copy(
                arrays[index].at[pl.ds(first, rows)],
                whole.at[chunk(2 * (z ^ k) + core, rows), chunk(q ^ plane, columns)],
                sems.at[len(copies)],
            )
        )
    start_all(copies)
    for index, ref in enumerate(tails):
        core = e if index < count else 1 - e
        wides[2 * (z ^ (index % count)) + core] = ref[...]
    filters = jnp.zeros((128, size), F32)
    for p in range(2 * count):
        column = iota((TAIL, size), 1) // BLK
        row = iota((TAIL, size), 0)
        near = ((row < row_blocks) & (column == row + p * row_blocks)).astype(BF16)
        filters += lax.dot_general(
            wides[p][:, :128], near, (((0,), (0,)), ((), ())), preferred_element_type=F32
        )
    spread[...] = filters

    wait_all(copies)

    def turn(t):
        tile = jnp.concatenate(
            [whole[chunk(order[t * column_blocks + a], BLK), :] for a in range(column_blocks)],
            axis=0,
        )
        turned[:, chunk(t, columns)] = tile.T

    def place_rows(b):
        whole[chunk(b, BLK), :] = turned[chunk(order[b], BLK), :]

    repeat(count, turn, small)
    repeat(blocks, place_rows, small)

    first = (2 * q + e) * rows
    unit = (iota((rows, size), 1) == iota((rows, size), 0) + first).astype(F32)
    own = unit + whole[chunk(2 * q + e, rows), :].astype(F32) / TERMS
    panel[...] = own.astype(BF16)
    width = size if small else 512
    for number in range(1, TERMS):
        current = panel[...]
        base = (FIRST + number - 1) * column_blocks + e * row_blocks

        def advance(t):
            part = chunk(t, width)
            product = dot(current, whole[:, part])
            mask = jnp.concatenate(
                [
                    jnp.broadcast_to(spread[pl.ds(base + b, 1), part], (BLK, width))
                    for b in range(row_blocks)
                ],
                axis=0,
            )
            here = iota((rows, width), 1) + t * width == iota((rows, width), 0) + first
            panel[:, part] = (here.astype(F32) + product * mask / (TERMS - number)).astype(BF16)

        repeat(size // width, advance, small)
    mine[...] = panel[:, chunk(z, columns)]


def turned_mask(tails, number, e, rows, columns):
    row_blocks, column_blocks = rows // BLK, columns // BLK
    pick = iota((rows, 128), 0) // BLK + number * column_blocks + e * row_blocks
    pick = (pick == iota((rows, 128), 1)).astype(BF16)
    mask = jnp.zeros((rows, columns), F32)
    for core in range(2):
        row = iota((TAIL, columns), 0)
        near = (row < row_blocks) & (iota((TAIL, columns), 1) // BLK == row + core * row_blocks)
        chosen = lax.dot_general(
            pick, tails[core][:, :128], (((1,), (1,)), ((), ())), preferred_element_type=F32
        )
        mask += dot(chosen.astype(BF16), near.astype(BF16))
    return mask


def square_kernel(count, take, panel, out):
    z, q, e = place()
    rows, columns = out.shape
    tails = in_order(take("tail", 0, TAIL), take("tail", 1, TAIL), e)
    mask = turned_mask([tails[:TAIL], tails[TAIL:]], FIRST + TERMS - 1, e, rows, columns)
    total = jnp.zeros((rows, columns), F32)
    for s in range(count):
        right = in_order(take("near", s, rows), take("far", s, rows), e)
        total += dot(panel[:, chunk(q ^ s, columns)], right)
    out[...] = (total * mask).astype(BF16)


def evolve_kernel(count, take, out, right):
    z, q, e = place()
    rows, columns = out.shape
    for s in range(count):
        right[q ^ s] = in_order(take("plane_near", s, rows), take("plane_far", s, rows), e)
    mask = block_mask(take("tail", 0, TAIL), FIRST + TERMS, rows, columns)
    total = jnp.zeros((columns, columns), F32)
    for s in range(count):
        total += dot(
            in_order(take("line_near", s, rows), take("line_far", s, rows), e), right[z ^ s]
        )
    total = total.T
    chosen = jnp.where(e == 0, total[:rows], total[rows:])
    out[...] = (chosen * mask).astype(BF16)


def on_device(
    mesh_rows,
    mesh_cols,
    fock_matrix,
    density,
    margin,
    fill_patterns,
    first_filters,
    owner_order,
    second_filters,
):
    moves = Moves(mesh_rows, mesh_cols)
    count = mesh_cols
    half = count // 2
    rows, columns = fock_matrix.shape
    size = rows * mesh_rows
    block = jax.ShapeDtypeStruct((rows, columns), BF16)
    barrier = lax.optimization_barrier

    def whole(values):
        return [(value, 0) for value in values]

    inputs = (
        fill_patterns,
        density,
        fock_matrix,
        margin,
        first_filters,
        second_filters.transpose(1, 0, 2),
    )
    masked_density, duo, sent, trio = call(
        functools.partial(mask_kernel, len(inputs)),
        [
            block,
            jax.ShapeDtypeStruct((2 * rows, columns), BF16),
            jax.ShapeDtypeStruct((TAIL + 2 * rows, columns), BF16),
            jax.ShapeDtypeStruct((TAIL + 3 * rows, columns), BF16),
        ],
        [ANY] * len(inputs),
        [pltpu.VMEM(value.shape, value.dtype) for value in inputs]
        + [pltpu.SemaphoreType.DMA((len(inputs),))],
        "mask",
        room=60,
    )(*inputs)

    trio = moves.relabel(trio)
    fock_rows = moves.plane(duo, True)
    density_line = moves.line(masked_density, True, gate=tuple(fock_rows[-1:]))
    density_near = [(trio, TAIL + 2 * rows)] + whole(density_line)
    span = TAIL + 2 * rows
    pair_second, *_ = barrier((trio[:span], *density_line))
    gated, _ = barrier((sent, density_line[half - 1]))
    pair_line = moves.line(gated, True, second=pair_second)
    early = barrier((*density_line, trio, pair_line[half - 1], *fock_rows))
    density_line, trio, pair_line[half - 1] = list(early[: count - 1]), early[count - 1], early[count]
    trio_far = moves.core(trio)
    density_far = [(trio_far, TAIL + 2 * rows)] + moves.cores(density_line)

    products = views_call(
        functools.partial(first_kernel, count),
        {
            "plane": [(trio, TAIL)] + whole(fock_rows),
            "tail": [(trio, 0)],
            "near": density_near,
            "far": density_far,
        },
        jax.ShapeDtypeStruct((2 * rows, columns), BF16),
        [pltpu.VMEM((count, 2 * rows, columns), BF16)],
        "first",
        10**10,
    )
    product_rows = [products] + moves.plane(products)
    pair_line = list(barrier((*pair_line, *product_rows[1:]))[: count - 1])
    pair_far = [(trio_far, 0)] + moves.cores(pair_line[:half]) + moves.cores(pair_line[half:])
    pair_near = [(trio, 0)] + whole(pair_line)

    generator = views_call(
        functools.partial(generator_kernel, count),
        {
            "plane": whole(product_rows),
            "tail": [(trio, 0)],
            "near": [(value, first + TAIL) for value, first in pair_near],
            "far": [(value, first + TAIL) for value, first in pair_far],
        },
        block,
        [pltpu.VMEM((2, count, rows, columns), BF16)],
        "generator",
    )

    lines = [generator] + moves.line(generator)
    arrays, layout, planes, done = [], [], [], []
    for held in (range(1), range(1, half + 1), range(half + 1, count)):
        group = lines[held[0]]
        if len(held) > 1:
            group = jnp.concatenate([lines[k] for k in held], axis=0)
        if held[0] == 1:
            group, *planes = barrier((group, *planes))
        planes = [group] + moves.plane(group)
        done.append((held, planes))
    done[1] = (done[1][0], list(barrier((*done[1][1], *done[2][1][1:]))[:count]))
    own_far = moves.cores(done[0][1])
    done[2] = (done[2][0], list(barrier((*done[2][1], own_far[0][0]))[:count]))
    for held, planes in done:
        far = own_far if held[0] == 0 else moves.cores(planes)
        for s, value in enumerate(planes):
            for lane, (array, start) in enumerate(((value, 0), far[s])):
                if not any(other is array for other in arrays):
                    arrays.append(array)
                index = [n for n, other in enumerate(arrays) if other is array][0]
                for n, k in enumerate(held):
                    layout.append((index, start + n * rows, k, s, lane))
    tails = [value[first : first + TAIL] for value, first in pair_near + pair_far]

    panel, mine = call(
        functools.partial(series_kernel, layout, count, len(arrays)),
        [jax.ShapeDtypeStruct((rows, size), BF16), block],
        [ANY] * len(arrays) + [INVMEM] * (2 * count) + [INSMEM],
        [
            pltpu.VMEM((size, size), BF16),
            pltpu.VMEM((size, size), BF16),
            pltpu.VMEM((mesh_rows, TAIL, columns), BF16),
            pltpu.VMEM((128, size), F32),
            pltpu.SemaphoreType.DMA((len(layout),)),
        ],
        "series",
        room=16 + 4 * size * size // MEGABYTE,
    )(*arrays, *tails, owner_order)

    near = [mine] + moves.plane(mine)
    square = views_call(
        functools.partial(square_kernel, count),
        {"near": whole(near), "far": moves.cores(near), "tail": [(trio, 0), (trio_far, 0)]},
        block,
        [],
        "square",
        extra=[panel],
    )

    line = moves.line(square)
    plane_near = [square] + moves.plane(square)
    plane_far = moves.cores(plane_near)
    evolved = views_call(
        functools.partial(evolve_kernel, count),
        {
            "plane_near": whole(plane_near),
            "plane_far": plane_far,
            "line_near": whole([square] + line),
            "line_far": plane_far[:1] + moves.cores(line),
            "tail": [(trio, 0)],
        },
        block,
        [pltpu.VMEM((count, columns, columns), BF16)],
        "evolve",
    )
    return moves.relabel(evolved)


def solution(mesh):
    return jax.shard_map(
        functools.partial(on_device, mesh.shape["row"], mesh.shape["col"]),
        mesh=mesh,
        in_specs=(
            P("row", "col"),
            P("row", "col"),
            P("row", "col"),
            P(None, "row", "col"),
            P(None, "row", "col"),
            P(),
            P(None, "row", "col"),
        ),
        out_specs=P("row", "col"),
        check_vma=False,
    )
```

```python
import functools

import jax
import jax.numpy as jnp
from jax import lax
from jax.experimental import pallas as pl
from jax.experimental.pallas import tpu as pltpu
from jax.sharding import PartitionSpec as P

BLK = 32
TERMS = 6
SQUARINGS = 2
FIRST = 3
AXES = ("row", "col")
F32 = jnp.float32
BF16 = jnp.bfloat16
TAIL = 16
MEGABYTE = 1024 * 1024


def coordinates(r, c):
    return r // 2, r % 2, c // 2, c % 2


def permutation(rows, cols, source):
    pairs = []
    for r in range(rows):
        for c in range(cols):
            sr, sc = source(*coordinates(r, c))
            pairs.append((sr * cols + sc, r * cols + c))
    return pairs


class Moves:
    def __init__(self, rows, cols):
        self.rows, self.cols = rows, cols

    def move(self, value, source):
        return lax.ppermute(value, AXES, permutation(self.rows, self.cols, source))

    def relabel(self, value, k=0):
        return self.move(value, lambda z, y, x, e: (2 * (z ^ k) + e, 2 * x + y))

    def along_z(self, value, k):
        return self.move(value, lambda z, y, x, e: (2 * (z ^ k) + y, 2 * x + e))

    def line(self, value, relabel=False, second=None, gate=None):
        bits = [1 << b for b in range((self.rows // 2).bit_length() - 1)]
        held = {0: value}
        for bit in reversed(bits):
            for k, part in list(held.items()):
                if k == 0 and relabel and (second is None or bit == bits[-1]):
                    held[bit] = self.relabel(value, bit)
                else:
                    if k and gate is not None:
                        part, _ = lax.optimization_barrier((part, (gate, held[bit])))
                    held[k | bit] = self.along_z(part, bit)
            if second is not None:
                held[0] = second
        return [held[k] for k in range(1, self.rows // 2)]

    def in_plane(self, value, s):
        return self.move(value, lambda z, y, x, e: (2 * z + (y ^ (s & 1)), 2 * (x ^ (s >> 1)) + e))

    def plane(self, value, relabel=False):
        if relabel:
            return [
                self.move(value, lambda z, y, x, e: (2 * z + e, 2 * (x ^ (s >> 1)) + (y ^ (s & 1))))
                for s in range(1, self.cols)
            ]
        return [self.in_plane(value, s) for s in range(1, self.cols)]

    def core(self, value):
        return self.move(value, lambda z, y, x, e: (2 * z + y, 2 * x + 1 - e))

    def cores(self, values):
        length = values[0].shape[0]
        far = self.core(jnp.concatenate(values, axis=0) if len(values) > 1 else values[0])
        return [(far, n * length) for n in range(len(values))]


def place():
    r, c = lax.axis_index("row"), lax.axis_index("col")
    z, y, x, e = r // 2, r % 2, c // 2, c % 2
    return z, 2 * x + y, e


def iota(shape, axis):
    return lax.broadcasted_iota(jnp.int32, shape, axis)


def dot(a, b):
    return jnp.dot(a, b, preferred_element_type=F32)


def repeat_rows(rows, blocks):
    return (iota((rows, blocks), 0) // BLK == iota((rows, blocks), 1)).astype(BF16)


def repeat_columns(blocks, columns, first=0):
    return (iota((blocks, columns), 0) == iota((blocks, columns), 1) // BLK + first).astype(BF16)


def block_mask(tail, number, rows, columns):
    blocks = columns // BLK
    wide = dot(repeat_rows(rows, tail.shape[0]), tail).astype(BF16)
    return dot(wide, repeat_columns(tail.shape[1], columns, number * blocks))


def call(kernel, outs, ins, scratch, name, flops=1000, room=16):
    return pl.pallas_call(
        kernel,
        out_shape=outs,
        in_specs=ins,
        out_specs=jax.tree.map(lambda _: pl.BlockSpec(memory_space=pltpu.VMEM), outs),
        scratch_shapes=scratch,
        name=name,
        compiler_params=pltpu.CompilerParams(vmem_limit_bytes=room * MEGABYTE),
        cost_estimate=pl.CostEstimate(flops=flops, bytes_accessed=1000, transcendentals=0),
    )


def views_call(kernel, views, outs, scratch, name, flops=1000, extra=()):
    arrays, spec = [], {}
    for key, items in views.items():
        spec[key] = []
        for value, first in items:
            known = [n for n, other in enumerate(arrays) if other is value]
            if not known:
                arrays.append(value)
            spec[key].append((known[0] if known else len(arrays) - 1, first))

    def body(*refs):
        def take(key, n, length, shift=0):
            index, first = spec[key][n]
            return refs[index][first + shift : first + shift + length, :]

        kernel(take, *refs[len(arrays) :])

    operands = [*arrays, *extra]
    return call(body, outs, [INVMEM] * len(operands), scratch, name, flops)(*operands)


ANY = pl.BlockSpec(memory_space=pl.ANY)
INVMEM = pl.BlockSpec(memory_space=pltpu.VMEM)
INSMEM = pl.BlockSpec(memory_space=pltpu.SMEM)


def mask_kernel(inputs, *refs):
    sources, (masked_density, duo, sent, trio) = refs[:inputs], refs[inputs : inputs + 4]
    held, sems = refs[inputs + 4 : -1], refs[-1]
    copies = [
        pltpu.make_async_copy(source, target, sems.at[n])
        for n, (source, target) in enumerate(zip(sources, held))
    ]
    fills, density, fock, margin, firsts, seconds = held
    rows, columns = density.shape
    row_blocks, column_blocks = rows // BLK, columns // BLK
    start_all(copies)
    tall = repeat_rows(rows, row_blocks)
    wide = repeat_columns(column_blocks, columns)

    def masked(ref, number):
        mask = dot(dot(tall, fills[number].astype(BF16)).astype(BF16), wide)
        return (ref[...].astype(F32) * mask).astype(BF16)

    wait_all(copies)
    value = masked(density, 1)
    masked_density[...] = value
    trio[TAIL + 2 * rows :, :] = value
    for half, (ref, number) in enumerate(((fock, 0), (margin, 2))):
        value = masked(ref, number)
        duo[half * rows : (half + 1) * rows, :] = value
        sent[TAIL + half * rows : TAIL + (half + 1) * rows, :] = value
        trio[TAIL + half * rows : TAIL + (half + 1) * rows, :] = value
    top = (iota((TAIL, row_blocks), 0) == iota((TAIL, row_blocks), 1)).astype(BF16)
    packed = jnp.zeros((row_blocks, columns), F32)
    for number in range(FIRST + seconds.shape[1]):
        block = firsts[number] if number < FIRST else seconds[:, number - FIRST, :]
        column = iota((column_blocks, columns), 1) - number * column_blocks
        spread = (iota((column_blocks, columns), 0) == column).astype(BF16)
        packed += dot(block.astype(BF16), spread)
    tail = dot(top, packed.astype(BF16))
    sent[:TAIL, :] = tail.astype(BF16)
    trio[:TAIL, :] = tail.astype(BF16)


def chunk(index, length):
    return pl.ds(pl.multiple_of(index * length, length), length)


def start_all(copies):
    for one in copies:
        one.start()


def wait_all(copies):
    for one in copies:
        one.wait()


def repeat(times, body, unrolled):
    if unrolled:
        for t in range(times):
            body(t)
    else:

        def step(t, carry):
            body(t)
            return carry

        lax.fori_loop(0, times, step, 0)


def in_order(near, far, e):
    low = jnp.where(e == 0, near, far)
    high = jnp.where(e == 0, far, near)
    return jnp.concatenate([low, high], axis=0)


def first_kernel(count, take, out, left):
    z, q, e = place()
    rows, columns = out.shape[0] // 2, out.shape[1]
    for s in range(count):
        left[q ^ s] = take("plane", s, 2 * rows)
    tail = take("tail", 0, TAIL)
    masks = [block_mask(tail, n, rows, columns) for n in range(2)]
    total = jnp.zeros((2 * rows, columns), F32)
    for s in range(count):
        total += dot(left[z ^ s], in_order(take("near", s, rows), take("far", s, rows), e))
    for n in range(2):
        part = slice(n * rows, (n + 1) * rows)
        out[part, :] = (total[part] * masks[n]).astype(BF16)


def generator_kernel(count, take, out, left):
    z, q, e = place()
    rows, columns = out.shape
    for s in range(count):
        for half in range(2):
            left[half, q ^ s] = take("plane", s, rows, half * rows)
    mask = block_mask(take("tail", 0, TAIL), 2, rows, columns)
    total = jnp.zeros((rows, columns), F32)
    for half in range(2):
        shift = (1 - half) * rows
        for s in range(count):
            right = in_order(take("near", s, rows, shift), take("far", s, rows, shift), e)
            product = dot(left[half, z ^ s], right)
            total = total + product if half == 0 else total - product
    generator = (total * mask).astype(BF16)
    out[...] = (generator.astype(F32) * 0.25).astype(BF16)


def series_kernel(layout, count, pieces, *refs):
    arrays, tails, order = refs[:pieces], refs[pieces : pieces + 2 * count], refs[pieces + 2 * count]
    panel, mine, whole, turned, wides, spread, sems = refs[pieces + 2 * count + 1 :]
    z, q, e = place()
    rows, columns = mine.shape
    size = panel.shape[1]
    row_blocks, column_blocks, blocks = rows // BLK, columns // BLK, size // BLK
    small = size <= 1536
    copies = []
    for index, first, k, plane, lane in layout:
        core = e if lane == 0 else 1 - e
        copies.append(
            pltpu.make_async_copy(
                arrays[index].at[pl.ds(first, rows)],
                whole.at[chunk(2 * (z ^ k) + core, rows), chunk(q ^ plane, columns)],
                sems.at[len(copies)],
            )
        )
    start_all(copies)
    for index, ref in enumerate(tails):
        core = e if index < count else 1 - e
        wides[2 * (z ^ (index % count)) + core] = ref[...]
    filters = jnp.zeros((128, size), F32)
    for p in range(2 * count):
        column = iota((TAIL, size), 1) // BLK
        row = iota((TAIL, size), 0)
        near = ((row < row_blocks) & (column == row + p * row_blocks)).astype(BF16)
        filters += lax.dot_general(
            wides[p][:, :128], near, (((0,), (0,)), ((), ())), preferred_element_type=F32
        )
    spread[...] = filters

    wait_all(copies)

    def turn(t):
        tile = jnp.concatenate(
            [whole[chunk(order[t * column_blocks + a], BLK), :] for a in range(column_blocks)],
            axis=0,
        )
        turned[:, chunk(t, columns)] = tile.T

    def place_rows(b):
        whole[chunk(b, BLK), :] = turned[chunk(order[b], BLK), :]

    repeat(count, turn, small)
    repeat(blocks, place_rows, small)

    first = (2 * q + e) * rows
    unit = (iota((rows, size), 1) == iota((rows, size), 0) + first).astype(F32)
    own = unit + whole[chunk(2 * q + e, rows), :].astype(F32) / TERMS
    panel[...] = own.astype(BF16)
    width = size if small else 512
    for number in range(1, TERMS):
        current = panel[...]
        base = (FIRST + number - 1) * column_blocks + e * row_blocks

        def advance(t):
            part = chunk(t, width)
            product = dot(current, whole[:, part])
            mask = jnp.concatenate(
                [
                    jnp.broadcast_to(spread[pl.ds(base + b, 1), part], (BLK, width))
                    for b in range(row_blocks)
                ],
                axis=0,
            )
            here = iota((rows, width), 1) + t * width == iota((rows, width), 0) + first
            panel[:, part] = (here.astype(F32) + product * mask / (TERMS - number)).astype(BF16)

        repeat(size // width, advance, small)
    mine[...] = panel[:, chunk(z, columns)]


def turned_mask(tails, number, e, rows, columns):
    row_blocks, column_blocks = rows // BLK, columns // BLK
    pick = iota((rows, 128), 0) // BLK + number * column_blocks + e * row_blocks
    pick = (pick == iota((rows, 128), 1)).astype(BF16)
    mask = jnp.zeros((rows, columns), F32)
    for core in range(2):
        row = iota((TAIL, columns), 0)
        near = (row < row_blocks) & (iota((TAIL, columns), 1) // BLK == row + core * row_blocks)
        chosen = lax.dot_general(
            pick, tails[core][:, :128], (((1,), (1,)), ((), ())), preferred_element_type=F32
        )
        mask += dot(chosen.astype(BF16), near.astype(BF16))
    return mask


def square_kernel(count, take, panel, out):
    z, q, e = place()
    rows, columns = out.shape
    tails = in_order(take("tail", 0, TAIL), take("tail", 1, TAIL), e)
    mask = turned_mask([tails[:TAIL], tails[TAIL:]], FIRST + TERMS - 1, e, rows, columns)
    total = jnp.zeros((rows, columns), F32)
    for s in range(count):
        right = in_order(take("near", s, rows), take("far", s, rows), e)
        total += dot(panel[:, chunk(q ^ s, columns)], right)
    out[...] = (total * mask).astype(BF16)


def evolve_kernel(count, take, out, right):
    z, q, e = place()
    rows, columns = out.shape
    for s in range(count):
        right[q ^ s] = in_order(take("plane_near", s, rows), take("plane_far", s, rows), e)
    mask = block_mask(take("tail", 0, TAIL), FIRST + TERMS, rows, columns)
    total = jnp.zeros((columns, columns), F32)
    for s in range(count):
        total += dot(
            in_order(take("line_near", s, rows), take("line_far", s, rows), e), right[z ^ s]
        )
    total = total.T
    chosen = jnp.where(e == 0, total[:rows], total[rows:])
    out[...] = (chosen * mask).astype(BF16)


def on_device(
    mesh_rows,
    mesh_cols,
    fock_matrix,
    density,
    margin,
    fill_patterns,
    first_filters,
    owner_order,
    second_filters,
):
    moves = Moves(mesh_rows, mesh_cols)
    count = mesh_cols
    half = count // 2
    rows, columns = fock_matrix.shape
    size = rows * mesh_rows
    block = jax.ShapeDtypeStruct((rows, columns), BF16)
    barrier = lax.optimization_barrier

    def whole(values):
        return [(value, 0) for value in values]

    inputs = (
        fill_patterns,
        density,
        fock_matrix,
        margin,
        first_filters,
        second_filters.transpose(1, 0, 2),
    )
    masked_density, duo, sent, trio = call(
        functools.partial(mask_kernel, len(inputs)),
        [
            block,
            jax.ShapeDtypeStruct((2 * rows, columns), BF16),
            jax.ShapeDtypeStruct((TAIL + 2 * rows, columns), BF16),
            jax.ShapeDtypeStruct((TAIL + 3 * rows, columns), BF16),
        ],
        [ANY] * len(inputs),
        [pltpu.VMEM(value.shape, value.dtype) for value in inputs]
        + [pltpu.SemaphoreType.DMA((len(inputs),))],
        "mask",
        room=60,
    )(*inputs)

    trio = moves.relabel(trio)
    fock_rows = moves.plane(duo, True)
    density_line = moves.line(masked_density, True, gate=tuple(fock_rows[-1:]))
    density_near = [(trio, TAIL + 2 * rows)] + whole(density_line)
    span = TAIL + 2 * rows
    pair_second, *_ = barrier((trio[:span], *density_line))
    gated, _ = barrier((sent, density_line[half - 1]))
    pair_line = moves.line(gated, True, second=pair_second)
    early = barrier((*density_line, trio, pair_line[half - 1], *fock_rows))
    density_line, trio, pair_line[half - 1] = list(early[: count - 1]), early[count - 1], early[count]
    trio_far = moves.core(trio)
    density_far = [(trio_far, TAIL + 2 * rows)] + moves.cores(density_line)

    products = views_call(
        functools.partial(first_kernel, count),
        {
            "plane": [(trio, TAIL)] + whole(fock_rows),
            "tail": [(trio, 0)],
            "near": density_near,
            "far": density_far,
        },
        jax.ShapeDtypeStruct((2 * rows, columns), BF16),
        [pltpu.VMEM((count, 2 * rows, columns), BF16)],
        "first",
        10**10,
    )
    product_rows = [products] + moves.plane(products)
    pair_line = list(barrier((*pair_line, *product_rows[1:]))[: count - 1])
    pair_far = [(trio_far, 0)] + moves.cores(pair_line[:half]) + moves.cores(pair_line[half:])
    pair_near = [(trio, 0)] + whole(pair_line)

    generator = views_call(
        functools.partial(generator_kernel, count),
        {
            "plane": whole(product_rows),
            "tail": [(trio, 0)],
            "near": [(value, first + TAIL) for value, first in pair_near],
            "far": [(value, first + TAIL) for value, first in pair_far],
        },
        block,
        [pltpu.VMEM((2, count, rows, columns), BF16)],
        "generator",
    )

    lines = [generator] + moves.line(generator)
    arrays, layout, planes, done = [], [], [], []
    for held in (range(1), range(1, half + 1), range(half + 1, count)):
        group = lines[held[0]]
        if len(held) > 1:
            group = jnp.concatenate([lines[k] for k in held], axis=0)
        if held[0] == 1:
            group, *planes = barrier((group, *planes))
        planes = [group] + moves.plane(group)
        done.append((held, planes))
    done[1] = (done[1][0], list(barrier((*done[1][1], *done[2][1][1:]))[:count]))
    own_far = moves.cores(done[0][1])
    done[2] = (done[2][0], list(barrier((*done[2][1], own_far[0][0]))[:count]))
    for held, planes in done:
        far = own_far if held[0] == 0 else moves.cores(planes)
        for s, value in enumerate(planes):
            for lane, (array, start) in enumerate(((value, 0), far[s])):
                if not any(other is array for other in arrays):
                    arrays.append(array)
                index = [n for n, other in enumerate(arrays) if other is array][0]
                for n, k in enumerate(held):
                    layout.append((index, start + n * rows, k, s, lane))
    tails = [value[first : first + TAIL] for value, first in pair_near + pair_far]

    panel, mine = call(
        functools.partial(series_kernel, layout, count, len(arrays)),
        [jax.ShapeDtypeStruct((rows, size), BF16), block],
        [ANY] * len(arrays) + [INVMEM] * (2 * count) + [INSMEM],
        [
            pltpu.VMEM((size, size), BF16),
            pltpu.VMEM((size, size), BF16),
            pltpu.VMEM((mesh_rows, TAIL, columns), BF16),
            pltpu.VMEM((128, size), F32),
            pltpu.SemaphoreType.DMA((len(layout),)),
        ],
        "series",
        room=16 + 4 * size * size // MEGABYTE,
    )(*arrays, *tails, owner_order)

    near = [mine] + moves.plane(mine)
    square = views_call(
        functools.partial(square_kernel, count),
        {"near": whole(near), "far": moves.cores(near), "tail": [(trio, 0), (trio_far, 0)]},
        block,
        [],
        "square",
        extra=[panel],
    )

    line = moves.line(square)
    plane_near = [square] + moves.plane(square)
    plane_far = moves.cores(plane_near)
    evolved = views_call(
        functools.partial(evolve_kernel, count),
        {
            "plane_near": whole(plane_near),
            "plane_far": plane_far,
            "line_near": whole([square] + line),
            "line_far": plane_far[:1] + moves.cores(line),
            "tail": [(trio, 0)],
        },
        block,
        [pltpu.VMEM((count, columns, columns), BF16)],
        "evolve",
    )
    return moves.relabel(evolved)


def solution(mesh):
    return jax.shard_map(
        functools.partial(on_device, mesh.shape["row"], mesh.shape["col"]),
        mesh=mesh,
        in_specs=(
            P("row", "col"),
            P("row", "col"),
            P("row", "col"),
            P(None, "row", "col"),
            P(None, "row", "col"),
            P(),
            P(None, "row", "col"),
        ),
        out_specs=P("row", "col"),
        check_vma=False,
    )
```
